128 devices in a mesh: seq: 8 (over y, z_lo), dp: 16 (over x, z_hi, core).
Axes of the slice: x: 4, y: 4, z: 4 (z_hi: 2, z_lo: 2; z = z_hi * 2 + z_lo), core: 2. Of those that a mesh axis runs over, the one named last changes fastest.
Arguments:
- frames: bfloat16 [16, 2048, 1024], P('dp', 'seq'), may hold values from -6 to 6
- layernorm_gain: float32 [1024], replicated, may hold values from 0.25 to 1.75
- w_qkv: bfloat16 [1024, 3072], replicated
- w_out: bfloat16 [1024, 1024], replicated, may hold values from -0.1875 to 0.1875
- segment_ids: int32 [16, 2048], P('dp'), may hold values from 0 to 2, never falling along the last dimension, each value on 1 to 1536 neighbouring positions
- output_gradient: bfloat16 [16, 2048, 1024], P('dp', 'seq'), may hold values from -6 to 6
Outputs:
- layer_out: bfloat16 [16, 2048, 1024], P('dp', 'seq')
- frame_gradient: bfloat16 [16, 2048, 1024], P('dp', 'seq')
- grad_wqkv: bfloat16 [1024, 3072], P(('seq', 'dp'))
- grad_wout: bfloat16 [1024, 1024], P(('seq', 'dp'))
- grad_gain: float32 [1024], replicated
The draws below stay inside these ranges and needn't reach their ends.
Inputs may be any that keep to these rules, and one draw needn't show every extreme that they name: `segment_ids`: frames of one recording are contiguous and numbered in order in each group; a recording has at most 1536 frames.
All inputs are finite; a program needn't handle non-finite values.
Results may differ from the reference program's by a relative error of at most 0.0095.
Values may be sent and summed in bfloat16 or wider, within the bound.
No kernel may reach another device: no remote copies, remote signals or barrier semaphores. Data moves between devices by JAX's collectives and lax.ppermute only.
A program may use at most 192 MiB of HBM per device.

```python
import math
import jax
import jax.numpy as jnp
import numpy as np
from jax import lax

D = 1024
HEADS = 8
REC = 3
GROUP_FRAMES = 2048
GROUPS = 16


def draw_w_qkv(key, part):
    key = jax.random.fold_in(key, 7)
    base = jax.random.normal(key, (D, 3 * D), jnp.float32) * D ** (-0.5)
    return base.astype(jnp.bfloat16)


def block_levels(stream_key, dims, split, least, top_value):
    factor_of = 1.0
    for position, shards_of in split:
        steps = jax.random.uniform(jax.random.fold_in(jax.random.fold_in(stream_key, 6), position), (shards_of,), jnp.float32, least / len(split), top_value / len(split))
        factor_of = factor_of * jnp.repeat(jnp.exp(steps), dims[position] // shards_of).reshape((-1,) + (1,) * (len(dims) - 1 - position))
    return factor_of


def split_up(number_of, total, limit, lean):
    portions = [(1 << 20) // math.isqrt(grade ** lean) + 1 for grade in range(2, number_of + 1)]
    surplus, given = total - limit - (number_of - 1), [1] * (number_of - 1)
    while surplus > 0:
        free = [i for i in range(number_of - 1) if given[i] < limit]
        pool, budget = sum([portions[i] for i in free]), surplus
        for i in free:
            extra = min(limit - given[i], max(1, budget * portions[i] // pool), surplus)
            given[i] = given[i] + extra
            surplus = surplus - extra
    return np.array([limit] + given)


def uneven_parts(stream_key, number_of, total, reach, lean):
    if number_of == 2:
        one = jax.random.randint(stream_key, (), max(1, total - reach), min(reach, total - 1) + 1)
        return jnp.stack([one, total - one])
    lengths = jnp.asarray(split_up(number_of, total, reach, lean), jnp.int32)
    couples = (number_of - 1) // 2
    source_of, taker = lengths[1:1 + 2 * couples:2], lengths[2:2 + 2 * couples:2]
    slack = jnp.minimum(source_of - 1, reach - taker)
    moved = jax.random.randint(jax.random.fold_in(stream_key, 1), (couples,), 0, 1 << 20) % (slack + 1)
    lengths = lengths.at[1:1 + 2 * couples:2].set(source_of - moved).at[2:2 + 2 * couples:2].set(taker + moved)
    return lengths[jax.random.permutation(jax.random.fold_in(stream_key, 2), number_of)]


def gaussian(stream_key, shape, spread, bound, shards=(), dtype=jnp.bfloat16):
    result = jax.random.normal(stream_key, shape, jnp.float32) * spread
    if len(shards) > 0:
        result = block_levels(stream_key, shape, shards, -0.22, 0.18) * result
    return jnp.clip(result, min=-bound, max=bound).astype(dtype)


def setup_inputs(seed: int = 0) -> dict:
    seeds = jax.random.split(jax.random.key(seed), 7)
    frames = gaussian(seeds[0], (GROUPS, GROUP_FRAMES, D), 1.0, 6.0, ((0, 16), (1, 8)))
    layernorm_gain = jnp.clip(1.0 + 0.15 * jax.random.normal(seeds[1], (D,), jnp.float32), 0.25, 1.75)
    w_qkv = draw_w_qkv(jax.random.fold_in(seeds[6], 71), 0)
    w_out = gaussian(seeds[3], (D, D), D ** -0.5, 0.1875)
    segment_ids = jax.vmap(lambda own: jnp.searchsorted(jnp.cumsum(uneven_parts(own, REC, GROUP_FRAMES, GROUP_FRAMES - GROUP_FRAMES // 4, 2)), jnp.arange(GROUP_FRAMES), side="right"))(jax.random.split(seeds[4], GROUPS)).reshape((GROUPS, GROUP_FRAMES)).astype(jnp.int32)
    output_gradient = gaussian(seeds[5], (GROUPS, GROUP_FRAMES, D), 1.0, 6.0, ((0, 16), (1, 8)))
    return dict(frames=frames, layernorm_gain=layernorm_gain, w_qkv=w_qkv, w_out=w_out, segment_ids=segment_ids, output_gradient=output_gradient)


def apply_layernorm(frames_f):
    center = frames_f - lax.optimization_barrier(jnp.mean(frames_f, axis=-1, keepdims=True))
    inverse_deviation = lax.rsqrt(lax.optimization_barrier(jnp.mean(center * center, axis=-1, keepdims=True)) + 1e-05)
    return (center * inverse_deviation, inverse_deviation)

def group_pass(frames, segment_ids, output_gradient, layernorm_gain, w_qkv, w_out):
    frame_count = frames.shape[0]
    head_size = D // HEADS
    scale = head_size ** (-0.5)
    centered_scaled, inverse_deviation = apply_layernorm(frames.astype(jnp.float32))
    normalized_frames = (centered_scaled * layernorm_gain).astype(jnp.bfloat16)
    qkv = jnp.dot(normalized_frames, w_qkv, preferred_element_type=jnp.float32).astype(jnp.bfloat16)
    queries = qkv[:, :D].reshape(frame_count, HEADS, head_size).astype(jnp.float32)
    keys_all = qkv[:, D:2 * D].reshape(frame_count, HEADS, head_size).astype(jnp.float32)
    values_all = qkv[:, 2 * D:].reshape(frame_count, HEADS, head_size).astype(jnp.float32)
    match_mask = segment_ids[:, None] == segment_ids[None, :]
    scores = jnp.einsum('qhd,khd->hqk', queries, keys_all) * scale
    scores = jnp.where(match_mask[None], scores, -1e+30)
    peak = lax.optimization_barrier(jnp.max(scores, axis=-1, keepdims=True))
    expo = jnp.exp(scores - peak)
    probs = expo / lax.optimization_barrier(jnp.sum(expo, axis=-1, keepdims=True))
    probs_low = probs.astype(jnp.bfloat16)
    attn = jnp.einsum('hqk,khd->qhd', probs_low.astype(jnp.float32), values_all)
    attn = attn.reshape(frame_count, D).astype(jnp.bfloat16)
    layer_out = (frames.astype(jnp.float32) + jnp.dot(attn, w_out, preferred_element_type=jnp.float32)).astype(jnp.bfloat16)
    dattn = jnp.dot(output_gradient, w_out.T, preferred_element_type=jnp.float32).astype(jnp.bfloat16)
    dattn_heads = dattn.reshape(frame_count, HEADS, head_size).astype(jnp.float32)
    dprobs = jnp.einsum('qhd,khd->hqk', dattn_heads, values_all)
    delta = lax.optimization_barrier(jnp.sum(probs * dprobs, axis=-1, keepdims=True))
    dscores = (probs * (dprobs - delta) * scale).astype(jnp.bfloat16).astype(jnp.float32)
    grad_q = jnp.einsum('hqk,khd->qhd', dscores, keys_all).reshape(frame_count, D).astype(jnp.bfloat16)
    grad_k = jnp.einsum('hqk,qhd->khd', dscores, queries).reshape(frame_count, D).astype(jnp.bfloat16)
    grad_v = jnp.einsum('hqk,qhd->khd', probs_low.astype(jnp.float32), dattn_heads).reshape(frame_count, D).astype(jnp.bfloat16)
    dqkv = jnp.concatenate([grad_q, grad_k, grad_v], axis=1)
    normalized_gradient = jnp.dot(dqkv, w_qkv.T, preferred_element_type=jnp.float32)
    gain_product = lax.optimization_barrier(jnp.sum(normalized_gradient * centered_scaled, axis=0))
    centered_gradient = normalized_gradient * layernorm_gain
    frame_gradient = output_gradient.astype(jnp.float32) + inverse_deviation * (centered_gradient - lax.optimization_barrier(jnp.mean(centered_gradient, axis=-1, keepdims=True)) - centered_scaled * lax.optimization_barrier(jnp.mean(centered_gradient * centered_scaled, axis=-1, keepdims=True)))
    wqkv_term = jnp.dot(normalized_frames.T, dqkv, preferred_element_type=jnp.float32)
    wout_term = jnp.dot(attn.T, output_gradient, preferred_element_type=jnp.float32)
    return (layer_out, frame_gradient.astype(jnp.bfloat16), wqkv_term, wout_term, gain_product)

def reference(frames, layernorm_gain, w_qkv, w_out, segment_ids, output_gradient):

    def advance(carry, items):
        layer_out, frame_gradient, wqkv_term, wout_term, gain_product = group_pass(items[0], items[1], items[2], layernorm_gain, w_qkv, w_out)
        return ((carry[0] + wqkv_term, carry[1] + wout_term, carry[2] + gain_product), (layer_out, frame_gradient))
    start_sums = (jnp.zeros((D, 3 * D), jnp.float32), jnp.zeros((D, D), jnp.float32), jnp.zeros((D,), jnp.float32))
    sums, results = lax.scan(advance, start_sums, (frames, segment_ids, output_gradient))
    return (results[0], results[1], sums[0].astype(jnp.bfloat16), sums[1].astype(jnp.bfloat16), sums[2])
```

```python
import functools

import jax
import jax.numpy as jnp
from jax import lax
from jax.experimental import pallas as pl
from jax.experimental.pallas import tpu as pltpu
from jax.sharding import PartitionSpec as P

HEADS = 8
BF = jnp.bfloat16
F32 = jnp.float32
LOG2E = 1.4426950408889634


def swap(x, bits, axis, size):
    return lax.ppermute(x, axis, [(i, i ^ bits) for i in range(size)])


def seq_swap(x, bits):
    return x if bits == 0 else swap(x, bits, "seq", 8)


def dp_swap(x, bits):
    return swap(x, bits, "dp", 16)


def pick(x, index, axis):
    return lax.dynamic_index_in_dim(x, index, axis, keepdims=False)


def mm(a, b, ca, cb):
    return lax.dot_general(a, b, (((ca,), (cb,)), ((), ())), preferred_element_type=F32)


def attention_kernel(scale, *refs):
    qkv, dout = refs[:8], refs[8:16]
    key_tag, query_tag, attn, dqkv = refs[16:20]
    q_s, k_s, v_s, do_s, kt_s, vt_s, dk_s, dv_s = refs[20:]
    rows = qkv[0].shape[0]
    for r in range(8):
        part = pl.ds(r * rows, rows)
        q_s[part, :128] = qkv[r][:, :128]
        k_s[part, :128] = qkv[r][:, 128:256]
        v_s[part, :] = qkv[r][:, 256:]
        do_s[part, :] = dout[r][...]
        kt_s[:, part] = qkv[r][:, 128:256].T
        vt_s[:, part] = qkv[r][:, 256:].T
    q_s[:, 128:] = query_tag[...]
    k_s[:, 128:] = key_tag[...]
    dk_s[...] = jnp.zeros_like(dk_s)
    dv_s[...] = jnp.zeros_like(dv_s)

    def step(i, carry):
        part = pl.ds(pl.multiple_of(i * rows, rows), rows)
        q = q_s[part, :]
        do = do_s[part, :]
        scores = mm(k_s[...], q, 1, 1)
        peak = jnp.max(scores, axis=0, keepdims=True)
        expo = jnp.exp2((scores - peak) * (scale * LOG2E))
        probs = expo * (1.0 / jnp.sum(expo, axis=0, keepdims=True))
        low = probs.astype(BF)
        out_t = mm(vt_s[...], low, 1, 0)
        delta = jnp.sum(out_t * do.astype(F32).T, axis=0, keepdims=True)
        dprobs = mm(v_s[...], do, 1, 1)
        dscores = (probs * (dprobs - delta)).astype(BF)
        dq_t = mm(kt_s[...], dscores, 1, 0) * scale
        dk_s[...] += mm(dscores, q[:, :128], 1, 0)
        dv_s[...] += mm(low, do, 1, 0)
        attn[part, :] = out_t.T.astype(BF)
        dqkv[part, :128] = dq_t.T.astype(BF)
        return carry

    lax.fori_loop(0, 8, step, 0)
    dqkv[:, 128:256] = (dk_s[...] * scale).astype(BF)
    dqkv[:, 256:] = dv_s[...].astype(BF)


def attention(qkv, dout, key_tag, query_tag, scale):
    rows = qkv[0].shape[0]
    total = 8 * rows
    whole = pl.BlockSpec(memory_space=pltpu.VMEM)
    return pl.pallas_call(
        functools.partial(attention_kernel, scale),
        out_shape=(
            jax.ShapeDtypeStruct((total, 128), BF),
            jax.ShapeDtypeStruct((total, 384), BF),
        ),
        in_specs=[whole] * 18,
        out_specs=(whole, whole),
        scratch_shapes=[
            pltpu.VMEM((total, 256), BF),
            pltpu.VMEM((total, 256), BF),
            pltpu.VMEM((total, 128), BF),
            pltpu.VMEM((total, 128), BF),
            pltpu.VMEM((128, total), BF),
            pltpu.VMEM((128, total), BF),
            pltpu.VMEM((total, 128), F32),
            pltpu.VMEM((total, 128), F32),
        ],
        compiler_params=pltpu.CompilerParams(vmem_limit_bytes=48 * 1024 * 1024),
        name="attention",
    )(*qkv, *dout, key_tag, query_tag)


def projection_gradient_kernel(*refs):
    normed, dqkv, weights, gain, grad, gain_part = refs[:8], *refs[8:13]
    rows = normed[0].shape[0]
    total = mm(dqkv[:rows, :], normed[0][...], 0, 0)
    for r in range(1, 8):
        total += mm(dqkv[r * rows : (r + 1) * rows, :], normed[r][...], 0, 0)
    total = total.T
    grad[...] = total
    gain_part[...] = jnp.sum(total * weights[...].astype(F32), axis=1, keepdims=True) / gain[...]


def projection_gradient(normed, dqkv, weights, gain):
    whole = pl.BlockSpec(memory_space=pltpu.VMEM)
    width, columns = weights.shape
    return pl.pallas_call(
        projection_gradient_kernel,
        out_shape=(
            jax.ShapeDtypeStruct((width, columns), F32),
            jax.ShapeDtypeStruct((width, 1), F32),
        ),
        in_specs=[whole] * 11,
        out_specs=(whole, whole),
        compiler_params=pltpu.CompilerParams(vmem_limit_bytes=48 * 1024 * 1024),
        name="projection_gradient",
    )(*normed, dqkv, weights, gain)


def on_device(frames, layernorm_gain, w_qkv, w_out, segment_ids, output_gradient):
    x = frames[0].astype(F32)
    grad_out = output_gradient[0]
    rows, width = x.shape
    head = width // HEADS
    scale = head**-0.5
    seq, dp = lax.axis_index("seq"), lax.axis_index("dp")
    order = [seq ^ r for r in range(8)]

    center = x - jnp.mean(x, axis=-1, keepdims=True)
    rstd = lax.rsqrt(jnp.mean(center * center, axis=-1, keepdims=True) + 1e-05)
    xhat = center * rstd
    normed = [None] * 8
    normed[0] = (xhat * layernorm_gain).astype(BF)
    normed[1] = seq_swap(normed[0], 1)
    normed[2] = seq_swap(normed[0], 2)
    normed[6] = seq_swap(normed[0], 6)
    normed[4] = seq_swap(normed[0], 4)
    normed[3] = seq_swap(normed[1], 2)
    normed[7] = seq_swap(normed[1], 6)
    normed[5] = seq_swap(normed[4], 1)

    w_out_here = jnp.concatenate(
        [lax.dynamic_slice_in_dim(w_out, o * head, head, 0) for o in order], axis=0
    )
    dattn = mm(grad_out, w_out_here, 1, 1).astype(BF)
    dout = [seq_swap(dattn[:, r * head : (r + 1) * head], r) for r in range(8)]

    columns = [
        [lax.dynamic_slice_in_dim(w_qkv, t * width + o * head, head, 1) for t in range(3)]
        for o in order
    ]
    w_head = jnp.concatenate(columns[0], axis=1)
    w_here = jnp.concatenate([c for group in columns for c in group], axis=1)
    qkv = [mm(n, w_head, 1, 0).astype(BF) for n in normed]

    ids = segment_ids[0]
    ids_here = jnp.concatenate([lax.dynamic_slice_in_dim(ids, o * rows, rows) for o in order])
    same = ids_here[:, None] == jnp.arange(128)[None, :]
    key_tag = same.astype(BF)
    query_tag = jnp.where(same, 0.0, -1e30).astype(BF)

    attn_head, dqkv_head = attention(qkv, dout, key_tag, query_tag, scale)

    attn = jnp.concatenate(
        [seq_swap(attn_head[r * rows : (r + 1) * rows], r) for r in range(8)], axis=1
    )
    dqkv = jnp.concatenate(
        [seq_swap(dqkv_head[r * rows : (r + 1) * rows], r) for r in range(8)], axis=1
    )

    grad_head, gain_part = projection_gradient(
        normed, dqkv_head, w_head, layernorm_gain[:, None]
    )
    grad_gain = gain_part.reshape(8, width // 8)
    for bits in (1, 2, 4, 8):
        grad_gain = grad_gain + dp_swap(grad_gain, bits)
    for bits in (1, 2, 4):
        grad_gain = grad_gain + seq_swap(grad_gain, bits)
    grad_gain = grad_gain.reshape(width)

    layer_out = (x + mm(attn, w_out_here, 1, 0)).astype(BF)
    wout_part = mm(attn, grad_out, 0, 0)

    dnormed = mm(dqkv, w_here, 1, 1)
    g = dnormed * layernorm_gain
    frame_gradient = grad_out.astype(F32) + rstd * (
        g
        - jnp.mean(g, axis=-1, keepdims=True)
        - xhat * jnp.mean(g * xhat, axis=-1, keepdims=True)
    )

    per = width // 128
    head_rows = jnp.concatenate(
        [lax.dynamic_slice_in_dim(grad_head, o * head, head, 0) for o in order], axis=0
    )
    sums = jnp.concatenate([head_rows, wout_part], axis=1)
    sums = sums.reshape(8, 4, 2, 2, per, sums.shape[1])
    core, along_x, along_z = dp & 1, dp >> 2, (dp >> 1) & 1
    sums = pick(sums, core, 3) + dp_swap(pick(sums, 1 - core, 3).astype(BF), 1).astype(F32)
    parts = [dp_swap(pick(sums, along_x ^ r, 1).astype(BF), 4 * r) for r in range(1, 4)]
    sums = pick(sums, along_x, 1) + sum(part.astype(F32) for part in parts)
    sums = pick(sums, along_z, 1) + dp_swap(pick(sums, 1 - along_z, 1).astype(BF), 2).astype(F32)
    pieces = [seq_swap(sums[r].astype(BF), r) for r in range(8)]
    stacked = jnp.stack([p[:, : 3 * head].reshape(per, 3, head) for p in pieces])
    grad_wqkv = jnp.stack([pick(stacked, o, 0) for o in order], axis=2).reshape(per, 3 * width)
    grad_wout = sum(p[:, 3 * head :].astype(F32) for p in pieces).astype(BF)
    return (
        layer_out[None],
        frame_gradient.astype(BF)[None],
        grad_wqkv,
        grad_wout,
        grad_gain,
    )


def solution(mesh):
    placed = (P("dp", "seq", None), P(), P(), P(), P("dp", None), P("dp", "seq", None))
    return jax.shard_map(
        on_device,
        mesh=mesh,
        in_specs=placed,
        out_specs=(
            P("dp", "seq", None),
            P("dp", "seq", None),
            P(("seq", "dp"), None),
            P(("seq", "dp"), None),
            P(),
        ),
        check_vma=False,
    )
```

```python
import functools

import jax
import jax.numpy as jnp
from jax import lax
from jax.experimental import pallas as pl
from jax.experimental.pallas import tpu as pltpu
from jax.sharding import PartitionSpec as P

HEADS = 8
BF = jnp.bfloat16
F32 = jnp.float32
LOG2E = 1.4426950408889634
VMEM_LIMIT = 48 * 1024 * 1024
WHOLE = pl.BlockSpec(memory_space=pltpu.VMEM)
SCALARS = pl.BlockSpec(memory_space=pltpu.SMEM)


def seq_swap(x, bits):
    return lax.ppermute(x, "seq", [(i, i ^ bits) for i in range(8)])


def dp_swap(x, bits):
    return lax.ppermute(x, "dp", [(i, i ^ bits) for i in range(16)])


def seq_exchange(x):
    return lax.all_to_all(x, "seq", 0, 0, tiled=True)


def mm(a, b, ca, cb):
    return lax.dot_general(a, b, (((ca,), (cb,)), ((), ())), preferred_element_type=F32)


def call(kernel, name, out_shape, **options):
    return pl.pallas_call(
        kernel,
        out_shape=out_shape,
        compiler_params=pltpu.CompilerParams(vmem_limit_bytes=VMEM_LIMIT),
        name=name,
        **options,
    )


def shape(dtype, *dims):
    return jax.ShapeDtypeStruct(dims, dtype)


def layernorm(x):
    center = x - jnp.mean(x, axis=-1, keepdims=True)
    rstd = lax.rsqrt(jnp.mean(center * center, axis=-1, keepdims=True) + 1e-05)
    return center * rstd, rstd


def layernorm_kernel(frames, gain, normed):
    xhat, _ = layernorm(frames[...].astype(F32))
    normed[...] = (xhat * gain[...]).astype(BF)


def dattn_kernel(pos, grad_out, w_out, wq, wk, wv, dattn, w_head):
    w_head[:, :128] = wq[...]
    w_head[:, 128:256] = wk[...]
    w_head[:, 256:] = wv[...]
    full = mm(grad_out[...], w_out[...], 1, 1).astype(BF)
    for h in range(HEADS):
        dattn[h] = full[:, h * 128 : (h + 1) * 128]


def forward_kernel(scale, pos, *refs):
    parts, (key_tag, query_tag, attn, probs, qkv, q_s, k_s, vt_s) = refs[:8], refs[8:]
    rows = parts[0].shape[0]
    i = pl.program_id(0)

    @pl.when(i == 0)
    def _():
        for r in range(8):
            rng = pl.ds(pl.multiple_of((pos[0] ^ r) * rows, rows), rows)
            qkv[rng, :] = parts[r][...]
            q_s[rng, :128] = parts[r][:, :128]
            k_s[rng, :128] = parts[r][:, 128:256]
        vt_s[...] = qkv[:, 256:].T
        q_s[:, 128:] = query_tag[...]
        k_s[:, 128:] = key_tag[...]

    rng = pl.ds(pl.multiple_of(i * rows, rows), rows)
    scores = mm(k_s[...], q_s[rng, :], 1, 1)
    peak = jnp.max(scores, axis=0, keepdims=True)
    expo = jnp.exp2((scores - peak) * (scale * LOG2E))
    low = (expo * (1.0 / jnp.sum(expo, axis=0, keepdims=True))).astype(BF)
    probs[0] = low
    attn[...] = mm(vt_s[...], low, 1, 0).T.astype(BF)


def forward(pos, parts, key_tag, query_tag, scale):
    rows = parts[0].shape[0]
    total = 8 * rows
    return call(
        functools.partial(forward_kernel, scale),
        "forward",
        (shape(BF, total, 128), shape(BF, 8, total, rows), shape(BF, total, 384)),
        grid=(8,),
        in_specs=[SCALARS] + [WHOLE] * 10,
        out_specs=(
            pl.BlockSpec((rows, 128), lambda i: (i, 0)),
            pl.BlockSpec((1, total, rows), lambda i: (i, 0, 0)),
            WHOLE,
        ),
        scratch_shapes=[
            pltpu.VMEM((total, 256), BF),
            pltpu.VMEM((total, 256), BF),
            pltpu.VMEM((128, total), BF),
        ],
    )(pos, *parts, key_tag, query_tag)


def backward_kernel(scale, qkv, dout, attn, probs, dqkv, kt_s, dk_s, dv_s):
    rows = attn.shape[0]
    i = pl.program_id(0)

    @pl.when(i == 0)
    def _():
        kt_s[...] = qkv[:, 128:256].T
        dk_s[...] = jnp.zeros_like(dk_s)
        dv_s[...] = jnp.zeros_like(dv_s)

    rng = pl.ds(pl.multiple_of(i * rows, rows), rows)
    do = dout[0]
    low = probs[0]
    delta = jnp.sum((attn[...].astype(F32) * do.astype(F32)).T, axis=0, keepdims=True)
    dprobs = mm(qkv[:, 256:], do, 1, 1)
    dscores = (low.astype(F32) * (dprobs - delta)).astype(BF)
    dk_s[...] += mm(dscores, qkv[rng, :128], 1, 0)
    dv_s[...] += mm(low, do, 1, 0)
    dqkv[rng, :128] = (mm(kt_s[...], dscores, 1, 0) * scale).T.astype(BF)

    @pl.when(i == 7)
    def _():
        dqkv[:, 128:256] = (dk_s[...] * scale).astype(BF)
        dqkv[:, 256:] = dv_s[...].astype(BF)


def backward(qkv, dout, attn, probs, scale):
    total = qkv.shape[0]
    rows = total // 8
    return call(
        functools.partial(backward_kernel, scale),
        "backward",
        shape(BF, total, 384),
        grid=(8,),
        in_specs=[
            WHOLE,
            pl.BlockSpec((1, rows, 128), lambda i: (i, 0, 0)),
            pl.BlockSpec((rows, 128), lambda i: (i, 0)),
            pl.BlockSpec((1, total, rows), lambda i: (i, 0, 0)),
        ],
        out_specs=WHOLE,
        scratch_shapes=[
            pltpu.VMEM((128, total), BF),
            pltpu.VMEM((total, 128), F32),
            pltpu.VMEM((total, 128), F32),
        ],
    )(qkv, dout, attn, probs)


def split_rows(dp, source, keep, other):
    for r in range(16):
        half = other if r & 1 else keep
        for s in range(8):
            rows = pl.ds(pl.multiple_of(s * 128 + (dp ^ r) * 8, 8), 8)
            half[(r >> 1) * 64 + s * 8 : (r >> 1) * 64 + s * 8 + 8, :] = source[rows, :]


def projection_kernel(pos, *refs):
    normed = refs[:8]
    dqkv, weights, gain, keep, send, gain_part, grad, other = refs[8:]
    rows = normed[0].shape[0]
    total = None
    for r in range(8):
        rng = pl.ds(pl.multiple_of((pos[0] ^ r) * rows, rows), rows)
        term = mm(dqkv[rng, :], normed[r][...], 0, 0)
        total = term if total is None else total + term
    grad[...] = total.T
    gain_part[...] = (
        jnp.sum(grad[...] * weights[...].astype(F32), axis=1, keepdims=True) / gain[...]
    )
    split_rows(pos[1], grad, keep, other)
    send[...] = other[...].astype(BF)


def projection_gradient(pos, normed, dqkv, weights, gain):
    return call(
        projection_kernel,
        "projection_gradient",
        (shape(F32, 512, 384), shape(BF, 512, 384), shape(F32, 1024, 1)),
        in_specs=[SCALARS] + [WHOLE] * 11,
        out_specs=(WHOLE,) * 3,
        scratch_shapes=[pltpu.VMEM((1024, 384), F32), pltpu.VMEM((512, 384), F32)],
    )(pos, *normed, dqkv, weights, gain)


def output_kernel(pos, attn, grad_out, w_out, frames, layer_out, keep, send, grad, other):
    total = frames[...].astype(F32)
    for h in range(HEADS):
        rows = slice(h * 128, (h + 1) * 128)
        total += mm(attn[h], w_out[rows, :], 1, 0)
        grad[rows, :] = mm(attn[h], grad_out[...], 0, 0)
    layer_out[...] = total.astype(BF)
    split_rows(pos[1], grad, keep, other)
    send[...] = other[...].astype(BF)


def output_projection(pos, attn, grad_out, w_out, frames):
    return call(
        output_kernel,
        "output_projection",
        (shape(BF, *frames.shape), shape(F32, 512, 1024), shape(BF, 512, 1024)),
        in_specs=[SCALARS] + [WHOLE] * 4,
        out_specs=(WHOLE,) * 3,
        scratch_shapes=[pltpu.VMEM((1024, 1024), F32), pltpu.VMEM((512, 1024), F32)],
    )(pos, attn, grad_out, w_out, frames)


def frame_kernel(dqkv, wq, wk, wv, frames, gain, grad_out, result, total):
    h = pl.program_id(0)
    weights = jnp.concatenate([wq[...], wk[...], wv[...]], axis=1)
    term = mm(dqkv[0], weights, 1, 1)

    @pl.when(h == 0)
    def _():
        total[...] = term

    @pl.when(h > 0)
    def _():
        total[...] += term

    @pl.when(h == HEADS - 1)
    def _():
        xhat, rstd = layernorm(frames[...].astype(F32))
        g = total[...] * gain[...]
        mean_g = jnp.mean(g, axis=-1, keepdims=True)
        mean_gx = jnp.mean(g * xhat, axis=-1, keepdims=True)
        result[...] = (
            grad_out[...].astype(F32) + rstd * (g - mean_g - xhat * mean_gx)
        ).astype(BF)


def frame_gradient(dqkv, w_qkv, frames, gain, grad_out):
    rows, width = frames.shape
    return call(
        frame_kernel,
        "frame_gradient",
        shape(BF, rows, width),
        grid=(HEADS,),
        in_specs=[pl.BlockSpec((1, rows, 384), lambda h: (h, 0, 0))]
        + [pl.BlockSpec((width, 128), lambda h, t=t: (0, t * HEADS + h)) for t in range(3)]
        + [WHOLE] * 3,
        out_specs=WHOLE,
        scratch_shapes=[pltpu.VMEM((rows, width), F32)],
    )(dqkv, w_qkv, w_qkv, w_qkv, frames, gain, grad_out)


def high_low(x):
    high = lax.reduce_precision(x, 8, 7)
    low = lax.reduce_precision(x - high, 8, 7)
    return high, low


def packed(x, columns):
    high, low = high_low(x)
    both = jnp.concatenate([high, low], axis=1).astype(BF)
    return jnp.pad(both, ((0, 0), (0, columns - 256)))


def unpacked(x):
    return x[:, :128].astype(F32) + x[:, 128:256].astype(F32)


def settled(x):
    high, low = high_low(x)
    return high + low


def on_device(frames, layernorm_gain, w_qkv, w_out, segment_ids, output_gradient):
    x = frames[0]
    grad_out = output_gradient[0]
    rows, width = x.shape
    head = width // HEADS
    scale = head**-0.5
    pos = jnp.stack([lax.axis_index("seq"), lax.axis_index("dp")]).astype(jnp.int32)
    gain_row = layernorm_gain[None, :]

    normed = [None] * 8
    normed[0] = call(
        layernorm_kernel, "layernorm", shape(BF, rows, width), in_specs=[WHOLE] * 2, out_specs=WHOLE
    )(x, gain_row)
    normed[1] = seq_swap(normed[0], 1)
    normed[2] = seq_swap(normed[0], 2)
    normed[6] = seq_swap(normed[0], 6)
    normed[4] = seq_swap(normed[0], 4)
    normed[3] = seq_swap(normed[1], 2)
    normed[7] = seq_swap(normed[1], 6)
    normed[5] = seq_swap(normed[4], 1)

    dattn, w_head = pl.pallas_call(
        dattn_kernel,
        out_shape=(shape(BF, HEADS, rows, head), shape(BF, width, 384)),
        grid_spec=pltpu.PrefetchScalarGridSpec(
            num_scalar_prefetch=1,
            grid=(1,),
            in_specs=[WHOLE] * 2
            + [
                pl.BlockSpec((width, head), lambda i, p, t=t: (0, t * HEADS + p[0]))
                for t in range(3)
            ],
            out_specs=(WHOLE, WHOLE),
        ),
        compiler_params=pltpu.CompilerParams(vmem_limit_bytes=VMEM_LIMIT),
        name="dattn",
    )(pos, grad_out, w_out, w_qkv, w_qkv, w_qkv)
    dout = seq_exchange(dattn)

    parts = [mm(n, w_head, 1, 0).astype(BF) for n in normed]
    same = segment_ids[0][:, None] == jnp.arange(128)[None, :]
    key_tag = same.astype(BF)
    query_tag = jnp.where(same, 0.0, -1e30).astype(BF)

    attn_head, probs, qkv = forward(pos, parts, key_tag, query_tag, scale)
    attn = seq_exchange(attn_head.reshape(8, rows, head))
    dqkv_head = backward(qkv, dout, attn_head, probs, scale)
    dqkv = seq_exchange(dqkv_head.reshape(8, rows, 384))

    layer_out, wout_keep, wout_send = output_projection(pos, attn, grad_out, w_out, x)
    wqkv_keep, wqkv_send, gain_part = projection_gradient(
        pos, normed, dqkv_head, w_head, layernorm_gain[:, None]
    )
    frame_grad = frame_gradient(dqkv, w_qkv, x, gain_row, grad_out)

    gain_part = gain_part.reshape(8, 128)
    wout_sum = wout_keep + dp_swap(wout_send, 1).astype(F32)
    got = dp_swap(jnp.concatenate([wqkv_send, packed(gain_part, 384)], axis=0), 1)
    wqkv_sum = wqkv_keep + got[:512].astype(F32)
    gain_sum = settled(gain_part) + unpacked(got[512:])

    sums = jnp.concatenate([wqkv_sum, wout_sum], axis=1).reshape(4, 128, 1408)
    note = packed(gain_sum, 1408)
    got = [
        dp_swap(jnp.concatenate([sums[r].astype(BF), note], axis=0), 4 * r) for r in range(1, 4)
    ]
    sums = sums[0] + sum(part[:128].astype(F32) for part in got)
    notes = [settled(gain_sum)] + [unpacked(part[128:]) for part in got]
    gain_sum = (notes[0] + notes[1]) + (notes[2] + notes[3])

    got = dp_swap(jnp.concatenate([sums[64:].astype(BF), packed(gain_sum, 1408)], axis=0), 2)
    sums = sums[:64] + got[:64].astype(F32)
    gain_sum = settled(gain_sum) + unpacked(got[64:])

    note = jnp.broadcast_to(packed(gain_sum, 256)[None], (8, 8, 256))
    got = seq_exchange(jnp.concatenate([sums.reshape(8, 8, 1408).astype(BF), note], axis=2))
    grad_wqkv = got[:, :, :384].reshape(8, 8, 3, head).transpose(1, 2, 0, 3).reshape(8, 3 * width)
    grad_wout = jnp.sum(got[:, :, 384:1408].astype(F32), axis=0).astype(BF)
    totals = [unpacked(got[s, :, 1408:]) for s in range(8)]
    grad_gain = functools.reduce(lambda a, b: a + b, totals).reshape(width)
    return (
        layer_out[None],
        frame_grad[None],
        grad_wqkv,
        grad_wout,
        grad_gain,
    )


def solution(mesh):
    placed = (P("dp", "seq", None), P(), P(), P(), P("dp", None), P("dp", "seq", None))
    return jax.shard_map(
        on_device,
        mesh=mesh,
        in_specs=placed,
        out_specs=(
            P("dp", "seq", None),
            P("dp", "seq", None),
            P(("seq", "dp"), None),
            P(("seq", "dp"), None),
            P(),
        ),
        check_vma=False,
    )
```

```python
import functools

import jax
import jax.numpy as jnp
from jax import lax
from jax.experimental import pallas as pl
from jax.experimental.pallas import tpu as pltpu
from jax.sharding import PartitionSpec as P

HEADS = 8
BF = jnp.bfloat16
F32 = jnp.float32
LOG2E = 1.4426950408889634
UNROLL = 4
VMEM_LIMIT = 24 * 1024 * 1024
SMALL = pl.CostEstimate(flops=1, bytes_accessed=1, transcendentals=0)
WHOLE = pl.BlockSpec(memory_space=pltpu.VMEM)
SCALARS = pl.BlockSpec(memory_space=pltpu.SMEM)


def seq_swap(x, bits):
    return lax.ppermute(x, "seq", [(i, i ^ bits) for i in range(8)])


def dp_swap(x, bits):
    return lax.ppermute(x, "dp", [(i, i ^ bits) for i in range(16)])


def seq_exchange(x):
    return lax.all_to_all(x, "seq", 0, 0, tiled=True)


def mm(a, b, ca, cb):
    return lax.dot_general(a, b, (((ca,), (cb,)), ((), ())), preferred_element_type=F32)


def call(kernel, name, out_shape, **options):
    return pl.pallas_call(
        kernel,
        out_shape=out_shape,
        compiler_params=pltpu.CompilerParams(vmem_limit_bytes=VMEM_LIMIT),
        name=name,
        **options,
    )


def shape(dtype, *dims):
    return jax.ShapeDtypeStruct(dims, dtype)


def layernorm(x):
    center = x - jnp.mean(x, axis=-1, keepdims=True)
    rstd = lax.rsqrt(jnp.mean(center * center, axis=-1, keepdims=True) + 1e-05)
    return center * rstd, rstd


def layernorm_kernel(frames, gain, normed):
    xhat, _ = layernorm(frames[...].astype(F32))
    normed[...] = (xhat * gain[...]).astype(BF)


def dattn_kernel(pos, grad_out, w_out, wq, wk, wv, dattn, w_head):
    w_head[:, :128] = wq[...]
    w_head[:, 128:256] = wk[...]
    w_head[:, 256:] = wv[...]
    full = mm(grad_out[...], w_out[...], 1, 1).astype(BF)
    for h in range(HEADS):
        dattn[h] = full[:, h * 128 : (h + 1) * 128]


def forward_kernel(scale, pos, *refs):
    parts, (key_tag, query_tag, attn, probs, qkv, q_s, k_s, vt_s) = refs[:8], refs[8:]
    rows = parts[0].shape[0]
    for r in range(8):
        rng = pl.ds(pl.multiple_of((pos[0] ^ r) * rows, rows), rows)
        qkv[rng, :] = parts[r][...]
        q_s[rng, :128] = parts[r][:, :128]
        k_s[rng, :128] = parts[r][:, 128:256]
    vt_s[...] = qkv[:, 256:].T
    q_s[:, 128:] = query_tag[...]
    k_s[:, 128:] = key_tag[...]

    def step(i, carry):
        for u in range(UNROLL):
            block = i * UNROLL + u
            rng = pl.ds(pl.multiple_of(block * rows, rows), rows)
            scores = mm(k_s[...], q_s[rng, :], 1, 1)
            peak = jnp.max(scores, axis=0, keepdims=True)
            expo = jnp.exp2((scores - peak) * (scale * LOG2E))
            low = (expo * (1.0 / jnp.sum(expo, axis=0, keepdims=True))).astype(BF)
            probs[block] = low
            attn[rng, :] = mm(vt_s[...], low, 1, 0).T.astype(BF)
        return carry

    lax.fori_loop(0, 8 // UNROLL, step, 0)


def forward(pos, parts, key_tag, query_tag, scale):
    rows = parts[0].shape[0]
    total = 8 * rows
    return call(
        functools.partial(forward_kernel, scale),
        "forward",
        (shape(BF, total, 128), shape(BF, 8, total, rows), shape(BF, total, 384)),
        in_specs=[SCALARS] + [WHOLE] * 10,
        out_specs=(WHOLE,) * 3,
        scratch_shapes=[
            pltpu.VMEM((total, 256), BF),
            pltpu.VMEM((total, 256), BF),
            pltpu.VMEM((128, total), BF),
        ],
    )(pos, *parts, key_tag, query_tag)


def backward_kernel(scale, qkv, dout, attn, probs, dqkv, kt_s, dk_s, dv_s):
    rows = dout.shape[1]
    kt_s[...] = qkv[:, 128:256].T
    dk_s[...] = jnp.zeros_like(dk_s)
    dv_s[...] = jnp.zeros_like(dv_s)

    def step(i, carry):
        for u in range(UNROLL):
            block = i * UNROLL + u
            rng = pl.ds(pl.multiple_of(block * rows, rows), rows)
            do, low = dout[block], probs[block]
            delta = jnp.sum((attn[rng, :].astype(F32) * do.astype(F32)).T, axis=0, keepdims=True)
            dprobs = mm(qkv[:, 256:], do, 1, 1)
            dscores = (low.astype(F32) * (dprobs - delta)).astype(BF)
            dk_s[...] += mm(dscores, qkv[rng, :128], 1, 0)
            dv_s[...] += mm(low, do, 1, 0)
            dqkv[rng, :128] = (mm(kt_s[...], dscores, 1, 0) * scale).T.astype(BF)
        return carry

    lax.fori_loop(0, 8 // UNROLL, step, 0)
    dqkv[:, 128:256] = (dk_s[...] * scale).astype(BF)
    dqkv[:, 256:] = dv_s[...].astype(BF)


def backward(qkv, dout, attn, probs, scale):
    total = qkv.shape[0]
    return call(
        functools.partial(backward_kernel, scale),
        "backward",
        shape(BF, total, 384),
        in_specs=[WHOLE] * 4,
        out_specs=WHOLE,
        scratch_shapes=[
            pltpu.VMEM((128, total), BF),
            pltpu.VMEM((total, 128), F32),
            pltpu.VMEM((total, 128), F32),
        ],
    )(qkv, dout, attn, probs)


def split_rows(dp, source, keep, other):
    for r in range(16):
        half = other if r & 1 else keep
        for s in range(8):
            rows = pl.ds(pl.multiple_of(s * 128 + (dp ^ r) * 8, 8), 8)
            half[(r >> 1) * 64 + s * 8 : (r >> 1) * 64 + s * 8 + 8, :] = source[rows, :]


def projection_kernel(pos, *refs):
    normed = refs[:8]
    dqkv, weights, gain, keep, send, gain_part, grad, other = refs[8:]
    rows = normed[0].shape[0]
    total = None
    for r in range(8):
        rng = pl.ds(pl.multiple_of((pos[0] ^ r) * rows, rows), rows)
        term = mm(dqkv[rng, :], normed[r][...], 0, 0)
        total = term if total is None else total + term
    grad[...] = total.T
    gain_part[...] = (
        jnp.sum(grad[...] * weights[...].astype(F32), axis=1, keepdims=True) / gain[...]
    )
    split_rows(pos[1], grad, keep, other)
    send[...] = other[...].astype(BF)


def projection_gradient(pos, normed, dqkv, weights, gain):
    return call(
        projection_kernel,
        "projection_gradient",
        (shape(F32, 512, 384), shape(BF, 512, 384), shape(F32, 1024, 1)),
        in_specs=[SCALARS] + [WHOLE] * 11,
        out_specs=(WHOLE,) * 3,
        scratch_shapes=[pltpu.VMEM((1024, 384), F32), pltpu.VMEM((512, 384), F32)],
        cost_estimate=SMALL,
    )(pos, *normed, dqkv, weights, gain)


def output_kernel(pos, attn, grad_out, w_out, frames, layer_out, keep, send, grad, other):
    total = frames[...].astype(F32)
    for h in range(HEADS):
        rows = slice(h * 128, (h + 1) * 128)
        total += mm(attn[h], w_out[rows, :], 1, 0)
        grad[rows, :] = mm(attn[h], grad_out[...], 0, 0)
    layer_out[...] = total.astype(BF)
    split_rows(pos[1], grad, keep, other)
    send[...] = other[...].astype(BF)


def output_projection(pos, attn, grad_out, w_out, frames):
    return call(
        output_kernel,
        "output_projection",
        (shape(BF, *frames.shape), shape(F32, 512, 1024), shape(BF, 512, 1024)),
        in_specs=[SCALARS] + [WHOLE] * 4,
        out_specs=(WHOLE,) * 3,
        scratch_shapes=[pltpu.VMEM((1024, 1024), F32), pltpu.VMEM((512, 1024), F32)],
        cost_estimate=SMALL,
    )(pos, attn, grad_out, w_out, frames)


def frame_kernel(dqkv, wq, wk, wv, frames, gain, grad_out, result, total):
    h = pl.program_id(0)
    weights = jnp.concatenate([wq[...], wk[...], wv[...]], axis=1)
    term = mm(weights, dqkv[0], 1, 1)

    @pl.when(h == 0)
    def _():
        total[...] = term

    @pl.when(h > 0)
    def _():
        total[...] += term

    @pl.when(h == HEADS - 1)
    def _():
        xhat, rstd = layernorm(frames[...].astype(F32))
        g = total[...].T * gain[...]
        mean_g = jnp.mean(g, axis=-1, keepdims=True)
        mean_gx = jnp.mean(g * xhat, axis=-1, keepdims=True)
        result[...] = (
            grad_out[...].astype(F32) + rstd * (g - mean_g - xhat * mean_gx)
        ).astype(BF)


def frame_gradient(dqkv, w_qkv, frames, gain, grad_out):
    rows, width = frames.shape
    return call(
        frame_kernel,
        "frame_gradient",
        shape(BF, rows, width),
        grid=(HEADS,),
        in_specs=[pl.BlockSpec((1, rows, 384), lambda h: (h, 0, 0))]
        + [pl.BlockSpec((width, 128), lambda h, t=t: (0, t * HEADS + h)) for t in range(3)]
        + [WHOLE] * 3,
        out_specs=WHOLE,
        scratch_shapes=[pltpu.VMEM((width, rows), F32)],
    )(dqkv, w_qkv, w_qkv, w_qkv, frames, gain, grad_out)


def high_low(x):
    high = lax.reduce_precision(x, 8, 7)
    low = lax.reduce_precision(x - high, 8, 7)
    return high, low


def packed(x, columns):
    high, low = high_low(x)
    both = jnp.concatenate([high, low], axis=1).astype(BF)
    return jnp.pad(both, ((0, 0), (0, columns - 256)))


def unpacked(x):
    return x[:, :128].astype(F32) + x[:, 128:256].astype(F32)


def settled(x):
    high, low = high_low(x)
    return high + low


def on_device(frames, layernorm_gain, w_qkv, w_out, segment_ids, output_gradient):
    x = frames[0]
    grad_out = output_gradient[0]
    rows, width = x.shape
    head = width // HEADS
    scale = head**-0.5
    pos = jnp.stack([lax.axis_index("seq"), lax.axis_index("dp")]).astype(jnp.int32)
    gain_row = layernorm_gain[None, :]

    normed = [None] * 8
    normed[0] = call(
        layernorm_kernel, "layernorm", shape(BF, rows, width), in_specs=[WHOLE] * 2, out_specs=WHOLE
    )(x, gain_row)
    normed[1] = seq_swap(normed[0], 1)
    normed[2] = seq_swap(normed[0], 2)
    normed[6] = seq_swap(normed[0], 6)
    half = rows // 2
    far = [seq_swap(normed[2][:half], 6), seq_swap(normed[6][half:], 2)]
    normed[3] = seq_swap(normed[1], 2)
    normed[7] = seq_swap(normed[1], 6)
    beyond = [seq_swap(part, 1) for part in far]

    dattn, w_head = pl.pallas_call(
        dattn_kernel,
        out_shape=(shape(BF, HEADS, rows, head), shape(BF, width, 384)),
        grid_spec=pltpu.PrefetchScalarGridSpec(
            num_scalar_prefetch=1,
            grid=(1,),
            in_specs=[WHOLE] * 2
            + [
                pl.BlockSpec((width, head), lambda i, p, t=t: (0, t * HEADS + p[0]))
                for t in range(3)
            ],
            out_specs=(WHOLE, WHOLE),
        ),
        compiler_params=pltpu.CompilerParams(vmem_limit_bytes=VMEM_LIMIT),
        name="dattn",
    )(pos, grad_out, w_out, w_qkv, w_qkv, w_qkv)
    dout = seq_exchange(dattn)

    normed[4] = jnp.concatenate(far, axis=0)
    normed[5] = jnp.concatenate(beyond, axis=0)
    parts = [mm(n, w_head, 1, 0).astype(BF) for n in normed]
    same = segment_ids[0][:, None] == jnp.arange(128)[None, :]
    key_tag = same.astype(BF)
    query_tag = jnp.where(same, 0.0, -1e30).astype(BF)

    attn_head, probs, qkv = forward(pos, parts, key_tag, query_tag, scale)
    attn = seq_exchange(attn_head.reshape(8, rows, head))
    dqkv_head = backward(qkv, dout, attn_head, probs, scale)

    dqkv = seq_exchange(dqkv_head.reshape(8, rows, 384))
    attn, dqkv_head = lax.optimization_barrier((attn, dqkv_head))
    layer_out, wout_keep, wout_send = output_projection(pos, attn, grad_out, w_out, x)
    wout_send, dqkv_head = lax.optimization_barrier((wout_send, dqkv_head))
    wout_sum = wout_keep + dp_swap(wout_send, 1).astype(F32)
    wqkv_keep, wqkv_send, gain_part = projection_gradient(
        pos, normed, dqkv_head, w_head, layernorm_gain[:, None]
    )
    gain_part = gain_part.reshape(8, 128)
    got = dp_swap(jnp.concatenate([wqkv_send, packed(gain_part, 384)], axis=0), 1)
    wqkv_sum = wqkv_keep + got[:512].astype(F32)
    gain_sum = settled(gain_part) + unpacked(got[512:])
    wout_sum = wout_sum.reshape(4, 128, 1024)
    got_out = [dp_swap(wout_sum[r].astype(BF), 4 * r) for r in range(1, 4)]
    wqkv_sum = wqkv_sum.reshape(4, 128, 384)
    note = packed(gain_sum, 384)
    got = [
        dp_swap(jnp.concatenate([wqkv_sum[r].astype(BF), note], axis=0), 4 * r)
        for r in range(1, 4)
    ]
    dqkv, got, got_out = lax.optimization_barrier((dqkv, got, got_out))
    frame_grad = frame_gradient(dqkv, w_qkv, x, gain_row, grad_out)
    wout_sum = wout_sum[0] + sum(part.astype(F32) for part in got_out)
    wout_sum = wout_sum[:64] + dp_swap(wout_sum[64:].astype(BF), 2).astype(F32)
    wqkv_sum = wqkv_sum[0] + sum(part[:128].astype(F32) for part in got)
    notes = [settled(gain_sum)] + [unpacked(part[128:]) for part in got]
    gain_sum = (notes[0] + notes[1]) + (notes[2] + notes[3])
    got = dp_swap(jnp.concatenate([wqkv_sum[64:].astype(BF), packed(gain_sum, 384)], axis=0), 2)
    wqkv_sum = wqkv_sum[:64] + got[:64].astype(F32)
    gain_sum = settled(gain_sum) + unpacked(got[64:])
    sums = jnp.concatenate([wqkv_sum, wout_sum], axis=1)

    note = jnp.broadcast_to(packed(gain_sum, 256)[None], (8, 8, 256))
    got = seq_exchange(jnp.concatenate([sums.reshape(8, 8, 1408).astype(BF), note], axis=2))
    grad_wqkv = got[:, :, :384].reshape(8, 8, 3, head).transpose(1, 2, 0, 3).reshape(8, 3 * width)
    grad_wout = jnp.sum(got[:, :, 384:1408].astype(F32), axis=0).astype(BF)
    totals = [unpacked(got[s, :, 1408:]) for s in range(8)]
    grad_gain = functools.reduce(lambda a, b: a + b, totals).reshape(width)
    return (
        layer_out[None],
        frame_grad[None],
        grad_wqkv,
        grad_wout,
        grad_gain,
    )


def solution(mesh):
    placed = (P("dp", "seq", None), P(), P(), P(), P("dp", None), P("dp", "seq", None))
    return jax.shard_map(
        on_device,
        mesh=mesh,
        in_specs=placed,
        out_specs=(
            P("dp", "seq", None),
            P("dp", "seq", None),
            P(("seq", "dp"), None),
            P(("seq", "dp"), None),
            P(),
        ),
        check_vma=False,
    )
```

```python
import functools

import jax
import jax.numpy as jnp
from jax import lax
from jax.experimental import pallas as pl
from jax.experimental.pallas import tpu as pltpu
from jax.sharding import PartitionSpec as P

HEADS = 8
BF = jnp.bfloat16
F32 = jnp.float32
LOG2E = 1.4426950408889634
PAIR = 2
VMEM_LIMIT = 36 * 1024 * 1024
WHOLE = pl.BlockSpec(memory_space=pltpu.VMEM)
SCALARS = pl.BlockSpec(memory_space=pltpu.SMEM)


def seq_swap(x, bits):
    return lax.ppermute(x, "seq", [(i, i ^ bits) for i in range(8)])


def dp_swap(x, bits):
    return lax.ppermute(x, "dp", [(i, i ^ bits) for i in range(16)])


def seq_exchange(x):
    return lax.all_to_all(x, "seq", 0, 0, tiled=True)


def mm(a, b, ca, cb):
    return lax.dot_general(a, b, (((ca,), (cb,)), ((), ())), preferred_element_type=F32)


def call(kernel, name, out_shape, **options):
    return pl.pallas_call(
        kernel,
        out_shape=out_shape,
        compiler_params=pltpu.CompilerParams(vmem_limit_bytes=VMEM_LIMIT),
        name=name,
        **options,
    )


def shape(dtype, *dims):
    return jax.ShapeDtypeStruct(dims, dtype)


def layernorm(x):
    center = x - jnp.mean(x, axis=-1, keepdims=True)
    rstd = lax.rsqrt(jnp.mean(center * center, axis=-1, keepdims=True) + 1e-05)
    return center * rstd, rstd


def layernorm_kernel(frames, gain, normed):
    xhat, _ = layernorm(frames[...].astype(F32))
    normed[...] = (xhat * gain[...]).astype(BF)


def dattn_kernel(pos, grad_out, w_out, wq, wk, wv, dattn, w_head):
    w_head[:, :128] = wq[...]
    w_head[:, 128:256] = wk[...]
    w_head[:, 256:] = wv[...]
    full = mm(grad_out[...], w_out[...], 1, 1).astype(BF)
    for h in range(HEADS):
        dattn[h] = full[:, h * 128 : (h + 1) * 128]


def forward_kernel(scale, pos, *refs):
    parts, (key_tag, query_tag, attn, probs, qkv, q_s, k_s, vt_s) = refs[:8], refs[8:]
    rows = parts[0].shape[0]
    i = pl.program_id(0)

    @pl.when(i == 0)
    def _():
        for r in range(8):
            rng = pl.ds(pl.multiple_of((pos[0] ^ r) * rows, rows), rows)
            qkv[rng, :] = parts[r][...]
            q_s[rng, :128] = parts[r][:, :128]
            k_s[rng, :128] = parts[r][:, 128:256]
        vt_s[...] = qkv[:, 256:].T
        q_s[:, 128:] = query_tag[...]
        k_s[:, 128:] = key_tag[...]

    for u in range(PAIR):
        rng = pl.ds(pl.multiple_of((i * PAIR + u) * rows, rows), rows)
        scores = mm(k_s[...], q_s[rng, :], 1, 1)
        peak = jnp.max(scores, axis=0, keepdims=True)
        expo = jnp.exp2((scores - peak) * (scale * LOG2E))
        low = (expo * (1.0 / jnp.sum(expo, axis=0, keepdims=True))).astype(BF)
        probs[u] = low
        attn[u * rows : (u + 1) * rows, :] = mm(vt_s[...], low, 1, 0).T.astype(BF)


def forward(pos, parts, key_tag, query_tag, scale):
    rows = parts[0].shape[0]
    total = 8 * rows
    return call(
        functools.partial(forward_kernel, scale),
        "forward",
        (shape(BF, total, 128), shape(BF, 8, total, rows), shape(BF, total, 384)),
        grid=(8 // PAIR,),
        in_specs=[SCALARS] + [WHOLE] * 10,
        out_specs=(
            pl.BlockSpec((PAIR * rows, 128), lambda i: (i, 0)),
            pl.BlockSpec((PAIR, total, rows), lambda i: (i, 0, 0)),
            WHOLE,
        ),
        scratch_shapes=[
            pltpu.VMEM((total, 256), BF),
            pltpu.VMEM((total, 256), BF),
            pltpu.VMEM((128, total), BF),
        ],
    )(pos, *parts, key_tag, query_tag)


def backward_kernel(scale, qkv, dout, attn, probs, dqkv, kt_s, dk_s, dv_s):
    rows = dout.shape[1]
    i = pl.program_id(0)

    @pl.when(i == 0)
    def _():
        kt_s[...] = qkv[:, 128:256].T
        dk_s[...] = jnp.zeros_like(dk_s)
        dv_s[...] = jnp.zeros_like(dv_s)

    for u in range(PAIR):
        rng = pl.ds(pl.multiple_of((i * PAIR + u) * rows, rows), rows)
        do, low = dout[u], probs[u]
        out = attn[u * rows : (u + 1) * rows, :]
        delta = jnp.sum((out.astype(F32) * do.astype(F32)).T, axis=0, keepdims=True)
        dprobs = mm(qkv[:, 256:], do, 1, 1)
        dscores = (low.astype(F32) * (dprobs - delta)).astype(BF)
        dk_s[...] += mm(dscores, qkv[rng, :128], 1, 0)
        dv_s[...] += mm(low, do, 1, 0)
        dqkv[rng, :128] = (mm(kt_s[...], dscores, 1, 0) * scale).T.astype(BF)

    @pl.when(i == 8 // PAIR - 1)
    def _():
        dqkv[:, 128:256] = (dk_s[...] * scale).astype(BF)
        dqkv[:, 256:] = dv_s[...].astype(BF)


def backward(qkv, dout, attn, probs, scale):
    total = qkv.shape[0]
    rows = total // 8
    return call(
        functools.partial(backward_kernel, scale),
        "backward",
        shape(BF, total, 384),
        grid=(8 // PAIR,),
        in_specs=[
            WHOLE,
            pl.BlockSpec((PAIR, rows, 128), lambda i: (i, 0, 0)),
            pl.BlockSpec((PAIR * rows, 128), lambda i: (i, 0)),
            pl.BlockSpec((PAIR, total, rows), lambda i: (i, 0, 0)),
        ],
        out_specs=WHOLE,
        scratch_shapes=[
            pltpu.VMEM((128, total), BF),
            pltpu.VMEM((total, 128), F32),
            pltpu.VMEM((total, 128), F32),
        ],
    )(qkv, dout, attn, probs)


def split_rows(dp, source, keep, other):
    for r in range(16):
        half = other if r & 1 else keep
        for s in range(8):
            rows = pl.ds(pl.multiple_of(s * 128 + (dp ^ r) * 8, 8), 8)
            half[(r >> 1) * 64 + s * 8 : (r >> 1) * 64 + s * 8 + 8, :] = source[rows, :]


def projection_kernel(pos, *refs):
    normed = refs[:8]
    dqkv, weights, gain, keep, send, gain_part, grad, other = refs[8:]
    rows = normed[0].shape[0]
    total = None
    for r in range(8):
        rng = pl.ds(pl.multiple_of((pos[0] ^ r) * rows, rows), rows)
        term = mm(dqkv[rng, :], normed[r][...], 0, 0)
        total = term if total is None else total + term
    grad[...] = total.T
    gain_part[...] = (
        jnp.sum(grad[...] * weights[...].astype(F32), axis=1, keepdims=True) / gain[...]
    )
    split_rows(pos[1], grad, keep, other)
    send[...] = other[...].astype(BF)


def projection_gradient(pos, normed, dqkv, weights, gain):
    return call(
        projection_kernel,
        "projection_gradient",
        (shape(F32, 512, 384), shape(BF, 512, 384), shape(F32, 1024, 1)),
        in_specs=[SCALARS] + [WHOLE] * 11,
        out_specs=(WHOLE,) * 3,
        scratch_shapes=[pltpu.VMEM((1024, 384), F32), pltpu.VMEM((512, 384), F32)],
    )(pos, *normed, dqkv, weights, gain)


def output_gradient_kernel(
    pos, attn, attn_twin, grad_out, grad_twin, send_near, send_far, keep, middle, grad, chosen
):
    for h in range(HEADS):
        rows = slice(h * 128, (h + 1) * 128)
        grad[rows, :] = mm(attn[h], grad_out[...], 0, 0) + mm(attn_twin[h], grad_twin[...], 0, 0)
    for r in range(8):
        for s in range(8):
            rows = pl.ds(pl.multiple_of(s * 128 + (pos[1] ^ (2 * r)) * 8, 8), 8)
            chosen[r * 64 + s * 8 : r * 64 + s * 8 + 8, :] = grad[rows, :]
    send_near[...] = chosen[128:384, :512].astype(BF)
    send_far[...] = chosen[256:, 512:].astype(BF)
    keep[...] = chosen[:128, :]
    middle[:, :512] = chosen[384:, :512]
    middle[:, 512:] = chosen[128:256, 512:]


def output_weight_gradient(pos, attn, attn_twin, grad_out, grad_twin):
    return call(
        output_gradient_kernel,
        "output_gradient",
        (
            shape(BF, 256, 512),
            shape(BF, 256, 512),
            shape(F32, 128, 1024),
            shape(F32, 128, 1024),
        ),
        in_specs=[SCALARS] + [WHOLE] * 4,
        out_specs=(WHOLE,) * 4,
        scratch_shapes=[pltpu.VMEM((1024, 1024), F32), pltpu.VMEM((512, 1024), F32)],
    )(pos, attn, attn_twin, grad_out, grad_twin)


def result_kernel(dqkv, attn, w_qkv, w_out, frames, gain, grad_out, layer_out, result):
    width = frames.shape[1]
    x = frames[...].astype(F32)
    total, out = None, x
    for h in range(HEADS):
        cols = [slice(t * width + h * 128, t * width + (h + 1) * 128) for t in range(3)]
        weights = jnp.concatenate([w_qkv[:, c] for c in cols], axis=1)
        term = mm(weights, dqkv[h], 1, 1)
        total = term if total is None else total + term
        out = out + mm(attn[h], w_out[h * 128 : (h + 1) * 128, :], 1, 0)
    layer_out[...] = out.astype(BF)
    xhat, rstd = layernorm(x)
    g = total.T * gain[...]
    mean_g = jnp.mean(g, axis=-1, keepdims=True)
    mean_gx = jnp.mean(g * xhat, axis=-1, keepdims=True)
    result[...] = (grad_out[...].astype(F32) + rstd * (g - mean_g - xhat * mean_gx)).astype(BF)


def results(dqkv, attn, w_qkv, w_out, frames, gain, grad_out):
    return call(
        result_kernel,
        "results",
        (shape(BF, *frames.shape),) * 2,
        in_specs=[WHOLE] * 7,
        out_specs=(WHOLE,) * 2,
    )(dqkv, attn, w_qkv, w_out, frames, gain, grad_out)


def high_low(x):
    high = lax.reduce_precision(x, 8, 7)
    low = lax.reduce_precision(x - high, 8, 7)
    return high, low


def packed(x, columns):
    high, low = high_low(x)
    both = jnp.concatenate([high, low], axis=1).astype(BF)
    return jnp.pad(both, ((0, 0), (0, columns - 256)))


def unpacked(x):
    return x[:, :128].astype(F32) + x[:, 128:256].astype(F32)


def settled(x):
    high, low = high_low(x)
    return high + low


def on_device(frames, layernorm_gain, w_qkv, w_out, segment_ids, output_gradient):
    x = frames[0]
    grad_out = output_gradient[0]
    rows, width = x.shape
    head = width // HEADS
    scale = head**-0.5
    pos = jnp.stack([lax.axis_index("seq"), lax.axis_index("dp")]).astype(jnp.int32)
    gain_row = layernorm_gain[None, :]

    normed = [None] * 8
    normed[0] = call(
        layernorm_kernel, "layernorm", shape(BF, rows, width), in_specs=[WHOLE] * 2, out_specs=WHOLE
    )(x, gain_row)
    grad_twin = dp_swap(grad_out, 1)
    normed[1] = seq_swap(normed[0], 1)
    normed[2] = seq_swap(normed[0], 2)
    normed[6] = seq_swap(normed[0], 6)
    half = rows // 2
    far = [seq_swap(normed[2][:half], 6), seq_swap(normed[6][half:], 2)]
    normed[3] = seq_swap(normed[1], 2)
    normed[7] = seq_swap(normed[1], 6)
    beyond = [seq_swap(part, 1) for part in far]
    normed[4] = jnp.concatenate(far, axis=0)
    normed[5] = jnp.concatenate(beyond, axis=0)

    dattn, w_head = pl.pallas_call(
        dattn_kernel,
        out_shape=(shape(BF, HEADS, rows, head), shape(BF, width, 384)),
        grid_spec=pltpu.PrefetchScalarGridSpec(
            num_scalar_prefetch=1,
            grid=(1,),
            in_specs=[WHOLE] * 2
            + [
                pl.BlockSpec((width, head), lambda i, p, t=t: (0, t * HEADS + p[0]))
                for t in range(3)
            ],
            out_specs=(WHOLE, WHOLE),
        ),
        compiler_params=pltpu.CompilerParams(vmem_limit_bytes=VMEM_LIMIT),
        name="dattn",
    )(pos, grad_out, w_out, w_qkv, w_qkv, w_qkv)
    dattn, grad_twin, _ = lax.optimization_barrier((dattn, grad_twin, far))
    dout = seq_exchange(dattn)

    parts = [mm(n, w_head, 1, 0).astype(BF) for n in normed]
    same = segment_ids[0][:, None] == jnp.arange(128)[None, :]
    key_tag = same.astype(BF)
    query_tag = jnp.where(same, 0.0, -1e30).astype(BF)

    attn_head, probs, qkv = forward(pos, parts, key_tag, query_tag, scale)
    attn = seq_exchange(attn_head.reshape(8, rows, head))
    dqkv_head = backward(qkv, dout, attn_head, probs, scale)
    dqkv = seq_exchange(dqkv_head.reshape(8, rows, 384))

    attn, dqkv_head = lax.optimization_barrier((attn, dqkv_head))
    attn_twin = dp_swap(attn, 1)
    near, away, wout_sum, middle = output_weight_gradient(
        pos, attn, attn_twin, grad_out, grad_twin
    )
    wqkv_keep, wqkv_send, gain_part = projection_gradient(
        pos, normed, dqkv_head, w_head, layernorm_gain[:, None]
    )
    near, away, wqkv_send = lax.optimization_barrier((near, away, wqkv_send))
    layer_out, frame_grad = results(dqkv, attn, w_qkv, w_out, x, gain_row, grad_out)

    gain_part = gain_part.reshape(8, 128)
    got = dp_swap(jnp.concatenate([wqkv_send, packed(gain_part, 384)], axis=0), 1)
    near, away = dp_swap(near, 4), dp_swap(away, 12)
    near, away, got = lax.optimization_barrier((near, away, got))
    near_next = dp_swap((middle[:, :512] + near[128:].astype(F32)).astype(BF), 12)
    away_next = dp_swap((middle[:, 512:] + away[:128].astype(F32)).astype(BF), 4)
    wout_sum = wout_sum + jnp.concatenate(
        [
            near[:128].astype(F32) + near_next.astype(F32),
            away[128:].astype(F32) + away_next.astype(F32),
        ],
        axis=1,
    )
    wout_sum = wout_sum[:64] + dp_swap(wout_sum[64:].astype(BF), 2).astype(F32)

    wqkv_sum = wqkv_keep + got[:512].astype(F32)
    gain_sum = settled(gain_part) + unpacked(got[512:])
    wqkv_sum = wqkv_sum.reshape(4, 128, 384)
    note = packed(gain_sum, 384)
    got = [
        dp_swap(jnp.concatenate([wqkv_sum[r].astype(BF), note], axis=0), 4 * r)
        for r in range(1, 4)
    ]
    wqkv_sum = wqkv_sum[0] + sum(part[:128].astype(F32) for part in got)
    notes = [settled(gain_sum)] + [unpacked(part[128:]) for part in got]
    gain_sum = (notes[0] + notes[1]) + (notes[2] + notes[3])
    got = dp_swap(jnp.concatenate([wqkv_sum[64:].astype(BF), packed(gain_sum, 384)], axis=0), 2)
    wqkv_sum = wqkv_sum[:64] + got[:64].astype(F32)
    gain_sum = settled(gain_sum) + unpacked(got[64:])
    sums = jnp.concatenate([wqkv_sum, wout_sum], axis=1)

    note = jnp.broadcast_to(packed(gain_sum, 256)[None], (8, 8, 256))
    got = seq_exchange(jnp.concatenate([sums.reshape(8, 8, 1408).astype(BF), note], axis=2))
    grad_wqkv = got[:, :, :384].reshape(8, 8, 3, head).transpose(1, 2, 0, 3).reshape(8, 3 * width)
    grad_wout = jnp.sum(got[:, :, 384:1408].astype(F32), axis=0).astype(BF)
    totals = [unpacked(got[s, :, 1408:]) for s in range(8)]
    grad_gain = functools.reduce(lambda a, b: a + b, totals).reshape(width)
    return (
        layer_out[None],
        frame_grad[None],
        grad_wqkv,
        grad_wout,
        grad_gain,
    )


def solution(mesh):
    placed = (P("dp", "seq", None), P(), P(), P(), P("dp", None), P("dp", "seq", None))
    return jax.shard_map(
        on_device,
        mesh=mesh,
        in_specs=placed,
        out_specs=(
            P("dp", "seq", None),
            P("dp", "seq", None),
            P(("seq", "dp"), None),
            P(("seq", "dp"), None),
            P(),
        ),
        check_vma=False,
    )
```

```python
import functools

import jax
import jax.numpy as jnp
from jax import lax
from jax.experimental import pallas as pl
from jax.experimental.pallas import tpu as pltpu
from jax.sharding import PartitionSpec as P

HEADS = 8
BF = jnp.bfloat16
F32 = jnp.float32
LOG2E = 1.4426950408889634
PAIR = 2
VMEM_LIMIT = 60 * 1024 * 1024
WHOLE = pl.BlockSpec(memory_space=pltpu.VMEM)
SCALARS = pl.BlockSpec(memory_space=pltpu.SMEM)


def seq_swap(x, bits):
    return lax.ppermute(x, "seq", [(i, i ^ bits) for i in range(8)])


def dp_swap(x, bits):
    return lax.ppermute(x, "dp", [(i, i ^ bits) for i in range(16)])


def seq_exchange(x):
    return lax.all_to_all(x, "seq", 0, 0, tiled=True)


def mm(a, b, ca, cb):
    return lax.dot_general(a, b, (((ca,), (cb,)), ((), ())), preferred_element_type=F32)


def call(kernel, name, out_shape, **options):
    return pl.pallas_call(
        kernel,
        out_shape=out_shape,
        compiler_params=pltpu.CompilerParams(vmem_limit_bytes=VMEM_LIMIT),
        name=name,
        **options,
    )


def shape(dtype, *dims):
    return jax.ShapeDtypeStruct(dims, dtype)


def layernorm(x):
    center = x - jnp.mean(x, axis=-1, keepdims=True)
    rstd = lax.rsqrt(jnp.mean(center * center, axis=-1, keepdims=True) + 1e-05)
    return center * rstd, rstd


def staged(body, name, out_shape, scalars, arrays, plain=(), left=(), scratch=()):
    n, m, k = len(scalars), len(arrays), len(plain) + len(left)

    def kernel(*refs):
        sources, others = refs[n : n + m], refs[n + m : n + m + k]
        outs = refs[n + m + k : n + m + k + len(out_shape)]
        rest = refs[n + m + k + len(out_shape) :]
        buffers, semaphores, rest = rest[:m], rest[m], rest[m + 1 :]
        copies = [
            pltpu.make_async_copy(sources[i], buffers[i], semaphores.at[i]) for i in range(m)
        ]
        for copy in copies:
            copy.start()
        waited = set()

        def get(i):
            if i not in waited:
                waited.add(i)
                copies[i].wait()
            return buffers[i]

        body(*refs[:n], get, *others, *outs, *rest)
        for i in range(m):
            get(i)

    return call(
        kernel,
        name,
        tuple(out_shape),
        in_specs=[SCALARS] * n
        + [pl.BlockSpec(memory_space=pltpu.HBM)] * m
        + [WHOLE] * len(plain)
        + [pl.BlockSpec(memory_space=pltpu.HBM)] * len(left),
        out_specs=(WHOLE,) * len(out_shape),
        scratch_shapes=[pltpu.VMEM(a.shape, a.dtype) for a in arrays]
        + [pltpu.SemaphoreType.DMA((m,))]
        + list(scratch),
    )(*scalars, *arrays, *plain, *left)


def layernorm_kernel(get, gain, normed):
    xhat, _ = layernorm(get(0)[...].astype(F32))
    normed[...] = (xhat * gain[...]).astype(BF)


def dattn_kernel(pos, get, w_qkv, dattn, w_head, semaphores):
    copies = []
    for t in range(3):
        start = pl.multiple_of(t * 1024 + pos[0] * 128, 128)
        copies.append(
            pltpu.make_async_copy(
                w_qkv.at[:, pl.ds(start, 128)],
                w_head.at[:, t * 128 : (t + 1) * 128],
                semaphores.at[t],
            )
        )
    for copy in copies:
        copy.start()
    full = mm(get(0)[...], get(1)[...], 1, 1).astype(BF)
    for h in range(HEADS):
        dattn[h] = full[:, h * 128 : (h + 1) * 128]
    for copy in copies:
        copy.wait()


def forward_kernel(scale, places, pos, *refs):
    count = len(places)
    parts, (ids, attn, probs, qkv, q_s, k_s, vt_s) = refs[:count], refs[count:]
    rows = qkv.shape[0] // 8
    i = pl.program_id(0)

    @pl.when(i == 0)
    def _():
        for part, (r, offset) in zip(parts, places):
            size = part.shape[0]
            rng = pl.ds(pl.multiple_of((pos[0] ^ r) * rows + offset, size), size)
            qkv[rng, :] = part[...]
            q_s[rng, :128] = part[:, :128]
            k_s[rng, :128] = part[:, 128:256]
        vt_s[...] = qkv[:, 256:].T
        names = lax.broadcasted_iota(jnp.int32, (128, 8 * rows), 0)
        same = jnp.where(ids[...] == names, 1.0, 0.0).T
        k_s[:, 128:] = same.astype(BF)
        q_s[:, 128:] = ((same - 1.0) * 1e30).astype(BF)

    for u in range(PAIR):
        rng = pl.ds(pl.multiple_of((i * PAIR + u) * rows, rows), rows)
        scores = mm(k_s[...], q_s[rng, :], 1, 1)
        peak = jnp.max(scores, axis=0, keepdims=True)
        expo = jnp.exp2((scores - peak) * (scale * LOG2E))
        low = (expo * (1.0 / jnp.sum(expo, axis=0, keepdims=True))).astype(BF)
        probs[u] = low
        attn[u * rows : (u + 1) * rows, :] = mm(vt_s[...], low, 1, 0).T.astype(BF)


def forward(pos, parts, places, ids, rows, scale):
    total = 8 * rows
    return call(
        functools.partial(forward_kernel, scale, places),
        "forward",
        (shape(BF, total, 128), shape(BF, 8, total, rows), shape(BF, total, 384)),
        grid=(8 // PAIR,),
        in_specs=[SCALARS] + [WHOLE] * (len(parts) + 1),
        out_specs=(
            pl.BlockSpec((PAIR * rows, 128), lambda i: (i, 0)),
            pl.BlockSpec((PAIR, total, rows), lambda i: (i, 0, 0)),
            WHOLE,
        ),
        scratch_shapes=[
            pltpu.VMEM((total, 256), BF),
            pltpu.VMEM((total, 256), BF),
            pltpu.VMEM((128, total), BF),
        ],
    )(pos, *parts, ids)


def backward_kernel(scale, qkv, dout, attn, probs, dqkv, kt_s, dk_s, dv_s):
    rows = dout.shape[1]
    i = pl.program_id(0)

    @pl.when(i == 0)
    def _():
        kt_s[...] = qkv[:, 128:256].T
        dk_s[...] = jnp.zeros_like(dk_s)
        dv_s[...] = jnp.zeros_like(dv_s)

    for u in range(PAIR):
        rng = pl.ds(pl.multiple_of((i * PAIR + u) * rows, rows), rows)
        do, low = dout[u], probs[u]
        out = attn[u * rows : (u + 1) * rows, :]
        delta = jnp.sum((out.astype(F32) * do.astype(F32)).T, axis=0, keepdims=True)
        dprobs = mm(qkv[:, 256:], do, 1, 1)
        dscores = (low.astype(F32) * (dprobs - delta)).astype(BF)
        dk_s[...] += mm(dscores, qkv[rng, :128], 1, 0)
        dv_s[...] += mm(low, do, 1, 0)
        dqkv[rng, :128] = (mm(kt_s[...], dscores, 1, 0) * scale).T.astype(BF)

    @pl.when(i == 8 // PAIR - 1)
    def _():
        dqkv[:, 128:256] = (dk_s[...] * scale).astype(BF)
        dqkv[:, 256:] = dv_s[...].astype(BF)


def backward(qkv, dout, attn, probs, scale):
    total = qkv.shape[0]
    rows = total // 8
    return call(
        functools.partial(backward_kernel, scale),
        "backward",
        shape(BF, total, 384),
        grid=(8 // PAIR,),
        in_specs=[
            WHOLE,
            pl.BlockSpec((PAIR, rows, 128), lambda i: (i, 0, 0)),
            pl.BlockSpec((PAIR * rows, 128), lambda i: (i, 0)),
            pl.BlockSpec((PAIR, total, rows), lambda i: (i, 0, 0)),
        ],
        out_specs=WHOLE,
        scratch_shapes=[
            pltpu.VMEM((128, total), BF),
            pltpu.VMEM((total, 128), F32),
            pltpu.VMEM((total, 128), F32),
        ],
    )(qkv, dout, attn, probs)


def chosen_rows(dp, source, half, target):
    for r in range(8):
        for s in range(8):
            rows = pl.ds(pl.multiple_of(s * 128 + (dp ^ (2 * r + half)) * 8, 8), 8)
            target[r * 64 + s * 8 : r * 64 + s * 8 + 8, :] = source[rows, :]


def projection_kernel(places, pos, get, gain, keep, send, gain_part, grad, other):
    dqkv, weights = get(0), get(1)
    rows = dqkv.shape[0] // 8
    total = None
    for i, (r, offset) in enumerate(places):
        normed = get(2 + i)
        size = normed.shape[0]
        rng = pl.ds(pl.multiple_of((pos[0] ^ r) * rows + offset, size), size)
        term = mm(dqkv[rng, :], normed[...], 0, 0)
        total = term if total is None else total + term
    grad[...] = total.T
    gain_part[...] = (
        jnp.sum(grad[...] * weights[...].astype(F32), axis=1, keepdims=True) / gain[...]
    )
    chosen_rows(pos[1], grad, 0, keep)
    chosen_rows(pos[1], grad, 1, other)
    send[...] = other[...].astype(BF)


def output_gradient_kernel(pos, get, send_near, send_far, keep, middle, grad, chosen):
    for h in range(HEADS):
        rows = slice(h * 128, (h + 1) * 128)
        grad[rows, :] = mm(get(0)[h], get(1)[...], 0, 0) + mm(get(2)[h], get(3)[...], 0, 0)
    chosen_rows(pos[1], grad, 0, chosen)
    send_near[...] = chosen[128:384, :512].astype(BF)
    send_far[...] = chosen[256:, 512:].astype(BF)
    keep[...] = chosen[:128, :]
    middle[:, :512] = chosen[384:, :512]
    middle[:, 512:] = chosen[128:256, 512:]


def result_kernel(get, gain, layer_out, result):
    x = get(0)[...].astype(F32)
    width = x.shape[1]
    out = x
    for h in range(HEADS):
        out = out + mm(get(1)[h], get(2)[h * 128 : (h + 1) * 128, :], 1, 0)
    layer_out[...] = out.astype(BF)
    total = None
    for h in range(HEADS):
        cols = [slice(t * width + h * 128, t * width + (h + 1) * 128) for t in range(3)]
        weights = jnp.concatenate([get(5)[:, c] for c in cols], axis=1)
        term = mm(weights, get(3)[h], 1, 1)
        total = term if total is None else total + term
    xhat, rstd = layernorm(x)
    g = total.T * gain[...]
    mean_g = jnp.mean(g, axis=-1, keepdims=True)
    mean_gx = jnp.mean(g * xhat, axis=-1, keepdims=True)
    result[...] = (get(4)[...].astype(F32) + rstd * (g - mean_g - xhat * mean_gx)).astype(BF)


def high_low(x):
    high = lax.reduce_precision(x, 8, 7)
    low = lax.reduce_precision(x - high, 8, 7)
    return high, low


def packed(x, columns):
    high, low = high_low(x)
    both = jnp.concatenate([high, low], axis=1).astype(BF)
    return jnp.pad(both, ((0, 0), (0, columns - 256)))


def unpacked(x):
    return x[:, :128].astype(F32) + x[:, 128:256].astype(F32)


def settled(x):
    high, low = high_low(x)
    return high + low


def on_device(frames, layernorm_gain, w_qkv, w_out, segment_ids, output_gradient):
    x = frames[0]
    grad_out = output_gradient[0]
    rows, width = x.shape
    head = width // HEADS
    scale = head**-0.5
    pos = jnp.stack([lax.axis_index("seq"), lax.axis_index("dp")]).astype(jnp.int32)
    gain_row = layernorm_gain[None, :]

    (own,) = staged(layernorm_kernel, "layernorm", [shape(BF, rows, width)], [], [x], [gain_row])
    grad_twin = dp_swap(grad_out, 1)
    beside = seq_swap(own, 1)
    after, before = seq_swap(own, 2), seq_swap(own, 6)
    half = rows // 2
    far = [seq_swap(after[:half], 6), seq_swap(before[half:], 2)]
    beyond = [seq_swap(part, 1) for part in far]
    normed = {
        (0, 0): own,
        (1, 0): beside,
        (2, 0): after,
        (6, 0): before,
        (3, 0): seq_swap(beside, 2),
        (7, 0): seq_swap(beside, 6),
        (4, 0): far[0],
        (4, half): far[1],
        (5, 0): beyond[0],
        (5, half): beyond[1],
    }
    places, normed = list(normed), list(normed.values())

    dattn, w_head = staged(
        dattn_kernel,
        "dattn",
        [shape(BF, HEADS, rows, head), shape(BF, width, 384)],
        [pos],
        [grad_out, w_out],
        left=[w_qkv],
        scratch=[pltpu.SemaphoreType.DMA((3,))],
    )
    dattn, grad_twin, _ = lax.optimization_barrier((dattn, grad_twin, beyond[0]))
    dout = seq_exchange(dattn)

    parts = [mm(n, w_head, 1, 0).astype(BF) for n in normed]
    attn_head, probs, qkv = forward(pos, parts, places, segment_ids, rows, scale)
    attn = seq_exchange(attn_head.reshape(8, rows, head))
    dqkv_head = backward(qkv, dout, attn_head, probs, scale)
    dqkv = seq_exchange(dqkv_head.reshape(8, rows, 384))

    attn, dqkv_head = lax.optimization_barrier((attn, dqkv_head))
    attn_twin = dp_swap(attn, 1)
    wqkv_keep, wqkv_send, gain_part = staged(
        functools.partial(projection_kernel, places),
        "projection_gradient",
        [shape(F32, 512, 384), shape(BF, 512, 384), shape(F32, 1024, 1)],
        [pos],
        [dqkv_head, w_head] + normed,
        [layernorm_gain[:, None]],
        scratch=[pltpu.VMEM((1024, 384), F32), pltpu.VMEM((512, 384), F32)],
    )
    near, away, wout_sum, middle = staged(
        output_gradient_kernel,
        "output_gradient",
        [shape(BF, 256, 512)] * 2 + [shape(F32, 128, 1024)] * 2,
        [pos],
        [attn, grad_out, attn_twin, grad_twin],
        scratch=[pltpu.VMEM((1024, 1024), F32), pltpu.VMEM((512, 1024), F32)],
    )
    near, away, wqkv_send = lax.optimization_barrier((near, away, wqkv_send))
    layer_out, frame_grad = staged(
        result_kernel,
        "results",
        [shape(BF, rows, width)] * 2,
        [],
        [x, attn, w_out, dqkv, grad_out, w_qkv],
        [gain_row],
    )

    gain_part = gain_part.reshape(8, 128)
    got = dp_swap(jnp.concatenate([wqkv_send, packed(gain_part, 384)], axis=0), 1)
    near, away = dp_swap(near, 4), dp_swap(away, 12)
    near, away, got = lax.optimization_barrier((near, away, got))
    near_next = dp_swap((middle[:, :512] + near[128:].astype(F32)).astype(BF), 12)
    away_next = dp_swap((middle[:, 512:] + away[:128].astype(F32)).astype(BF), 4)
    wout_sum = wout_sum + jnp.concatenate(
        [
            near[:128].astype(F32) + near_next.astype(F32),
            away[128:].astype(F32) + away_next.astype(F32),
        ],
        axis=1,
    )
    wout_sum = wout_sum[:64] + dp_swap(wout_sum[64:].astype(BF), 2).astype(F32)

    wqkv_sum = wqkv_keep + got[:512].astype(F32)
    gain_sum = settled(gain_part) + unpacked(got[512:])
    wqkv_sum = wqkv_sum.reshape(4, 128, 384)
    note = packed(gain_sum, 384)
    got = [
        dp_swap(jnp.concatenate([wqkv_sum[r].astype(BF), note], axis=0), 4 * r)
        for r in range(1, 4)
    ]
    wqkv_sum = wqkv_sum[0] + sum(part[:128].astype(F32) for part in got)
    notes = [settled(gain_sum)] + [unpacked(part[128:]) for part in got]
    gain_sum = (notes[0] + notes[1]) + (notes[2] + notes[3])
    got = dp_swap(jnp.concatenate([wqkv_sum[64:].astype(BF), packed(gain_sum, 384)], axis=0), 2)
    wqkv_sum = wqkv_sum[:64] + got[:64].astype(F32)
    gain_sum = settled(gain_sum) + unpacked(got[64:])
    sums = jnp.concatenate([wqkv_sum, wout_sum], axis=1)

    note = jnp.broadcast_to(packed(gain_sum, 256)[None], (8, 8, 256))
    got = seq_exchange(jnp.concatenate([sums.reshape(8, 8, 1408).astype(BF), note], axis=2))
    grad_wqkv = got[:, :, :384].reshape(8, 8, 3, head).transpose(1, 2, 0, 3).reshape(8, 3 * width)
    grad_wout = jnp.sum(got[:, :, 384:1408].astype(F32), axis=0).astype(BF)
    totals = [unpacked(got[s, :, 1408:]) for s in range(8)]
    grad_gain = functools.reduce(lambda a, b: a + b, totals).reshape(width)
    return (
        layer_out[None],
        frame_grad[None],
        grad_wqkv,
        grad_wout,
        grad_gain,
    )


def solution(mesh):
    placed = (P("dp", "seq", None), P(), P(), P(), P("dp", None), P("dp", "seq", None))
    return jax.shard_map(
        on_device,
        mesh=mesh,
        in_specs=placed,
        out_specs=(
            P("dp", "seq", None),
            P("dp", "seq", None),
            P(("seq", "dp"), None),
            P(("seq", "dp"), None),
            P(),
        ),
        check_vma=False,
    )
```

```python
import functools

import jax
import jax.numpy as jnp
from jax import lax
from jax.experimental import pallas as pl
from jax.experimental.pallas import tpu as pltpu
from jax.sharding import PartitionSpec as P

HEADS = 8
BF = jnp.bfloat16
F32 = jnp.float32
LOG2E = 1.4426950408889634
PAIR = 4
VMEM_LIMIT = 60 * 1024 * 1024
WHOLE = pl.BlockSpec(memory_space=pltpu.VMEM)
SCALARS = pl.BlockSpec(memory_space=pltpu.SMEM)


def seq_swap(x, bits):
    return lax.ppermute(x, "seq", [(i, i ^ bits) for i in range(8)])


def dp_swap(x, bits):
    return lax.ppermute(x, "dp", [(i, i ^ bits) for i in range(16)])


def seq_exchange(x):
    return lax.all_to_all(x, "seq", 0, 0, tiled=True)


def mm(a, b, ca, cb):
    return lax.dot_general(a, b, (((ca,), (cb,)), ((), ())), preferred_element_type=F32)


def call(kernel, name, out_shape, **options):
    return pl.pallas_call(
        kernel,
        out_shape=out_shape,
        compiler_params=pltpu.CompilerParams(vmem_limit_bytes=VMEM_LIMIT),
        name=name,
        **options,
    )


def shape(dtype, *dims):
    return jax.ShapeDtypeStruct(dims, dtype)


def layernorm(x):
    center = x - jnp.mean(x, axis=-1, keepdims=True)
    rstd = lax.rsqrt(jnp.mean(center * center, axis=-1, keepdims=True) + 1e-05)
    return center * rstd, rstd


def staged(body, name, out_shape, scalars, arrays, plain=(), left=(), scratch=()):
    n, m, k = len(scalars), len(arrays), len(plain) + len(left)

    def kernel(*refs):
        sources, others = refs[n : n + m], refs[n + m : n + m + k]
        outs = refs[n + m + k : n + m + k + len(out_shape)]
        rest = refs[n + m + k + len(out_shape) :]
        buffers, semaphores, rest = rest[:m], rest[m], rest[m + 1 :]
        copies = [
            pltpu.make_async_copy(sources[i], buffers[i], semaphores.at[i]) for i in range(m)
        ]
        for copy in copies:
            copy.start()
        waited = set()

        def get(i):
            if i not in waited:
                waited.add(i)
                copies[i].wait()
            return buffers[i]

        body(*refs[:n], get, *others, *outs, *rest)
        for i in range(m):
            get(i)

    return call(
        kernel,
        name,
        tuple(out_shape),
        in_specs=[SCALARS] * n
        + [pl.BlockSpec(memory_space=pltpu.HBM)] * m
        + [WHOLE] * len(plain)
        + [pl.BlockSpec(memory_space=pltpu.HBM)] * len(left),
        out_specs=(WHOLE,) * len(out_shape),
        scratch_shapes=[pltpu.VMEM(a.shape, a.dtype) for a in arrays]
        + [pltpu.SemaphoreType.DMA((m,))]
        + list(scratch),
    )(*scalars, *arrays, *plain, *left)


def layernorm_kernel(frames, gain, normed):
    xhat, _ = layernorm(frames[...].astype(F32))
    normed[...] = (xhat * gain[...]).astype(BF)


def dattn_kernel(pos, get, w_qkv, dattn, w_head, semaphores):
    copies = []
    for t in range(3):
        start = pl.multiple_of(t * 1024 + pos[0] * 128, 128)
        copies.append(
            pltpu.make_async_copy(
                w_qkv.at[:, pl.ds(start, 128)],
                w_head.at[:, t * 128 : (t + 1) * 128],
                semaphores.at[t],
            )
        )
    for copy in copies:
        copy.start()
    full = mm(get(0)[...], get(1)[...], 1, 1).astype(BF)
    for h in range(HEADS):
        dattn[h] = full[:, h * 128 : (h + 1) * 128]
    for copy in copies:
        copy.wait()


def attention_kernel(scale, places, pos, *refs):
    count = len(places)
    parts, (dout, key_tag, query_tag) = refs[:count], refs[count : count + 3]
    attn, dqkv, q_s, k_s, v_s, kt_s, vt_s, dk_s, dv_s = refs[count + 3 :]
    rows = dout.shape[1]
    for part, (r, offset) in zip(parts, places):
        size = part.shape[0]
        rng = pl.ds(pl.multiple_of((pos[0] ^ r) * rows + offset, size), size)
        q_s[rng, :128] = part[:, :128]
        k_s[rng, :128] = part[:, 128:256]
        v_s[rng, :] = part[:, 256:]
    q_s[:, 128:] = query_tag[...]
    k_s[:, 128:] = key_tag[...]
    kt_s[...] = k_s[:, :128].T
    vt_s[...] = v_s[...].T
    dk_s[...] = jnp.zeros_like(dk_s)
    dv_s[...] = jnp.zeros_like(dv_s)

    def step(i, carry):
        for u in range(PAIR):
            block = i * PAIR + u
            rng = pl.ds(pl.multiple_of(block * rows, rows), rows)
            q, do = q_s[rng, :], dout[block]
            scores = mm(k_s[...], q, 1, 1)
            peak = jnp.max(scores, axis=0, keepdims=True)
            expo = jnp.exp2((scores - peak) * (scale * LOG2E))
            low = (expo * (1.0 / jnp.sum(expo, axis=0, keepdims=True))).astype(BF)
            out = mm(vt_s[...], low, 1, 0)
            delta = jnp.sum(out * do.astype(F32).T, axis=0, keepdims=True)
            dprobs = mm(v_s[...], do, 1, 1)
            dscores = (low.astype(F32) * (dprobs - delta)).astype(BF)
            dk_s[...] += mm(dscores, q[:, :128], 1, 0)
            dv_s[...] += mm(low, do, 1, 0)
            attn[rng, :] = out.T.astype(BF)
            dqkv[rng, :128] = (mm(kt_s[...], dscores, 1, 0) * scale).T.astype(BF)
        return carry

    lax.fori_loop(0, 8 // PAIR, step, 0)
    dqkv[:, 128:256] = (dk_s[...] * scale).astype(BF)
    dqkv[:, 256:] = dv_s[...].astype(BF)


def attention(pos, parts, places, dout, key_tag, query_tag, scale):
    total = key_tag.shape[0]
    return call(
        functools.partial(attention_kernel, scale, places),
        "attention",
        (shape(BF, total, 128), shape(BF, total, 384)),
        in_specs=[SCALARS] + [WHOLE] * (len(parts) + 3),
        out_specs=(WHOLE, WHOLE),
        scratch_shapes=[
            pltpu.VMEM((total, 256), BF),
            pltpu.VMEM((total, 256), BF),
            pltpu.VMEM((total, 128), BF),
            pltpu.VMEM((128, total), BF),
            pltpu.VMEM((128, total), BF),
            pltpu.VMEM((total, 128), F32),
            pltpu.VMEM((total, 128), F32),
        ],
    )(pos, *parts, dout, key_tag, query_tag)


def chosen_rows(dp, source, half, target):
    for r in range(8):
        for s in range(8):
            rows = pl.ds(pl.multiple_of(s * 128 + (dp ^ (2 * r + half)) * 8, 8), 8)
            target[r * 64 + s * 8 : r * 64 + s * 8 + 8, :] = source[rows, :]


def projection_kernel(places, pos, get, gain, keep, send, gain_part, grad, other):
    dqkv, weights = get(0), get(1)
    rows = dqkv.shape[0] // 8
    total = None
    for i, (r, offset) in enumerate(places):
        normed = get(2 + i)
        size = normed.shape[0]
        rng = pl.ds(pl.multiple_of((pos[0] ^ r) * rows + offset, size), size)
        term = mm(dqkv[rng, :], normed[...], 0, 0)
        total = term if total is None else total + term
    grad[...] = total.T
    gain_part[...] = (
        jnp.sum(grad[...] * weights[...].astype(F32), axis=1, keepdims=True) / gain[...]
    )
    chosen_rows(pos[1], grad, 0, keep)
    chosen_rows(pos[1], grad, 1, other)
    send[...] = other[...].astype(BF)


def output_gradient_kernel(pos, get, send_near, send_far, keep, middle, grad, chosen):
    for h in range(HEADS):
        rows = slice(h * 128, (h + 1) * 128)
        grad[rows, :] = mm(get(0)[h], get(1)[...], 0, 0) + mm(get(2)[h], get(3)[...], 0, 0)
    chosen_rows(pos[1], grad, 0, chosen)
    qkv = get(4)[...] + get(5)[:512, :].astype(F32)
    left, right = slice(0, 640), slice(640, 1408)
    first, second = qkv[:, :128], qkv[:, 128:]
    send_near[:, :128] = first[128:384].astype(BF)
    send_near[:, 128:] = chosen[128:384, :512].astype(BF)
    send_far[:, :256] = second[256:].astype(BF)
    send_far[:, 256:] = chosen[256:, 512:].astype(BF)
    for target, near_rows, far_rows in (
        (keep, slice(0, 128), slice(0, 128)),
        (middle, slice(384, 512), slice(128, 256)),
    ):
        target[:, left] = jnp.concatenate([first[near_rows], chosen[near_rows, :512]], axis=1)
        target[:, right] = jnp.concatenate([second[far_rows], chosen[far_rows, 512:]], axis=1)


def result_kernel(get, gain, layer_out, result):
    x = get(0)[...].astype(F32)
    width = x.shape[1]
    out = x
    for h in range(HEADS):
        out = out + mm(get(1)[h], get(2)[h * 128 : (h + 1) * 128, :], 1, 0)
    layer_out[...] = out.astype(BF)
    total = None
    for h in range(HEADS):
        cols = [slice(t * width + h * 128, t * width + (h + 1) * 128) for t in range(3)]
        weights = jnp.concatenate([get(5)[:, c] for c in cols], axis=1)
        term = mm(weights, get(3)[h], 1, 1)
        total = term if total is None else total + term
    xhat, rstd = layernorm(x)
    g = total.T * gain[...]
    mean_g = jnp.mean(g, axis=-1, keepdims=True)
    mean_gx = jnp.mean(g * xhat, axis=-1, keepdims=True)
    result[...] = (get(4)[...].astype(F32) + rstd * (g - mean_g - xhat * mean_gx)).astype(BF)


def high_low(x):
    high = lax.reduce_precision(x, 8, 7)
    low = lax.reduce_precision(x - high, 8, 7)
    return high, low


def packed(x, columns):
    high, low = high_low(x)
    both = jnp.concatenate([high, low], axis=1).astype(BF)
    return jnp.pad(both, ((0, 0), (0, columns - 256)))


def unpacked(x):
    return x[:, :128].astype(F32) + x[:, 128:256].astype(F32)


def settled(x):
    high, low = high_low(x)
    return high + low


def on_device(frames, layernorm_gain, w_qkv, w_out, segment_ids, output_gradient):
    x = frames[0]
    grad_out = output_gradient[0]
    rows, width = x.shape
    head = width // HEADS
    scale = head**-0.5
    pos = jnp.stack([lax.axis_index("seq"), lax.axis_index("dp")]).astype(jnp.int32)
    gain_row = layernorm_gain[None, :]

    own = call(
        layernorm_kernel, "layernorm", shape(BF, rows, width), in_specs=[WHOLE] * 2, out_specs=WHOLE
    )(x, gain_row)
    grad_twin = dp_swap(grad_out, 1)
    beside = seq_swap(own, 1)
    after, before = seq_swap(own, 2), seq_swap(own, 6)
    half = rows // 2
    far = [seq_swap(after[:half], 6), seq_swap(before[half:], 2)]
    beyond = [seq_swap(part, 1) for part in far]
    normed = {
        (0, 0): own,
        (1, 0): beside,
        (2, 0): after,
        (6, 0): before,
        (3, 0): seq_swap(beside, 2),
        (7, 0): seq_swap(beside, 6),
        (4, 0): far[0],
        (4, half): far[1],
        (5, 0): beyond[0],
        (5, half): beyond[1],
    }
    places, normed = list(normed), list(normed.values())

    dattn, w_head = staged(
        dattn_kernel,
        "dattn",
        [shape(BF, HEADS, rows, head), shape(BF, width, 384)],
        [pos],
        [grad_out, w_out],
        left=[w_qkv],
        scratch=[pltpu.SemaphoreType.DMA((3,))],
    )
    dattn, grad_twin, _ = lax.optimization_barrier((dattn, grad_twin, far))
    dout = seq_exchange(dattn)

    parts = [mm(n, w_head, 1, 0).astype(BF) for n in normed]
    same = segment_ids[0][:, None] == jnp.arange(128)[None, :]
    key_tag = same.astype(BF)
    query_tag = jnp.where(same, 0.0, -1e30).astype(BF)
    attn_head, dqkv_head = attention(pos, parts, places, dout, key_tag, query_tag, scale)
    attn = seq_exchange(attn_head.reshape(8, rows, head))
    dqkv = seq_exchange(dqkv_head.reshape(8, rows, 384))
    wqkv_keep, wqkv_send, gain_part = staged(
        functools.partial(projection_kernel, places),
        "projection_gradient",
        [shape(F32, 512, 384), shape(BF, 512, 384), shape(F32, 1024, 1)],
        [pos],
        [dqkv_head, w_head] + normed,
        [layernorm_gain[:, None]],
        scratch=[pltpu.VMEM((1024, 384), F32), pltpu.VMEM((512, 384), F32)],
    )
    attn, wqkv_send, gain_part = lax.optimization_barrier((attn, wqkv_send, gain_part))
    attn_twin = dp_swap(attn, 1)
    gain_part = gain_part.reshape(8, 128)
    got = dp_swap(jnp.concatenate([wqkv_send, packed(gain_part, 384)], axis=0), 1)
    near, away, keep, middle = staged(
        output_gradient_kernel,
        "output_gradient",
        [shape(BF, 256, 640), shape(BF, 256, 768)] + [shape(F32, 128, 1408)] * 2,
        [pos],
        [attn, grad_out, attn_twin, grad_twin, wqkv_keep, got],
        scratch=[pltpu.VMEM((1024, 1024), F32), pltpu.VMEM((512, 1024), F32)],
    )
    gain_sum = settled(gain_part) + unpacked(got[512:])
    near = dp_swap(jnp.concatenate([near, packed(gain_sum, 640)], axis=0), 4)
    away = dp_swap(away, 12)
    gain_sum = settled(gain_sum) + unpacked(near[256:])
    near_next = (middle[:, :640] + near[128:256].astype(F32)).astype(BF)
    near_next = dp_swap(jnp.concatenate([near_next, packed(gain_sum, 640)], axis=0), 12)
    away_next = dp_swap((middle[:, 640:] + away[:128].astype(F32)).astype(BF), 4)
    gain_sum = settled(gain_sum) + unpacked(near_next[128:])
    sums = keep + jnp.concatenate(
        [
            near[:128].astype(F32) + near_next[:128].astype(F32),
            away[128:].astype(F32) + away_next.astype(F32),
        ],
        axis=1,
    )
    got = dp_swap(jnp.concatenate([sums[64:].astype(BF), packed(gain_sum, 1408)], axis=0), 2)
    gain_sum = settled(gain_sum) + unpacked(got[64:])
    sums = sums[:64] + got[:64].astype(F32)
    sums = jnp.concatenate(
        [sums[:, :128], sums[:, 640:896], sums[:, 128:640], sums[:, 896:]], axis=1
    )
    sums, dqkv = lax.optimization_barrier((sums, dqkv))
    layer_out, frame_grad = staged(
        result_kernel,
        "results",
        [shape(BF, rows, width)] * 2,
        [],
        [x, attn, w_out, dqkv, grad_out, w_qkv],
        [gain_row],
    )

    note = jnp.broadcast_to(packed(gain_sum, 256)[None], (8, 8, 256))
    got = seq_exchange(jnp.concatenate([sums.reshape(8, 8, 1408).astype(BF), note], axis=2))
    grad_wqkv = got[:, :, :384].reshape(8, 8, 3, head).transpose(1, 2, 0, 3).reshape(8, 3 * width)
    grad_wout = jnp.sum(got[:, :, 384:1408].astype(F32), axis=0).astype(BF)
    totals = [unpacked(got[s, :, 1408:]) for s in range(8)]
    grad_gain = functools.reduce(lambda a, b: a + b, totals).reshape(width)
    return (
        layer_out[None],
        frame_grad[None],
        grad_wqkv,
        grad_wout,
        grad_gain,
    )


def solution(mesh):
    placed = (P("dp", "seq", None), P(), P(), P(), P("dp", None), P("dp", "seq", None))
    return jax.shard_map(
        on_device,
        mesh=mesh,
        in_specs=placed,
        out_specs=(
            P("dp", "seq", None),
            P("dp", "seq", None),
            P(("seq", "dp"), None),
            P(("seq", "dp"), None),
            P(),
        ),
        check_vma=False,
    )
```

```python
import functools

import jax
import jax.numpy as jnp
from jax import lax
from jax.experimental import pallas as pl
from jax.experimental.pallas import tpu as pltpu
from jax.sharding import PartitionSpec as P

HEADS = 8
BF = jnp.bfloat16
F32 = jnp.float32
LOG2E = 1.4426950408889634
PAIR = 4
VMEM_LIMIT = 60 * 1024 * 1024
WHOLE = pl.BlockSpec(memory_space=pltpu.VMEM)
SCALARS = pl.BlockSpec(memory_space=pltpu.SMEM)


def seq_swap(x, bits):
    return lax.ppermute(x, "seq", [(i, i ^ bits) for i in range(8)])


def dp_swap(x, bits):
    return lax.ppermute(x, "dp", [(i, i ^ bits) for i in range(16)])


def seq_exchange(x):
    return lax.all_to_all(x, "seq", 0, 0, tiled=True)


def mm(a, b, ca, cb):
    return lax.dot_general(a, b, (((ca,), (cb,)), ((), ())), preferred_element_type=F32)


def call(kernel, name, out_shape, **options):
    return pl.pallas_call(
        kernel,
        out_shape=out_shape,
        compiler_params=pltpu.CompilerParams(vmem_limit_bytes=VMEM_LIMIT),
        name=name,
        **options,
    )


def shape(dtype, *dims):
    return jax.ShapeDtypeStruct(dims, dtype)


def layernorm(x):
    center = x - jnp.mean(x, axis=-1, keepdims=True)
    rstd = lax.rsqrt(jnp.mean(center * center, axis=-1, keepdims=True) + 1e-05)
    return center * rstd, rstd


def staged(body, name, out_shape, scalars, arrays, plain=(), left=(), scratch=()):
    n, m, k = len(scalars), len(arrays), len(plain) + len(left)

    def kernel(*refs):
        sources, others = refs[n : n + m], refs[n + m : n + m + k]
        outs = refs[n + m + k : n + m + k + len(out_shape)]
        rest = refs[n + m + k + len(out_shape) :]
        buffers, semaphores, rest = rest[:m], rest[m], rest[m + 1 :]
        copies = [
            pltpu.make_async_copy(sources[i], buffers[i], semaphores.at[i]) for i in range(m)
        ]
        for copy in copies:
            copy.start()
        waited = set()

        def get(i):
            if i not in waited:
                waited.add(i)
                copies[i].wait()
            return buffers[i]

        body(*refs[:n], get, *others, *outs, *rest)
        for i in range(m):
            get(i)

    return call(
        kernel,
        name,
        tuple(out_shape),
        in_specs=[SCALARS] * n
        + [pl.BlockSpec(memory_space=pltpu.HBM)] * m
        + [WHOLE] * len(plain)
        + [pl.BlockSpec(memory_space=pltpu.HBM)] * len(left),
        out_specs=(WHOLE,) * len(out_shape),
        scratch_shapes=[pltpu.VMEM(a.shape, a.dtype) for a in arrays]
        + [pltpu.SemaphoreType.DMA((m,))]
        + list(scratch),
    )(*scalars, *arrays, *plain, *left)


def layernorm_kernel(frames, gain, normed):
    xhat, _ = layernorm(frames[...].astype(F32))
    normed[...] = (xhat * gain[...]).astype(BF)


def dattn_kernel(pos, get, w_qkv, dattn, w_head, semaphores):
    copies = []
    for t in range(3):
        start = pl.multiple_of(t * 1024 + pos[0] * 128, 128)
        copies.append(
            pltpu.make_async_copy(
                w_qkv.at[:, pl.ds(start, 128)],
                w_head.at[:, t * 128 : (t + 1) * 128],
                semaphores.at[t],
            )
        )
    for copy in copies:
        copy.start()
    full = mm(get(0)[...], get(1)[...], 1, 1).astype(BF)
    for h in range(HEADS):
        dattn[h] = full[:, h * 128 : (h + 1) * 128]
    for copy in copies:
        copy.wait()


def attention_kernel(scale, places, pos, *refs):
    count = len(places)
    parts, (dout, ids) = refs[:count], refs[count : count + 2]
    attn, dqkv, q_s, k_s, v_s, kt_s, vt_s, dk_s, dv_s = refs[count + 2 :]
    rows = dout.shape[1]
    for part, (r, offset) in zip(parts, places):
        size = part.shape[0]
        rng = pl.ds(pl.multiple_of((pos[0] ^ r) * rows + offset, size), size)
        q_s[rng, :128] = part[:, :128]
        k_s[rng, :128] = part[:, 128:256]
        v_s[rng, :] = part[:, 256:]
    names = lax.broadcasted_iota(jnp.int32, (128, 8 * rows), 0)
    same = jnp.where(ids[...] == names, 1.0, 0.0).T
    q_s[:, 128:] = ((same - 1.0) * 1e30).astype(BF)
    k_s[:, 128:] = same.astype(BF)
    kt_s[...] = k_s[:, :128].T
    vt_s[...] = v_s[...].T
    dk_s[...] = jnp.zeros_like(dk_s)
    dv_s[...] = jnp.zeros_like(dv_s)

    def step(i, carry):
        for u in range(PAIR):
            block = i * PAIR + u
            rng = pl.ds(pl.multiple_of(block * rows, rows), rows)
            q, do = q_s[rng, :], dout[block]
            scores = mm(k_s[...], q, 1, 1)
            peak = jnp.max(scores, axis=0, keepdims=True)
            expo = jnp.exp2((scores - peak) * (scale * LOG2E))
            low = (expo * (1.0 / jnp.sum(expo, axis=0, keepdims=True))).astype(BF)
            out = mm(vt_s[...], low, 1, 0)
            delta = jnp.sum(out * do.astype(F32).T, axis=0, keepdims=True)
            dprobs = mm(v_s[...], do, 1, 1)
            dscores = (low.astype(F32) * (dprobs - delta)).astype(BF)
            dk_s[...] += mm(dscores, q[:, :128], 1, 0)
            dv_s[...] += mm(low, do, 1, 0)
            attn[rng, :] = out.T.astype(BF)
            dqkv[rng, :128] = (mm(kt_s[...], dscores, 1, 0) * scale).T.astype(BF)
        return carry

    lax.fori_loop(0, 8 // PAIR, step, 0)
    dqkv[:, 128:256] = (dk_s[...] * scale).astype(BF)
    dqkv[:, 256:] = dv_s[...].astype(BF)


def attention(pos, parts, places, dout, ids, scale):
    total = ids.shape[1]
    return call(
        functools.partial(attention_kernel, scale, places),
        "attention",
        (shape(BF, total, 128), shape(BF, total, 384)),
        in_specs=[SCALARS] + [WHOLE] * (len(parts) + 2),
        out_specs=(WHOLE, WHOLE),
        scratch_shapes=[
            pltpu.VMEM((total, 256), BF),
            pltpu.VMEM((total, 256), BF),
            pltpu.VMEM((total, 128), BF),
            pltpu.VMEM((128, total), BF),
            pltpu.VMEM((128, total), BF),
            pltpu.VMEM((total, 128), F32),
            pltpu.VMEM((total, 128), F32),
        ],
    )(pos, *parts, dout, ids)


def chosen_rows(dp, source, half, target):
    for r in range(8):
        for s in range(8):
            rows = pl.ds(pl.multiple_of(s * 128 + (dp ^ (2 * r + half)) * 8, 8), 8)
            target[r * 64 + s * 8 : r * 64 + s * 8 + 8, :] = source[rows, :]


def projection_kernel(places, pos, get, gain, keep, send, own_gain, grad, other, sums):
    dqkv, weights = get(0), get(1)
    rows = dqkv.shape[0] // 8
    total = None
    for i, (r, offset) in enumerate(places):
        normed = get(2 + i)
        size = normed.shape[0]
        rng = pl.ds(pl.multiple_of((pos[0] ^ r) * rows + offset, size), size)
        term = mm(dqkv[rng, :], normed[...], 0, 0)
        total = term if total is None else total + term
    grad[...] = total.T
    weighted = jnp.sum(total * weights[...].T.astype(F32), axis=0, keepdims=True) / gain[...]
    sums[...] = jnp.zeros_like(sums)
    for j in range(8):
        sums[j : j + 1, :] = weighted[:, j * 128 : (j + 1) * 128]
    high = sums[...].astype(BF)
    low = (sums[...] - high.astype(F32)).astype(BF)
    own_gain[...] = (high.astype(F32) + low.astype(F32))[:8, :]
    chosen_rows(pos[1], grad, 0, keep)
    chosen_rows(pos[1], grad, 1, other)
    send[:512, :] = other[...].astype(BF)
    send[512:, :128] = high
    send[512:, 128:256] = low
    send[512:, 256:] = jnp.zeros_like(low)


def output_gradient_kernel(pos, get, send_near, send_far, keep, middle, grad, chosen):
    for h in range(HEADS):
        rows = slice(h * 128, (h + 1) * 128)
        grad[rows, :] = mm(get(0)[h], get(1)[...], 0, 0) + mm(get(2)[h], get(3)[...], 0, 0)
    chosen_rows(pos[1], grad, 0, chosen)
    qkv = get(4)[...] + get(5)[:512, :].astype(F32)
    left, right = slice(0, 640), slice(640, 1408)
    first, second = qkv[:, :128], qkv[:, 128:]
    send_near[:, :128] = first[128:384].astype(BF)
    send_near[:, 128:] = chosen[128:384, :512].astype(BF)
    send_far[:, :256] = second[256:].astype(BF)
    send_far[:, 256:] = chosen[256:, 512:].astype(BF)
    for target, near_rows, far_rows in (
        (keep, slice(0, 128), slice(0, 128)),
        (middle, slice(384, 512), slice(128, 256)),
    ):
        target[:, left] = jnp.concatenate([first[near_rows], chosen[near_rows, :512]], axis=1)
        target[:, right] = jnp.concatenate([second[far_rows], chosen[far_rows, 512:]], axis=1)


def layer_out_kernel(get, layer_out):
    out = get(0)[...].astype(F32)
    for h in range(HEADS):
        out = out + mm(get(1)[h], get(2)[h * 128 : (h + 1) * 128, :], 1, 0)
    layer_out[...] = out.astype(BF)


def frame_gradient_kernel(get, gain, result):
    width = get(0).shape[1]
    total = None
    for h in range(HEADS):
        cols = [slice(t * width + h * 128, t * width + (h + 1) * 128) for t in range(3)]
        weights = jnp.concatenate([get(3)[:, c] for c in cols], axis=1)
        term = mm(weights, get(1)[h], 1, 1)
        total = term if total is None else total + term
    xhat, rstd = layernorm(get(0)[...].astype(F32))
    g = total.T * gain[...]
    mean_g = jnp.mean(g, axis=-1, keepdims=True)
    mean_gx = jnp.mean(g * xhat, axis=-1, keepdims=True)
    result[...] = (get(2)[...].astype(F32) + rstd * (g - mean_g - xhat * mean_gx)).astype(BF)


def high_low(x):
    high = lax.reduce_precision(x, 8, 7)
    low = lax.reduce_precision(x - high, 8, 7)
    return high, low


def packed(x, columns):
    high, low = high_low(x)
    both = jnp.concatenate([high, low], axis=1).astype(BF)
    return jnp.pad(both, ((0, 0), (0, columns - 256)))


def unpacked(x):
    return x[:, :128].astype(F32) + x[:, 128:256].astype(F32)


def settled(x):
    high, low = high_low(x)
    return high + low


def on_device(frames, layernorm_gain, w_qkv, w_out, segment_ids, output_gradient):
    x = frames[0]
    grad_out = output_gradient[0]
    rows, width = x.shape
    head = width // HEADS
    scale = head**-0.5
    pos = jnp.stack([lax.axis_index("seq"), lax.axis_index("dp")]).astype(jnp.int32)
    gain_row = layernorm_gain[None, :]

    own = call(
        layernorm_kernel, "layernorm", shape(BF, rows, width), in_specs=[WHOLE] * 2, out_specs=WHOLE
    )(x, gain_row)
    grad_twin = dp_swap(grad_out, 1)
    beside = seq_swap(own, 1)
    after, before = seq_swap(own, 2), seq_swap(own, 6)
    half = rows // 2
    far = [seq_swap(after[:half], 6), seq_swap(before[half:], 2)]
    beyond = [seq_swap(part, 1) for part in far]
    normed = {
        (0, 0): own,
        (1, 0): beside,
        (2, 0): after,
        (6, 0): before,
        (3, 0): seq_swap(beside, 2),
        (7, 0): seq_swap(beside, 6),
        (4, 0): far[0],
        (4, half): far[1],
        (5, 0): beyond[0],
        (5, half): beyond[1],
    }
    places, normed = list(normed), list(normed.values())

    dattn, w_head = staged(
        dattn_kernel,
        "dattn",
        [shape(BF, HEADS, rows, head), shape(BF, width, 384)],
        [pos],
        [grad_out, w_out],
        left=[w_qkv],
        scratch=[pltpu.SemaphoreType.DMA((3,))],
    )
    dattn, grad_twin, _ = lax.optimization_barrier((dattn, grad_twin, beyond[0]))
    dout = seq_exchange(dattn)

    parts = [mm(n, w_head, 1, 0).astype(BF) for n in normed]
    attn_head, dqkv_head = attention(pos, parts, places, dout, segment_ids, scale)
    attn = seq_exchange(attn_head.reshape(8, rows, head))
    dqkv = seq_exchange(dqkv_head.reshape(8, rows, 384))
    wqkv_keep, wqkv_send, gain_part = staged(
        functools.partial(projection_kernel, places),
        "projection_gradient",
        [shape(F32, 512, 384), shape(BF, 528, 384), shape(F32, 8, 128)],
        [pos],
        [dqkv_head, w_head] + normed,
        [gain_row],
        scratch=[
            pltpu.VMEM((1024, 384), F32),
            pltpu.VMEM((512, 384), F32),
            pltpu.VMEM((16, 128), F32),
        ],
    )
    attn, wqkv_send, gain_part = lax.optimization_barrier((attn, wqkv_send, gain_part))
    attn_twin = dp_swap(attn, 1)
    got = dp_swap(wqkv_send, 1)
    near, away, keep, middle = staged(
        output_gradient_kernel,
        "output_gradient",
        [shape(BF, 256, 640), shape(BF, 256, 768)] + [shape(F32, 128, 1408)] * 2,
        [pos],
        [attn, grad_out, attn_twin, grad_twin, wqkv_keep, got],
        scratch=[pltpu.VMEM((1024, 1024), F32), pltpu.VMEM((512, 1024), F32)],
    )
    gain_sum = gain_part + unpacked(got[512:520])
    near = dp_swap(jnp.concatenate([near, packed(gain_sum, 640)], axis=0), 4)
    away = dp_swap(away, 12)
    (layer_out,) = staged(
        layer_out_kernel, "layer_out", [shape(BF, rows, width)], [], [x, attn, w_out]
    )
    near, away, layer_out = lax.optimization_barrier((near, away, layer_out))
    gain_sum = settled(gain_sum) + unpacked(near[256:])
    near_next = (middle[:, :640] + near[128:256].astype(F32)).astype(BF)
    near_next = dp_swap(jnp.concatenate([near_next, packed(gain_sum, 640)], axis=0), 12)
    away_next = dp_swap((middle[:, 640:] + away[:128].astype(F32)).astype(BF), 4)
    gain_sum = settled(gain_sum) + unpacked(near_next[128:])
    sums = keep + jnp.concatenate(
        [
            near[:128].astype(F32) + near_next[:128].astype(F32),
            away[128:].astype(F32) + away_next.astype(F32),
        ],
        axis=1,
    )
    got = dp_swap(jnp.concatenate([sums[64:].astype(BF), packed(gain_sum, 1408)], axis=0), 2)
    gain_sum = settled(gain_sum) + unpacked(got[64:])
    sums = sums[:64] + got[:64].astype(F32)
    sums = jnp.concatenate(
        [sums[:, :128], sums[:, 640:896], sums[:, 128:640], sums[:, 896:]], axis=1
    )
    sums, dqkv = lax.optimization_barrier((sums, dqkv))
    (frame_grad,) = staged(
        frame_gradient_kernel,
        "frame_gradient",
        [shape(BF, rows, width)],
        [],
        [x, dqkv, grad_out, w_qkv],
        [gain_row],
    )

    note = jnp.broadcast_to(packed(gain_sum, 256)[None], (8, 8, 256))
    got = seq_exchange(jnp.concatenate([sums.reshape(8, 8, 1408).astype(BF), note], axis=2))
    grad_wqkv = got[:, :, :384].reshape(8, 8, 3, head).transpose(1, 2, 0, 3).reshape(8, 3 * width)
    grad_wout = jnp.sum(got[:, :, 384:1408].astype(F32), axis=0).astype(BF)
    totals = [unpacked(got[s, :, 1408:]) for s in range(8)]
    grad_gain = functools.reduce(lambda a, b: a + b, totals).reshape(width)
    return (
        layer_out[None],
        frame_grad[None],
        grad_wqkv,
        grad_wout,
        grad_gain,
    )


def solution(mesh):
    placed = (P("dp", "seq", None), P(), P(), P(), P("dp", None), P("dp", "seq", None))
    return jax.shard_map(
        on_device,
        mesh=mesh,
        in_specs=placed,
        out_specs=(
            P("dp", "seq", None),
            P("dp", "seq", None),
            P(("seq", "dp"), None),
            P(("seq", "dp"), None),
            P(),
        ),
        check_vma=False,
    )
```

```python
import functools

import jax
import jax.numpy as jnp
from jax import lax
from jax.experimental import pallas as pl
from jax.experimental.pallas import tpu as pltpu
from jax.sharding import PartitionSpec as P

HEADS = 8
BF = jnp.bfloat16
F32 = jnp.float32
LOG2E = 1.4426950408889634
PAIR = 4
VMEM_LIMIT = 60 * 1024 * 1024
WHOLE = pl.BlockSpec(memory_space=pltpu.VMEM)
SCALARS = pl.BlockSpec(memory_space=pltpu.SMEM)


def seq_swap(x, bits):
    return lax.ppermute(x, "seq", [(i, i ^ bits) for i in range(8)])


def dp_swap(x, bits):
    return lax.ppermute(x, "dp", [(i, i ^ bits) for i in range(16)])


def seq_exchange(x):
    return lax.all_to_all(x, "seq", 0, 0, tiled=True)


def mm(a, b, ca, cb):
    return lax.dot_general(a, b, (((ca,), (cb,)), ((), ())), preferred_element_type=F32)


def call(kernel, name, out_shape, **options):
    return pl.pallas_call(
        kernel,
        out_shape=out_shape,
        compiler_params=pltpu.CompilerParams(vmem_limit_bytes=VMEM_LIMIT),
        name=name,
        **options,
    )


def shape(dtype, *dims):
    return jax.ShapeDtypeStruct(dims, dtype)


def layernorm(x):
    center = x - jnp.mean(x, axis=-1, keepdims=True)
    rstd = lax.rsqrt(jnp.mean(center * center, axis=-1, keepdims=True) + 1e-05)
    return center * rstd, rstd


def staged(body, name, out_shape, scalars, arrays, plain=(), left=(), scratch=()):
    n, m, k = len(scalars), len(arrays), len(plain) + len(left)

    def kernel(*refs):
        sources, others = refs[n : n + m], refs[n + m : n + m + k]
        outs = refs[n + m + k : n + m + k + len(out_shape)]
        rest = refs[n + m + k + len(out_shape) :]
        buffers, semaphores, rest = rest[:m], rest[m], rest[m + 1 :]
        copies = [
            pltpu.make_async_copy(sources[i], buffers[i], semaphores.at[i]) for i in range(m)
        ]
        for copy in copies:
            copy.start()
        waited = set()

        def get(i):
            if i not in waited:
                waited.add(i)
                copies[i].wait()
            return buffers[i]

        body(*refs[:n], get, *others, *outs, *rest)
        for i in range(m):
            get(i)

    return call(
        kernel,
        name,
        tuple(out_shape),
        in_specs=[SCALARS] * n
        + [pl.BlockSpec(memory_space=pltpu.HBM)] * m
        + [WHOLE] * len(plain)
        + [pl.BlockSpec(memory_space=pltpu.HBM)] * len(left),
        out_specs=(WHOLE,) * len(out_shape),
        scratch_shapes=[pltpu.VMEM(a.shape, a.dtype) for a in arrays]
        + [pltpu.SemaphoreType.DMA((m,))]
        + list(scratch),
    )(*scalars, *arrays, *plain, *left)


def layernorm_kernel(frames, gain, normed):
    xhat, _ = layernorm(frames[...].astype(F32))
    normed[...] = (xhat * gain[...]).astype(BF)


def dattn_kernel(pos, get, w_qkv, dattn, w_head, semaphores):
    copies = []
    for t in range(3):
        start = pl.multiple_of(t * 1024 + pos[0] * 128, 128)
        copies.append(
            pltpu.make_async_copy(
                w_qkv.at[:, pl.ds(start, 128)],
                w_head.at[:, t * 128 : (t + 1) * 128],
                semaphores.at[t],
            )
        )
    for copy in copies:
        copy.start()
    full = mm(get(0)[...], get(1)[...], 1, 1).astype(BF)
    for h in range(HEADS):
        dattn[h] = full[:, h * 128 : (h + 1) * 128]
    for copy in copies:
        copy.wait()


def attention_kernel(scale, places, pos, *refs):
    count = len(places)
    parts, (dout, ids) = refs[:count], refs[count : count + 2]
    attn, dqkv, q_s, k_s, v_s, kt_s, vt_s, dk_s, dv_s = refs[count + 2 :]
    rows = dout.shape[1]
    for part, (r, offset) in zip(parts, places):
        size = part.shape[0]
        rng = pl.ds(pl.multiple_of((pos[0] ^ r) * rows + offset, size), size)
        q_s[rng, :128] = part[:, :128]
        k_s[rng, :128] = part[:, 128:256]
        v_s[rng, :] = part[:, 256:]
    names = lax.broadcasted_iota(jnp.int32, (128, 8 * rows), 0)
    same = jnp.where(ids[...] == names, 1.0, 0.0).T
    q_s[:, 128:] = ((same - 1.0) * 1e30).astype(BF)
    k_s[:, 128:] = same.astype(BF)
    kt_s[...] = k_s[:, :128].T
    vt_s[...] = v_s[...].T
    dk_s[...] = jnp.zeros_like(dk_s)
    dv_s[...] = jnp.zeros_like(dv_s)

    def step(i, carry):
        for u in range(PAIR):
            block = i * PAIR + u
            rng = pl.ds(pl.multiple_of(block * rows, rows), rows)
            q, do = q_s[rng, :], dout[block]
            scores = mm(k_s[...], q, 1, 1)
            peak = jnp.max(scores, axis=0, keepdims=True)
            expo = jnp.exp2((scores - peak) * (scale * LOG2E))
            low = (expo * (1.0 / jnp.sum(expo, axis=0, keepdims=True))).astype(BF)
            out = mm(vt_s[...], low, 1, 0)
            delta = jnp.sum(out * do.astype(F32).T, axis=0, keepdims=True)
            dprobs = mm(v_s[...], do, 1, 1)
            dscores = (low.astype(F32) * (dprobs - delta)).astype(BF)
            dk_s[...] += mm(dscores, q[:, :128], 1, 0)
            dv_s[...] += mm(low, do, 1, 0)
            attn[rng, :] = out.T.astype(BF)
            dqkv[rng, :128] = (mm(kt_s[...], dscores, 1, 0) * scale).T.astype(BF)
        return carry

    lax.fori_loop(0, 8 // PAIR, step, 0)
    dqkv[:, 128:256] = (dk_s[...] * scale).astype(BF)
    dqkv[:, 256:] = dv_s[...].astype(BF)


def attention(pos, parts, places, dout, ids, scale):
    total = ids.shape[1]
    return call(
        functools.partial(attention_kernel, scale, places),
        "attention",
        (shape(BF, total, 128), shape(BF, total, 384)),
        in_specs=[SCALARS] + [WHOLE] * (len(parts) + 2),
        out_specs=(WHOLE, WHOLE),
        scratch_shapes=[
            pltpu.VMEM((total, 256), BF),
            pltpu.VMEM((total, 256), BF),
            pltpu.VMEM((total, 128), BF),
            pltpu.VMEM((128, total), BF),
            pltpu.VMEM((128, total), BF),
            pltpu.VMEM((total, 128), F32),
            pltpu.VMEM((total, 128), F32),
        ],
    )(pos, *parts, dout, ids)


def chosen_rows(dp, source, half, target):
    for r in range(8):
        for s in range(8):
            rows = pl.ds(pl.multiple_of(s * 128 + (dp ^ (2 * r + half)) * 8, 8), 8)
            target[r * 64 + s * 8 : r * 64 + s * 8 + 8, :] = source[rows, :]


def projection_kernel(places, pos, get, gain, keep, send, own_gain, grad, other, sums):
    dqkv, weights = get(0), get(1)
    rows = dqkv.shape[0] // 8
    total = None
    for i, (r, offset) in enumerate(places):
        normed = get(2 + i)
        size = normed.shape[0]
        rng = pl.ds(pl.multiple_of((pos[0] ^ r) * rows + offset, size), size)
        term = mm(dqkv[rng, :], normed[...], 0, 0)
        total = term if total is None else total + term
    grad[...] = total.T
    weighted = jnp.sum(total * weights[...].T.astype(F32), axis=0, keepdims=True) / gain[...]
    sums[...] = jnp.zeros_like(sums)
    for j in range(8):
        sums[j : j + 1, :] = weighted[:, j * 128 : (j + 1) * 128]
    high = sums[...].astype(BF)
    low = (sums[...] - high.astype(F32)).astype(BF)
    own_gain[...] = (high.astype(F32) + low.astype(F32))[:8, :]
    chosen_rows(pos[1], grad, 0, keep)
    chosen_rows(pos[1], grad, 1, other)
    send[:512, :] = other[...].astype(BF)
    send[512:, :128] = high
    send[512:, 128:256] = low
    send[512:, 256:] = jnp.zeros_like(low)


def side_by_side(source, target):
    for h in range(HEADS):
        target[:, h * 128 : (h + 1) * 128] = source[h]


def output_gradient_kernel(
    pos, get, own_gain, send_near, send_far, keep, middle, gain_sum, grad, chosen, flat, twin, sums
):
    side_by_side(get(0), flat)
    own = mm(flat[...], get(1)[...], 0, 0)
    side_by_side(get(2), twin)
    grad[...] = own + mm(twin[...], get(3)[...], 0, 0)
    chosen_rows(pos[1], grad, 0, chosen)
    arrived = get(5)[...].astype(F32)
    qkv = get(4)[...] + arrived[:512, :]
    left, right = slice(0, 640), slice(640, 1408)
    first, second = qkv[:, :128], qkv[:, 128:]
    send_near[:256, :128] = first[128:384].astype(BF)
    send_near[:256, 128:] = chosen[128:384, :512].astype(BF)
    send_far[:, :256] = second[256:].astype(BF)
    send_far[:, 256:] = chosen[256:, 512:].astype(BF)
    for target, near_rows, far_rows in (
        (keep, slice(0, 128), slice(0, 128)),
        (middle, slice(384, 512), slice(128, 256)),
    ):
        target[:, left] = jnp.concatenate([first[near_rows], chosen[near_rows, :512]], axis=1)
        target[:, right] = jnp.concatenate([second[far_rows], chosen[far_rows, 512:]], axis=1)
    sums[...] = jnp.zeros_like(sums)
    sums[:8, :] = own_gain[...] + arrived[512:520, :128] + arrived[512:520, 128:256]
    high = sums[...].astype(BF)
    low = (sums[...] - high.astype(F32)).astype(BF)
    gain_sum[...] = (high.astype(F32) + low.astype(F32))[:8, :]
    send_near[256:, :128] = high
    send_near[256:, 128:256] = low
    send_near[256:, 256:] = jnp.zeros((16, 384), BF)


def layer_out_kernel(get, layer_out, flat):
    side_by_side(get(1), flat)
    layer_out[...] = (get(0)[...].astype(F32) + mm(flat[...], get(2)[...], 1, 0)).astype(BF)


def frame_gradient_kernel(get, gain, w_qkv, result, weights, flat, semaphores):
    width = get(0).shape[1]
    copies = []
    for t in range(3):
        part = w_qkv.at[:, t * width : (t + 1) * width]
        copies.append(pltpu.make_async_copy(part, weights.at[t], semaphores.at[t]))
    for copy in copies:
        copy.start()
    xhat, rstd = layernorm(get(0)[...].astype(F32))
    total = None
    for t in range(3):
        for h in range(HEADS):
            flat[t, :, h * 128 : (h + 1) * 128] = get(1)[h][:, t * 128 : (t + 1) * 128]
        copies[t].wait()
        term = mm(weights[t], flat[t], 1, 1)
        total = term if total is None else total + term
    g = total.T * gain[...]
    mean_g = jnp.mean(g, axis=-1, keepdims=True)
    mean_gx = jnp.mean(g * xhat, axis=-1, keepdims=True)
    result[...] = (get(2)[...].astype(F32) + rstd * (g - mean_g - xhat * mean_gx)).astype(BF)


def high_low(x):
    high = lax.reduce_precision(x, 8, 7)
    low = lax.reduce_precision(x - high, 8, 7)
    return high, low


def packed(x, columns):
    high, low = high_low(x)
    both = jnp.concatenate([high, low], axis=1).astype(BF)
    return jnp.pad(both, ((0, 0), (0, columns - 256)))


def unpacked(x):
    return x[:, :128].astype(F32) + x[:, 128:256].astype(F32)


def settled(x):
    high, low = high_low(x)
    return high + low


def on_device(frames, layernorm_gain, w_qkv, w_out, segment_ids, output_gradient):
    x = frames[0]
    grad_out = output_gradient[0]
    rows, width = x.shape
    head = width // HEADS
    scale = head**-0.5
    pos = jnp.stack([lax.axis_index("seq"), lax.axis_index("dp")]).astype(jnp.int32)
    gain_row = layernorm_gain[None, :]

    own = call(
        layernorm_kernel, "layernorm", shape(BF, rows, width), in_specs=[WHOLE] * 2, out_specs=WHOLE
    )(x, gain_row)
    grad_twin = dp_swap(grad_out, 1)
    beside = seq_swap(own, 1)
    after, before = seq_swap(own, 2), seq_swap(own, 6)
    half = rows // 2
    far = [seq_swap(after[:half], 6), seq_swap(before[half:], 2)]
    beyond = [seq_swap(part, 1) for part in far]
    normed = {
        (0, 0): own,
        (1, 0): beside,
        (2, 0): after,
        (6, 0): before,
        (3, 0): seq_swap(beside, 2),
        (7, 0): seq_swap(beside, 6),
        (4, 0): far[0],
        (4, half): far[1],
        (5, 0): beyond[0],
        (5, half): beyond[1],
    }
    places, normed = list(normed), list(normed.values())

    dattn, w_head = staged(
        dattn_kernel,
        "dattn",
        [shape(BF, HEADS, rows, head), shape(BF, width, 384)],
        [pos],
        [grad_out, w_out],
        left=[w_qkv],
        scratch=[pltpu.SemaphoreType.DMA((3,))],
    )
    parts = [mm(n, w_head, 1, 0).astype(BF) for n in normed]
    dattn, grad_twin, _ = lax.optimization_barrier((dattn, grad_twin, beyond[1]))
    dout = seq_exchange(dattn)

    attn_head, dqkv_head = attention(pos, parts, places, dout, segment_ids, scale)
    attn = seq_exchange(attn_head.reshape(8, rows, head))
    dqkv = seq_exchange(dqkv_head.reshape(8, rows, 384))
    wqkv_keep, wqkv_send, gain_part = staged(
        functools.partial(projection_kernel, places),
        "projection_gradient",
        [shape(F32, 512, 384), shape(BF, 528, 384), shape(F32, 8, 128)],
        [pos],
        [dqkv_head, w_head] + normed,
        [gain_row],
        scratch=[
            pltpu.VMEM((1024, 384), F32),
            pltpu.VMEM((512, 384), F32),
            pltpu.VMEM((16, 128), F32),
        ],
    )
    attn, wqkv_send, gain_part = lax.optimization_barrier((attn, wqkv_send, gain_part))
    attn_twin = dp_swap(attn, 1)
    got = dp_swap(wqkv_send, 1)
    near, away, keep, middle, gain_sum = staged(
        output_gradient_kernel,
        "output_gradient",
        [shape(BF, 272, 640), shape(BF, 256, 768)]
        + [shape(F32, 128, 1408)] * 2
        + [shape(F32, 8, 128)],
        [pos],
        [attn, grad_out, attn_twin, grad_twin, wqkv_keep, got],
        [gain_part],
        scratch=[
            pltpu.VMEM((1024, 1024), F32),
            pltpu.VMEM((512, 1024), F32),
            pltpu.VMEM((rows, width), BF),
            pltpu.VMEM((rows, width), BF),
            pltpu.VMEM((16, 128), F32),
        ],
    )
    near, away = dp_swap(near, 4), dp_swap(away, 12)
    (layer_out,) = staged(
        layer_out_kernel,
        "layer_out",
        [shape(BF, rows, width)],
        [],
        [x, attn, w_out],
        scratch=[pltpu.VMEM((rows, width), BF)],
    )
    near, away, layer_out = lax.optimization_barrier((near, away, layer_out))
    gain_sum = gain_sum + unpacked(near[256:264])
    near_next = (middle[:, :640] + near[128:256].astype(F32)).astype(BF)
    near_next = dp_swap(jnp.concatenate([near_next, packed(gain_sum, 640)], axis=0), 12)
    away_next = dp_swap((middle[:, 640:] + away[:128].astype(F32)).astype(BF), 4)
    gain_sum = settled(gain_sum) + unpacked(near_next[128:])
    sums = keep + jnp.concatenate(
        [
            near[:128].astype(F32) + near_next[:128].astype(F32),
            away[128:].astype(F32) + away_next.astype(F32),
        ],
        axis=1,
    )
    got = dp_swap(jnp.concatenate([sums[64:].astype(BF), packed(gain_sum, 1408)], axis=0), 2)
    gain_sum = settled(gain_sum) + unpacked(got[64:])
    sums = sums[:64] + got[:64].astype(F32)
    sums = jnp.concatenate(
        [sums[:, :128], sums[:, 640:896], sums[:, 128:640], sums[:, 896:]], axis=1
    )
    sums, dqkv = lax.optimization_barrier((sums, dqkv))
    (frame_grad,) = staged(
        frame_gradient_kernel,
        "frame_gradient",
        [shape(BF, rows, width)],
        [],
        [x, dqkv, grad_out],
        [gain_row],
        [w_qkv],
        [
            pltpu.VMEM((3, width, width), BF),
            pltpu.VMEM((3, rows, width), BF),
            pltpu.SemaphoreType.DMA((3,)),
        ],
    )

    note = jnp.broadcast_to(packed(gain_sum, 256)[None], (8, 8, 256))
    got = seq_exchange(jnp.concatenate([sums.reshape(8, 8, 1408).astype(BF), note], axis=2))
    grad_wqkv = got[:, :, :384].reshape(8, 8, 3, head).transpose(1, 2, 0, 3).reshape(8, 3 * width)
    grad_wout = jnp.sum(got[:, :, 384:1408].astype(F32), axis=0).astype(BF)
    totals = [unpacked(got[s, :, 1408:]) for s in range(8)]
    grad_gain = functools.reduce(lambda a, b: a + b, totals).reshape(width)
    return (
        layer_out[None],
        frame_grad[None],
        grad_wqkv,
        grad_wout,
        grad_gain,
    )


def solution(mesh):
    placed = (P("dp", "seq", None), P(), P(), P(), P("dp", None), P("dp", "seq", None))
    return jax.shard_map(
        on_device,
        mesh=mesh,
        in_specs=placed,
        out_specs=(
            P("dp", "seq", None),
            P("dp", "seq", None),
            P(("seq", "dp"), None),
            P(("seq", "dp"), None),
            P(),
        ),
        check_vma=False,
    )
```

```python
import functools

import jax
import jax.numpy as jnp
from jax import lax
from jax.experimental import pallas as pl
from jax.experimental.pallas import tpu as pltpu
from jax.sharding import PartitionSpec as P

HEADS = 8
BF = jnp.bfloat16
F32 = jnp.float32
LOG2E = 1.4426950408889634
PAIR = 4
CHUNK = 256
VMEM_LIMIT = 60 * 1024 * 1024
WHOLE = pl.BlockSpec(memory_space=pltpu.VMEM)
SCALARS = pl.BlockSpec(memory_space=pltpu.SMEM)


def seq_swap(x, bits):
    return lax.ppermute(x, "seq", [(i, i ^ bits) for i in range(8)])


def dp_swap(x, bits):
    return lax.ppermute(x, "dp", [(i, i ^ bits) for i in range(16)])


def seq_exchange(x):
    return lax.all_to_all(x, "seq", 0, 0, tiled=True)


def mm(a, b, ca, cb):
    return lax.dot_general(a, b, (((ca,), (cb,)), ((), ())), preferred_element_type=F32)


def call(kernel, name, out_shape, **options):
    return pl.pallas_call(
        kernel,
        out_shape=out_shape,
        compiler_params=pltpu.CompilerParams(vmem_limit_bytes=VMEM_LIMIT),
        name=name,
        **options,
    )


def shape(dtype, *dims):
    return jax.ShapeDtypeStruct(dims, dtype)


def layernorm(x):
    center = x - jnp.mean(x, axis=-1, keepdims=True)
    rstd = lax.rsqrt(jnp.mean(center * center, axis=-1, keepdims=True) + 1e-05)
    return center * rstd, rstd


def staged(body, name, out_shape, scalars, arrays, plain=(), left=(), scratch=()):
    n, m, k = len(scalars), len(arrays), len(plain) + len(left)

    def kernel(*refs):
        sources, others = refs[n : n + m], refs[n + m : n + m + k]
        outs = refs[n + m + k : n + m + k + len(out_shape)]
        rest = refs[n + m + k + len(out_shape) :]
        buffers, semaphores, rest = rest[:m], rest[m], rest[m + 1 :]
        copies = [
            pltpu.make_async_copy(sources[i], buffers[i], semaphores.at[i]) for i in range(m)
        ]
        for copy in copies:
            copy.start()
        waited = set()

        def get(i):
            if i not in waited:
                waited.add(i)
                copies[i].wait()
            return buffers[i]

        body(*refs[:n], get, *others, *outs, *rest)
        for i in range(m):
            get(i)

    return call(
        kernel,
        name,
        tuple(out_shape),
        in_specs=[SCALARS] * n
        + [pl.BlockSpec(memory_space=pltpu.HBM)] * m
        + [WHOLE] * len(plain)
        + [pl.BlockSpec(memory_space=pltpu.HBM)] * len(left),
        out_specs=(WHOLE,) * len(out_shape),
        scratch_shapes=[pltpu.VMEM(a.shape, a.dtype) for a in arrays]
        + [pltpu.SemaphoreType.DMA((m,))]
        + list(scratch),
    )(*scalars, *arrays, *plain, *left)


def layernorm_kernel(frames, gain, normed):
    xhat, _ = layernorm(frames[...].astype(F32))
    normed[...] = (xhat * gain[...]).astype(BF)


def dattn_kernel(pos, get, w_qkv, dattn, w_head, semaphores):
    copies = []
    for t in range(3):
        start = pl.multiple_of(t * 1024 + pos[0] * 128, 128)
        copies.append(
            pltpu.make_async_copy(
                w_qkv.at[:, pl.ds(start, 128)],
                w_head.at[:, t * 128 : (t + 1) * 128],
                semaphores.at[t],
            )
        )
    for copy in copies:
        copy.start()
    full = mm(get(0)[...], get(1)[...], 1, 1).astype(BF)
    for h in range(HEADS):
        dattn[h] = full[:, h * 128 : (h + 1) * 128]
    for copy in copies:
        copy.wait()


def attention_kernel(scale, places, pos, *refs):
    count = len(places)
    parts, (dout, ids) = refs[:count], refs[count : count + 2]
    attn, dqkv, q_s, k_s, v_s, kt_s, vt_s, dk_s, dv_s, s_s, p_s, l_s = refs[count + 2 :]
    rows = dout.shape[1]
    for part, (r, offset) in zip(parts, places):
        size = part.shape[0]
        rng = pl.ds(pl.multiple_of((pos[0] ^ r) * rows + offset, size), size)
        q_s[rng, :128] = part[:, :128]
        k_s[rng, :128] = part[:, 128:256]
        v_s[rng, :] = part[:, 256:]
    names = lax.broadcasted_iota(jnp.int32, (128, 8 * rows), 0)
    same = jnp.where(ids[...] == names, 1.0, 0.0).T
    q_s[:, 128:] = ((same - 1.0) * 1e30).astype(BF)
    k_s[:, 128:] = same.astype(BF)
    kt_s[...] = k_s[:, :128].T
    vt_s[...] = v_s[...].T
    dk_s[...] = jnp.zeros_like(dk_s)
    dv_s[...] = jnp.zeros_like(dv_s)

    size = min(CHUNK, 8 * rows)
    chunks = [slice(c, c + size) for c in range(0, 8 * rows, size)]

    def step(i, carry):
        for u in range(PAIR):
            block = i * PAIR + u
            rng = pl.ds(pl.multiple_of(block * rows, rows), rows)
            q, do, slot = q_s[rng, :], dout[block], u % 2
            peak = None
            for part in chunks:
                scores = mm(k_s[part, :], q, 1, 1)
                s_s[slot, part, :] = scores
                top = jnp.max(scores.reshape(-1, 8, rows), axis=0)
                peak = top if peak is None else jnp.maximum(peak, top)
            peak = jnp.max(peak, axis=0, keepdims=True)
            total = None
            for part in chunks:
                p_s[slot, part, :] = mm(v_s[part, :], do, 1, 1)
                expo = jnp.exp2((s_s[slot, part, :] - peak) * (scale * LOG2E))
                s_s[slot, part, :] = expo
                add = jnp.sum(expo.reshape(-1, 8, rows), axis=0)
                total = add if total is None else total + add
            inverse = 1.0 / jnp.sum(total, axis=0, keepdims=True)
            out = None
            for part in chunks:
                low = (s_s[slot, part, :] * inverse).astype(BF)
                l_s[slot, part, :] = low
                add = mm(vt_s[:, part], low, 1, 0)
                out = add if out is None else out + add
                dv_s[part, :] += mm(low, do, 1, 0)
            delta = jnp.sum(out * do.astype(F32).T, axis=0, keepdims=True)
            dq = None
            for part in chunks:
                dscores = l_s[slot, part, :].astype(F32) * (p_s[slot, part, :] - delta)
                dscores = dscores.astype(BF)
                dk_s[part, :] += mm(dscores, q[:, :128], 1, 0)
                add = mm(kt_s[:, part], dscores, 1, 0)
                dq = add if dq is None else dq + add
            attn[rng, :] = out.T.astype(BF)
            dqkv[rng, :128] = (dq * scale).T.astype(BF)
        return carry

    lax.fori_loop(0, 8 // PAIR, step, 0)
    dqkv[:, 128:256] = (dk_s[...] * scale).astype(BF)
    dqkv[:, 256:] = dv_s[...].astype(BF)


def attention(pos, parts, places, dout, ids, scale):
    total = ids.shape[1]
    return call(
        functools.partial(attention_kernel, scale, places),
        "attention",
        (shape(BF, total, 128), shape(BF, total, 384)),
        in_specs=[SCALARS] + [WHOLE] * (len(parts) + 2),
        out_specs=(WHOLE, WHOLE),
        scratch_shapes=[
            pltpu.VMEM((total, 256), BF),
            pltpu.VMEM((total, 256), BF),
            pltpu.VMEM((total, 128), BF),
            pltpu.VMEM((128, total), BF),
            pltpu.VMEM((128, total), BF),
            pltpu.VMEM((total, 128), F32),
            pltpu.VMEM((total, 128), F32),
            pltpu.VMEM((2, total, total // 8), F32),
            pltpu.VMEM((2, total, total // 8), F32),
            pltpu.VMEM((2, total, total // 8), BF),
        ],
    )(pos, *parts, dout, ids)


def chosen_rows(dp, source, half, target):
    for r in range(8):
        for s in range(8):
            rows = pl.ds(pl.multiple_of(s * 128 + (dp ^ (2 * r + half)) * 8, 8), 8)
            target[r * 64 + s * 8 : r * 64 + s * 8 + 8, :] = source[rows, :]


def projection_kernel(places, pos, get, gain, keep, send, own_gain, grad, other, sums):
    dqkv, weights = get(0), get(1)
    rows = dqkv.shape[0] // 8
    total = None
    for i, (r, offset) in enumerate(places):
        normed = get(2 + i)
        size = normed.shape[0]
        rng = pl.ds(pl.multiple_of((pos[0] ^ r) * rows + offset, size), size)
        term = mm(dqkv[rng, :], normed[...], 0, 0)
        total = term if total is None else total + term
    grad[...] = total.T
    weighted = jnp.sum(total * weights[...].T.astype(F32), axis=0, keepdims=True) / gain[...]
    sums[...] = jnp.zeros_like(sums)
    for j in range(8):
        sums[j : j + 1, :] = weighted[:, j * 128 : (j + 1) * 128]
    high = sums[...].astype(BF)
    low = (sums[...] - high.astype(F32)).astype(BF)
    own_gain[...] = (high.astype(F32) + low.astype(F32))[:8, :]
    chosen_rows(pos[1], grad, 0, keep)
    chosen_rows(pos[1], grad, 1, other)
    send[:512, :] = other[...].astype(BF)
    send[512:, :128] = high
    send[512:, 128:256] = low
    send[512:, 256:] = jnp.zeros_like(low)


def side_by_side(source, target):
    for h in range(HEADS):
        target[:, h * 128 : (h + 1) * 128] = source[h]


def output_gradient_kernel(
    pos, get, own_gain, send_near, send_far, keep, middle, gain_sum, grad, chosen, flat, twin, sums
):
    side_by_side(get(0), flat)
    own = mm(flat[...], get(1)[...], 0, 0)
    side_by_side(get(2), twin)
    grad[...] = own + mm(twin[...], get(3)[...], 0, 0)
    chosen_rows(pos[1], grad, 0, chosen)
    arrived = get(5)[...].astype(F32)
    qkv = get(4)[...] + arrived[:512, :]
    left, right = slice(0, 640), slice(640, 1408)
    first, second = qkv[:, :128], qkv[:, 128:]
    send_near[:256, :128] = first[128:384].astype(BF)
    send_near[:256, 128:] = chosen[128:384, :512].astype(BF)
    send_far[:, :256] = second[256:].astype(BF)
    send_far[:, 256:] = chosen[256:, 512:].astype(BF)
    for target, near_rows, far_rows in (
        (keep, slice(0, 128), slice(0, 128)),
        (middle, slice(384, 512), slice(128, 256)),
    ):
        target[:, left] = jnp.concatenate([first[near_rows], chosen[near_rows, :512]], axis=1)
        target[:, right] = jnp.concatenate([second[far_rows], chosen[far_rows, 512:]], axis=1)
    sums[...] = jnp.zeros_like(sums)
    sums[:8, :] = own_gain[...] + arrived[512:520, :128] + arrived[512:520, 128:256]
    high = sums[...].astype(BF)
    low = (sums[...] - high.astype(F32)).astype(BF)
    gain_sum[...] = (high.astype(F32) + low.astype(F32))[:8, :]
    send_near[256:, :128] = high
    send_near[256:, 128:256] = low
    send_near[256:, 256:] = jnp.zeros((16, 384), BF)


def layer_out_kernel(get, layer_out, flat):
    side_by_side(get(1), flat)
    layer_out[...] = (get(0)[...].astype(F32) + mm(flat[...], get(2)[...], 1, 0)).astype(BF)


def frame_gradient_kernel(get, gain, w_qkv, result, weights, flat, semaphores):
    width = get(0).shape[1]
    copies = []
    for t in range(3):
        part = w_qkv.at[:, t * width : (t + 1) * width]
        copies.append(pltpu.make_async_copy(part, weights.at[t], semaphores.at[t]))
    for copy in copies:
        copy.start()
    xhat, rstd = layernorm(get(0)[...].astype(F32))
    total = None
    for t in range(3):
        for h in range(HEADS):
            flat[t, :, h * 128 : (h + 1) * 128] = get(1)[h][:, t * 128 : (t + 1) * 128]
        copies[t].wait()
        term = mm(weights[t], flat[t], 1, 1)
        total = term if total is None else total + term
    g = total.T * gain[...]
    mean_g = jnp.mean(g, axis=-1, keepdims=True)
    mean_gx = jnp.mean(g * xhat, axis=-1, keepdims=True)
    result[...] = (get(2)[...].astype(F32) + rstd * (g - mean_g - xhat * mean_gx)).astype(BF)


def high_low(x):
    high = lax.reduce_precision(x, 8, 7)
    low = lax.reduce_precision(x - high, 8, 7)
    return high, low


def packed(x, columns):
    high, low = high_low(x)
    both = jnp.concatenate([high, low], axis=1).astype(BF)
    return jnp.pad(both, ((0, 0), (0, columns - 256)))


def unpacked(x):
    return x[:, :128].astype(F32) + x[:, 128:256].astype(F32)


def settled(x):
    high, low = high_low(x)
    return high + low


def on_device(frames, layernorm_gain, w_qkv, w_out, segment_ids, output_gradient):
    x = frames[0]
    grad_out = output_gradient[0]
    rows, width = x.shape
    head = width // HEADS
    scale = head**-0.5
    pos = jnp.stack([lax.axis_index("seq"), lax.axis_index("dp")]).astype(jnp.int32)
    gain_row = layernorm_gain[None, :]

    own = call(
        layernorm_kernel, "layernorm", shape(BF, rows, width), in_specs=[WHOLE] * 2, out_specs=WHOLE
    )(x, gain_row)
    grad_twin = dp_swap(grad_out, 1)
    beside = seq_swap(own, 1)
    after, before = seq_swap(own, 2), seq_swap(own, 6)
    half = rows // 2
    far = [seq_swap(after[:half], 6), seq_swap(before[half:], 2)]
    beyond = [seq_swap(part, 1) for part in far]
    normed = {
        (0, 0): own,
        (1, 0): beside,
        (2, 0): after,
        (6, 0): before,
        (3, 0): seq_swap(beside, 2),
        (7, 0): seq_swap(beside, 6),
        (4, 0): far[0],
        (4, half): far[1],
        (5, 0): beyond[0],
        (5, half): beyond[1],
    }
    places, normed = list(normed), list(normed.values())

    dattn, w_head = staged(
        dattn_kernel,
        "dattn",
        [shape(BF, HEADS, rows, head), shape(BF, width, 384)],
        [pos],
        [grad_out, w_out],
        left=[w_qkv],
        scratch=[pltpu.SemaphoreType.DMA((3,))],
    )
    parts = [mm(n, w_head, 1, 0).astype(BF) for n in normed]
    dattn, grad_twin, _ = lax.optimization_barrier((dattn, grad_twin, beyond[1]))
    dout = seq_exchange(dattn)

    attn_head, dqkv_head = attention(pos, parts, places, dout, segment_ids, scale)
    attn = seq_exchange(attn_head.reshape(8, rows, head))
    dqkv = seq_exchange(dqkv_head.reshape(8, rows, 384))
    wqkv_keep, wqkv_send, gain_part = staged(
        functools.partial(projection_kernel, places),
        "projection_gradient",
        [shape(F32, 512, 384), shape(BF, 528, 384), shape(F32, 8, 128)],
        [pos],
        [dqkv_head, w_head] + normed,
        [gain_row],
        scratch=[
            pltpu.VMEM((1024, 384), F32),
            pltpu.VMEM((512, 384), F32),
            pltpu.VMEM((16, 128), F32),
        ],
    )
    attn, wqkv_send, gain_part = lax.optimization_barrier((attn, wqkv_send, gain_part))
    attn_twin = dp_swap(attn, 1)
    got = dp_swap(wqkv_send, 1)
    near, away, keep, middle, gain_sum = staged(
        output_gradient_kernel,
        "output_gradient",
        [shape(BF, 272, 640), shape(BF, 256, 768)]
        + [shape(F32, 128, 1408)] * 2
        + [shape(F32, 8, 128)],
        [pos],
        [attn, grad_out, attn_twin, grad_twin, wqkv_keep, got],
        [gain_part],
        scratch=[
            pltpu.VMEM((1024, 1024), F32),
            pltpu.VMEM((512, 1024), F32),
            pltpu.VMEM((rows, width), BF),
            pltpu.VMEM((rows, width), BF),
            pltpu.VMEM((16, 128), F32),
        ],
    )
    near, away = dp_swap(near, 4), dp_swap(away, 12)
    (layer_out,) = staged(
        layer_out_kernel,
        "layer_out",
        [shape(BF, rows, width)],
        [],
        [x, attn, w_out],
        scratch=[pltpu.VMEM((rows, width), BF)],
    )
    near, away, layer_out = lax.optimization_barrier((near, away, layer_out))
    gain_sum = gain_sum + unpacked(near[256:264])
    near_next = (middle[:, :640] + near[128:256].astype(F32)).astype(BF)
    near_next = dp_swap(jnp.concatenate([near_next, packed(gain_sum, 640)], axis=0), 12)
    away_next = dp_swap((middle[:, 640:] + away[:128].astype(F32)).astype(BF), 4)
    gain_sum = settled(gain_sum) + unpacked(near_next[128:])
    sums = keep + jnp.concatenate(
        [
            near[:128].astype(F32) + near_next[:128].astype(F32),
            away[128:].astype(F32) + away_next.astype(F32),
        ],
        axis=1,
    )
    got = dp_swap(jnp.concatenate([sums[64:].astype(BF), packed(gain_sum, 1408)], axis=0), 2)
    gain_sum = settled(gain_sum) + unpacked(got[64:])
    sums = sums[:64] + got[:64].astype(F32)
    sums = jnp.concatenate(
        [sums[:, :128], sums[:, 640:896], sums[:, 128:640], sums[:, 896:]], axis=1
    )
    sums, dqkv = lax.optimization_barrier((sums, dqkv))
    (frame_grad,) = staged(
        frame_gradient_kernel,
        "frame_gradient",
        [shape(BF, rows, width)],
        [],
        [x, dqkv, grad_out],
        [gain_row],
        [w_qkv],
        [
            pltpu.VMEM((3, width, width), BF),
            pltpu.VMEM((3, rows, width), BF),
            pltpu.SemaphoreType.DMA((3,)),
        ],
    )

    note = jnp.broadcast_to(packed(gain_sum, 256)[None], (8, 8, 256))
    got = seq_exchange(jnp.concatenate([sums.reshape(8, 8, 1408).astype(BF), note], axis=2))
    grad_wqkv = got[:, :, :384].reshape(8, 8, 3, head).transpose(1, 2, 0, 3).reshape(8, 3 * width)
    grad_wout = jnp.sum(got[:, :, 384:1408].astype(F32), axis=0).astype(BF)
    totals = [unpacked(got[s, :, 1408:]) for s in range(8)]
    grad_gain = functools.reduce(lambda a, b: a + b, totals).reshape(width)
    return (
        layer_out[None],
        frame_grad[None],
        grad_wqkv,
        grad_wout,
        grad_gain,
    )


def solution(mesh):
    placed = (P("dp", "seq", None), P(), P(), P(), P("dp", None), P("dp", "seq", None))
    return jax.shard_map(
        on_device,
        mesh=mesh,
        in_specs=placed,
        out_specs=(
            P("dp", "seq", None),
            P("dp", "seq", None),
            P(("seq", "dp"), None),
            P(("seq", "dp"), None),
            P(),
        ),
        check_vma=False,
    )
```

```python
import functools

import jax
import jax.numpy as jnp
from jax import lax
from jax.experimental import pallas as pl
from jax.experimental.pallas import tpu as pltpu
from jax.sharding import PartitionSpec as P

HEADS = 8
BF = jnp.bfloat16
F32 = jnp.float32
LOG2E = 1.4426950408889634
PAIR = 4
CHUNK = 256
VMEM_LIMIT = 60 * 1024 * 1024
WHOLE = pl.BlockSpec(memory_space=pltpu.VMEM)
SCALARS = pl.BlockSpec(memory_space=pltpu.SMEM)


def seq_swap(x, bits):
    return lax.ppermute(x, "seq", [(i, i ^ bits) for i in range(8)])


def dp_swap(x, bits):
    return lax.ppermute(x, "dp", [(i, i ^ bits) for i in range(16)])


def seq_exchange(x):
    return lax.all_to_all(x, "seq", 0, 0, tiled=True)


def mm(a, b, ca, cb):
    return lax.dot_general(a, b, (((ca,), (cb,)), ((), ())), preferred_element_type=F32)


def call(kernel, name, out_shape, vmem=VMEM_LIMIT, **options):
    return pl.pallas_call(
        kernel,
        out_shape=out_shape,
        compiler_params=pltpu.CompilerParams(vmem_limit_bytes=vmem),
        name=name,
        **options,
    )


def shape(dtype, *dims):
    return jax.ShapeDtypeStruct(dims, dtype)


def layernorm(x):
    center = x - jnp.mean(x, axis=-1, keepdims=True)
    rstd = lax.rsqrt(jnp.mean(center * center, axis=-1, keepdims=True) + 1e-05)
    return center * rstd, rstd


def staged(
    body, name, out_shape, scalars, arrays, plain=(), left=(), scratch=(), vmem=VMEM_LIMIT
):
    n, m, k = len(scalars), len(arrays), len(plain) + len(left)

    def kernel(*refs):
        sources, others = refs[n : n + m], refs[n + m : n + m + k]
        outs = refs[n + m + k : n + m + k + len(out_shape)]
        rest = refs[n + m + k + len(out_shape) :]
        buffers, semaphores, rest = rest[:m], rest[m], rest[m + 1 :]
        copies = [
            pltpu.make_async_copy(sources[i], buffers[i], semaphores.at[i]) for i in range(m)
        ]
        for copy in copies:
            copy.start()
        waited = set()

        def get(i):
            if i not in waited:
                waited.add(i)
                copies[i].wait()
            return buffers[i]

        body(*refs[:n], get, *others, *outs, *rest)
        for i in range(m):
            get(i)

    return call(
        kernel,
        name,
        tuple(out_shape),
        vmem,
        in_specs=[SCALARS] * n
        + [pl.BlockSpec(memory_space=pltpu.HBM)] * m
        + [WHOLE] * len(plain)
        + [pl.BlockSpec(memory_space=pltpu.HBM)] * len(left),
        out_specs=(WHOLE,) * len(out_shape),
        scratch_shapes=[pltpu.VMEM(a.shape, a.dtype) for a in arrays]
        + [pltpu.SemaphoreType.DMA((m,))]
        + list(scratch),
    )(*scalars, *arrays, *plain, *left)


def layernorm_kernel(frames, gain, normed):
    xhat, _ = layernorm(frames[...].astype(F32))
    normed[...] = (xhat * gain[...]).astype(BF)


def dattn_kernel(pos, get, w_qkv, dattn, w_head, semaphores):
    copies = []
    for t in range(3):
        start = pl.multiple_of(t * 1024 + pos[0] * 128, 128)
        copies.append(
            pltpu.make_async_copy(
                w_qkv.at[:, pl.ds(start, 128)],
                w_head.at[:, t * 128 : (t + 1) * 128],
                semaphores.at[t],
            )
        )
    for copy in copies:
        copy.start()
    full = mm(get(0)[...], get(1)[...], 1, 1).astype(BF)
    for h in range(HEADS):
        dattn[h] = full[:, h * 128 : (h + 1) * 128]
    for copy in copies:
        copy.wait()


def attention_kernel(scale, places, pos, *refs):
    count = len(places)
    parts, (dout, ids) = refs[:count], refs[count : count + 2]
    attn, dqkv, q_s, k_s, v_s, kt_s, vt_s, dk_s, dv_s, s_s, p_s, l_s = refs[count + 2 :]
    rows = dout.shape[1]
    for part, (r, offset) in zip(parts, places):
        size = part.shape[0]
        rng = pl.ds(pl.multiple_of((pos[0] ^ r) * rows + offset, size), size)
        q_s[rng, :128] = part[:, :128]
        k_s[rng, :128] = part[:, 128:256]
        v_s[rng, :] = part[:, 256:]
    names = lax.broadcasted_iota(jnp.int32, (128, 8 * rows), 0)
    same = jnp.where(ids[...] == names, 1.0, 0.0).T
    q_s[:, 128:] = ((same - 1.0) * 1e30).astype(BF)
    k_s[:, 128:] = same.astype(BF)
    kt_s[...] = k_s[:, :128].T
    vt_s[...] = v_s[...].T
    dk_s[...] = jnp.zeros_like(dk_s)
    dv_s[...] = jnp.zeros_like(dv_s)

    size = min(CHUNK, 8 * rows)
    chunks = [slice(c, c + size) for c in range(0, 8 * rows, size)]

    def step(i, carry):
        for u in range(PAIR):
            block = i * PAIR + u
            rng = pl.ds(pl.multiple_of(block * rows, rows), rows)
            q, do, slot = q_s[rng, :], dout[block], u % 2
            peak = None
            for part in chunks:
                scores = mm(k_s[part, :], q, 1, 1)
                s_s[slot, part, :] = scores
                top = jnp.max(scores.reshape(-1, 8, rows), axis=0)
                peak = top if peak is None else jnp.maximum(peak, top)
            peak = jnp.max(peak, axis=0, keepdims=True)
            total = None
            for part in chunks:
                p_s[slot, part, :] = mm(v_s[part, :], do, 1, 1)
                expo = jnp.exp2((s_s[slot, part, :] - peak) * (scale * LOG2E))
                s_s[slot, part, :] = expo
                add = jnp.sum(expo.reshape(-1, 8, rows), axis=0)
                total = add if total is None else total + add
            inverse = 1.0 / jnp.sum(total, axis=0, keepdims=True)
            out = None
            for part in chunks:
                low = (s_s[slot, part, :] * inverse).astype(BF)
                l_s[slot, part, :] = low
                add = mm(vt_s[:, part], low, 1, 0)
                out = add if out is None else out + add
                dv_s[part, :] += mm(low, do, 1, 0)
            delta = jnp.sum(out * do.astype(F32).T, axis=0, keepdims=True)
            dq = None
            for part in chunks:
                dscores = l_s[slot, part, :].astype(F32) * (p_s[slot, part, :] - delta)
                dscores = dscores.astype(BF)
                dk_s[part, :] += mm(dscores, q[:, :128], 1, 0)
                add = mm(kt_s[:, part], dscores, 1, 0)
                dq = add if dq is None else dq + add
            attn[rng, :] = out.T.astype(BF)
            dqkv[rng, :128] = (dq * scale).T.astype(BF)
        return carry

    lax.fori_loop(0, 8 // PAIR, step, 0)
    dqkv[:, 128:256] = (dk_s[...] * scale).astype(BF)
    dqkv[:, 256:] = dv_s[...].astype(BF)


def attention(pos, parts, places, dout, ids, scale):
    total = ids.shape[1]
    return call(
        functools.partial(attention_kernel, scale, places),
        "attention",
        (shape(BF, total, 128), shape(BF, total, 384)),
        vmem=48 * 1024 * 1024,
        in_specs=[SCALARS] + [WHOLE] * (len(parts) + 2),
        out_specs=(WHOLE, WHOLE),
        scratch_shapes=[
            pltpu.VMEM((total, 256), BF),
            pltpu.VMEM((total, 256), BF),
            pltpu.VMEM((total, 128), BF),
            pltpu.VMEM((128, total), BF),
            pltpu.VMEM((128, total), BF),
            pltpu.VMEM((total, 128), F32),
            pltpu.VMEM((total, 128), F32),
            pltpu.VMEM((2, total, total // 8), F32),
            pltpu.VMEM((2, total, total // 8), F32),
            pltpu.VMEM((2, total, total // 8), BF),
        ],
    )(pos, *parts, dout, ids)


def chosen_rows(dp, source, half, target):
    for r in range(8):
        for s in range(8):
            rows = pl.ds(pl.multiple_of(s * 128 + (dp ^ (2 * r + half)) * 8, 8), 8)
            target[r * 64 + s * 8 : r * 64 + s * 8 + 8, :] = source[rows, :]


def projection_kernel(places, pos, get, gain, keep, send, own_gain, grad, other, sums):
    dqkv, weights = get(0), get(1)
    rows = dqkv.shape[0] // 8
    total = None
    for i, (r, offset) in enumerate(places):
        normed = get(2 + i)
        size = normed.shape[0]
        rng = pl.ds(pl.multiple_of((pos[0] ^ r) * rows + offset, size), size)
        term = mm(dqkv[rng, :], normed[...], 0, 0)
        total = term if total is None else total + term
    grad[...] = total.T
    weighted = jnp.sum(total * weights[...].T.astype(F32), axis=0, keepdims=True) / gain[...]
    sums[...] = jnp.zeros_like(sums)
    for j in range(8):
        sums[j : j + 1, :] = weighted[:, j * 128 : (j + 1) * 128]
    high = sums[...].astype(BF)
    low = (sums[...] - high.astype(F32)).astype(BF)
    own_gain[...] = (high.astype(F32) + low.astype(F32))[:8, :]
    chosen_rows(pos[1], grad, 0, keep)
    chosen_rows(pos[1], grad, 1, other)
    send[:512, :] = other[...].astype(BF)
    send[512:, :128] = high
    send[512:, 128:256] = low
    send[512:, 256:] = jnp.zeros_like(low)


def side_by_side(source, target):
    for h in range(HEADS):
        target[:, h * 128 : (h + 1) * 128] = source[h]


def output_gradient_kernel(
    pos, get, own_gain, send_near, send_far, keep, middle, gain_sum, grad, chosen, flat, twin, sums
):
    side_by_side(get(0), flat)
    own = mm(flat[...], get(1)[...], 0, 0)
    side_by_side(get(2), twin)
    grad[...] = own + mm(twin[...], get(3)[...], 0, 0)
    chosen_rows(pos[1], grad, 0, chosen)
    arrived = get(5)[...].astype(F32)
    qkv = get(4)[...] + arrived[:512, :]
    left, right = slice(0, 640), slice(640, 1408)
    first, second = qkv[:, :128], qkv[:, 128:]
    send_near[:256, :128] = first[128:384].astype(BF)
    send_near[:256, 128:] = chosen[128:384, :512].astype(BF)
    send_far[:, :256] = second[256:].astype(BF)
    send_far[:, 256:] = chosen[256:, 512:].astype(BF)
    for target, near_rows, far_rows in (
        (keep, slice(0, 128), slice(0, 128)),
        (middle, slice(384, 512), slice(128, 256)),
    ):
        target[:, left] = jnp.concatenate([first[near_rows], chosen[near_rows, :512]], axis=1)
        target[:, right] = jnp.concatenate([second[far_rows], chosen[far_rows, 512:]], axis=1)
    sums[...] = jnp.zeros_like(sums)
    sums[:8, :] = own_gain[...] + arrived[512:520, :128] + arrived[512:520, 128:256]
    high = sums[...].astype(BF)
    low = (sums[...] - high.astype(F32)).astype(BF)
    gain_sum[...] = (high.astype(F32) + low.astype(F32))[:8, :]
    send_near[256:, :128] = high
    send_near[256:, 128:256] = low
    send_near[256:, 256:] = jnp.zeros((16, 384), BF)


def layer_out_kernel(get, layer_out, flat):
    side_by_side(get(1), flat)
    layer_out[...] = (get(0)[...].astype(F32) + mm(flat[...], get(2)[...], 1, 0)).astype(BF)


def frame_gradient_kernel(get, gain, w_qkv, result, weights, flat, semaphores):
    width = get(0).shape[1]
    copies = []
    for t in range(3):
        part = w_qkv.at[:, t * width : (t + 1) * width]
        copies.append(pltpu.make_async_copy(part, weights.at[t], semaphores.at[t]))
    for copy in copies:
        copy.start()
    xhat, rstd = layernorm(get(0)[...].astype(F32))
    total = None
    for t in range(3):
        for h in range(HEADS):
            flat[t, :, h * 128 : (h + 1) * 128] = get(1)[h][:, t * 128 : (t + 1) * 128]
        copies[t].wait()
        term = mm(weights[t], flat[t], 1, 1)
        total = term if total is None else total + term
    g = total.T * gain[...]
    mean_g = jnp.mean(g, axis=-1, keepdims=True)
    mean_gx = jnp.mean(g * xhat, axis=-1, keepdims=True)
    result[...] = (get(2)[...].astype(F32) + rstd * (g - mean_g - xhat * mean_gx)).astype(BF)


def high_low(x):
    high = lax.reduce_precision(x, 8, 7)
    low = lax.reduce_precision(x - high, 8, 7)
    return high, low


def packed(x, columns):
    high, low = high_low(x)
    both = jnp.concatenate([high, low], axis=1).astype(BF)
    return jnp.pad(both, ((0, 0), (0, columns - 256)))


def unpacked(x):
    return x[:, :128].astype(F32) + x[:, 128:256].astype(F32)


def settled(x):
    high, low = high_low(x)
    return high + low


def on_device(frames, layernorm_gain, w_qkv, w_out, segment_ids, output_gradient):
    x = frames[0]
    grad_out = output_gradient[0]
    rows, width = x.shape
    head = width // HEADS
    scale = head**-0.5
    pos = jnp.stack([lax.axis_index("seq"), lax.axis_index("dp")]).astype(jnp.int32)
    gain_row = layernorm_gain[None, :]

    own = call(
        layernorm_kernel, "layernorm", shape(BF, rows, width), in_specs=[WHOLE] * 2, out_specs=WHOLE
    )(x, gain_row)
    grad_twin = dp_swap(grad_out, 1)
    beside = seq_swap(own, 1)
    after, before = seq_swap(own, 2), seq_swap(own, 6)
    half = rows // 2
    far = [seq_swap(after[:half], 6), seq_swap(before[half:], 2)]
    beyond = [seq_swap(part, 1) for part in far]
    normed = {
        (0, 0): own,
        (1, 0): beside,
        (2, 0): after,
        (6, 0): before,
        (3, 0): seq_swap(beside, 2),
        (7, 0): seq_swap(beside, 6),
        (4, 0): far[0],
        (4, half): far[1],
        (5, 0): beyond[0],
        (5, half): beyond[1],
    }
    places, normed = list(normed), list(normed.values())

    dattn, w_head = staged(
        dattn_kernel,
        "dattn",
        [shape(BF, HEADS, rows, head), shape(BF, width, 384)],
        [pos],
        [grad_out, w_out],
        left=[w_qkv],
        scratch=[pltpu.SemaphoreType.DMA((3,))],
    )
    parts = [mm(n, w_head, 1, 0).astype(BF) for n in normed]
    dattn, grad_twin, _ = lax.optimization_barrier((dattn, grad_twin, beyond[1]))
    dout = seq_exchange(dattn)

    attn_head, dqkv_head = attention(pos, parts, places, dout, segment_ids, scale)
    attn = seq_exchange(attn_head.reshape(8, rows, head))
    dqkv = seq_exchange(dqkv_head.reshape(8, rows, 384))
    wqkv_keep, wqkv_send, gain_part = staged(
        functools.partial(projection_kernel, places),
        "projection_gradient",
        [shape(F32, 512, 384), shape(BF, 528, 384), shape(F32, 8, 128)],
        [pos],
        [dqkv_head, w_head] + normed,
        [gain_row],
        scratch=[
            pltpu.VMEM((1024, 384), F32),
            pltpu.VMEM((512, 384), F32),
            pltpu.VMEM((16, 128), F32),
        ],
    )
    attn, wqkv_send, gain_part = lax.optimization_barrier((attn, wqkv_send, gain_part))
    attn_twin = dp_swap(attn, 1)
    got = dp_swap(wqkv_send, 1)
    near, away, keep, middle, gain_sum = staged(
        output_gradient_kernel,
        "output_gradient",
        [shape(BF, 272, 640), shape(BF, 256, 768)]
        + [shape(F32, 128, 1408)] * 2
        + [shape(F32, 8, 128)],
        [pos],
        [attn, grad_out, attn_twin, grad_twin, wqkv_keep, got],
        [gain_part],
        scratch=[
            pltpu.VMEM((1024, 1024), F32),
            pltpu.VMEM((512, 1024), F32),
            pltpu.VMEM((rows, width), BF),
            pltpu.VMEM((rows, width), BF),
            pltpu.VMEM((16, 128), F32),
        ],
        vmem=40 * 1024 * 1024,
    )
    near, away = dp_swap(near, 4), dp_swap(away, 12)
    (layer_out,) = staged(
        layer_out_kernel,
        "layer_out",
        [shape(BF, rows, width)],
        [],
        [x, attn, w_out],
        scratch=[pltpu.VMEM((rows, width), BF)],
    )
    near, away, layer_out = lax.optimization_barrier((near, away, layer_out))
    gain_sum = gain_sum + unpacked(near[256:264])
    near_next = (middle[:, :640] + near[128:256].astype(F32)).astype(BF)
    near_next = dp_swap(jnp.concatenate([near_next, packed(gain_sum, 640)], axis=0), 12)
    away_next = dp_swap((middle[:, 640:] + away[:128].astype(F32)).astype(BF), 4)
    gain_sum = settled(gain_sum) + unpacked(near_next[128:])
    sums = keep + jnp.concatenate(
        [
            near[:128].astype(F32) + near_next[:128].astype(F32),
            away[128:].astype(F32) + away_next.astype(F32),
        ],
        axis=1,
    )
    got = dp_swap(jnp.concatenate([sums[64:].astype(BF), packed(gain_sum, 1408)], axis=0), 2)
    gain_sum = settled(gain_sum) + unpacked(got[64:])
    sums = sums[:64] + got[:64].astype(F32)
    sums = jnp.concatenate(
        [sums[:, :128], sums[:, 640:896], sums[:, 128:640], sums[:, 896:]], axis=1
    )
    sums, dqkv = lax.optimization_barrier((sums, dqkv))
    (frame_grad,) = staged(
        frame_gradient_kernel,
        "frame_gradient",
        [shape(BF, rows, width)],
        [],
        [x, dqkv, grad_out],
        [gain_row],
        [w_qkv],
        [
            pltpu.VMEM((3, width, width), BF),
            pltpu.VMEM((3, rows, width), BF),
            pltpu.SemaphoreType.DMA((3,)),
        ],
    )

    note = jnp.broadcast_to(packed(gain_sum, 256)[None], (8, 8, 256))
    got = seq_exchange(jnp.concatenate([sums.reshape(8, 8, 1408).astype(BF), note], axis=2))
    grad_wqkv = got[:, :, :384].reshape(8, 8, 3, head).transpose(1, 2, 0, 3).reshape(8, 3 * width)
    grad_wout = jnp.sum(got[:, :, 384:1408].astype(F32), axis=0).astype(BF)
    totals = [unpacked(got[s, :, 1408:]) for s in range(8)]
    grad_gain = functools.reduce(lambda a, b: a + b, totals).reshape(width)
    return (
        layer_out[None],
        frame_grad[None],
        grad_wqkv,
        grad_wout,
        grad_gain,
    )


def solution(mesh):
    placed = (P("dp", "seq", None), P(), P(), P(), P("dp", None), P("dp", "seq", None))
    return jax.shard_map(
        on_device,
        mesh=mesh,
        in_specs=placed,
        out_specs=(
            P("dp", "seq", None),
            P("dp", "seq", None),
            P(("seq", "dp"), None),
            P(("seq", "dp"), None),
            P(),
        ),
        check_vma=False,
    )
```

```python
import functools

import jax
import jax.numpy as jnp
from jax import lax
from jax.experimental import pallas as pl
from jax.experimental.pallas import tpu as pltpu
from jax.sharding import PartitionSpec as P

HEADS = 8
BF = jnp.bfloat16
F32 = jnp.float32
LOG2E = 1.4426950408889634
PAIR = 4
CHUNK = 256
VMEM_LIMIT = 60 * 1024 * 1024
WHOLE = pl.BlockSpec(memory_space=pltpu.VMEM)
SCALARS = pl.BlockSpec(memory_space=pltpu.SMEM)


def seq_swap(x, bits):
    return lax.ppermute(x, "seq", [(i, i ^ bits) for i in range(8)])


def dp_swap(x, bits):
    return lax.ppermute(x, "dp", [(i, i ^ bits) for i in range(16)])


def seq_exchange(x):
    return lax.all_to_all(x, "seq", 0, 0, tiled=True)


def mm(a, b, ca, cb):
    return lax.dot_general(a, b, (((ca,), (cb,)), ((), ())), preferred_element_type=F32)


def call(kernel, name, out_shape, vmem=VMEM_LIMIT, **options):
    return pl.pallas_call(
        kernel,
        out_shape=out_shape,
        compiler_params=pltpu.CompilerParams(vmem_limit_bytes=vmem),
        name=name,
        **options,
    )


def shape(dtype, *dims):
    return jax.ShapeDtypeStruct(dims, dtype)


def layernorm(x):
    center = x - jnp.mean(x, axis=-1, keepdims=True)
    rstd = lax.rsqrt(jnp.mean(center * center, axis=-1, keepdims=True) + 1e-05)
    return center * rstd, rstd


def staged(
    body, name, out_shape, scalars, arrays, plain=(), left=(), scratch=(), vmem=VMEM_LIMIT
):
    n, m, k = len(scalars), len(arrays), len(plain) + len(left)

    def kernel(*refs):
        sources, others = refs[n : n + m], refs[n + m : n + m + k]
        outs = refs[n + m + k : n + m + k + len(out_shape)]
        rest = refs[n + m + k + len(out_shape) :]
        buffers, semaphores, rest = rest[:m], rest[m], rest[m + 1 :]
        copies = [
            pltpu.make_async_copy(sources[i], buffers[i], semaphores.at[i]) for i in range(m)
        ]
        for copy in copies:
            copy.start()
        waited = set()

        def get(i):
            if i not in waited:
                waited.add(i)
                copies[i].wait()
            return buffers[i]

        body(*refs[:n], get, *others, *outs, *rest)
        for i in range(m):
            get(i)

    return call(
        kernel,
        name,
        tuple(out_shape),
        vmem,
        in_specs=[SCALARS] * n
        + [pl.BlockSpec(memory_space=pltpu.HBM)] * m
        + [WHOLE] * len(plain)
        + [pl.BlockSpec(memory_space=pltpu.HBM)] * len(left),
        out_specs=(WHOLE,) * len(out_shape),
        scratch_shapes=[pltpu.VMEM(a.shape, a.dtype) for a in arrays]
        + [pltpu.SemaphoreType.DMA((m,))]
        + list(scratch),
    )(*scalars, *arrays, *plain, *left)


def layernorm_kernel(frames, gain, normed):
    xhat, _ = layernorm(frames[...].astype(F32))
    normed[...] = (xhat * gain[...]).astype(BF)


def dattn_kernel(pos, get, w_qkv, dattn, w_head, semaphores):
    copies = []
    for t in range(3):
        start = pl.multiple_of(t * 1024 + pos[0] * 128, 128)
        copies.append(
            pltpu.make_async_copy(
                w_qkv.at[:, pl.ds(start, 128)],
                w_head.at[:, t * 128 : (t + 1) * 128],
                semaphores.at[t],
            )
        )
    for copy in copies:
        copy.start()
    full = mm(get(0)[...], get(1)[...], 1, 1).astype(BF)
    for h in range(HEADS):
        dattn[h] = full[:, h * 128 : (h + 1) * 128]
    for copy in copies:
        copy.wait()


def attention_kernel(scale, places, pos, *refs):
    count = len(places)
    parts, (dout, ids) = refs[:count], refs[count : count + 2]
    attn, dqkv, q_s, k_s, v_s, kt_s, vt_s, dk_s, dv_s, s_s, p_s, l_s = refs[count + 2 :]
    rows = dout.shape[1]
    for part, (r, offset) in zip(parts, places):
        size = part.shape[0]
        rng = pl.ds(pl.multiple_of((pos[0] ^ r) * rows + offset, size), size)
        q_s[rng, :128] = part[:, :128]
        k_s[rng, :128] = part[:, 128:256]
        v_s[rng, :] = part[:, 256:]
    names = lax.broadcasted_iota(jnp.int32, (128, 8 * rows), 0)
    same = jnp.where(ids[...] == names, 1.0, 0.0).T
    q_s[:, 128:] = ((same - 1.0) * 1e30).astype(BF)
    k_s[:, 128:] = same.astype(BF)
    kt_s[...] = k_s[:, :128].T
    vt_s[...] = v_s[...].T
    dk_s[...] = jnp.zeros_like(dk_s)
    dv_s[...] = jnp.zeros_like(dv_s)

    size = min(CHUNK, 8 * rows)
    chunks = [slice(c, c + size) for c in range(0, 8 * rows, size)]

    def step(i, carry):
        for u in range(PAIR):
            block = i * PAIR + u
            rng = pl.ds(pl.multiple_of(block * rows, rows), rows)
            q, do, slot = q_s[rng, :], dout[block], u % 2
            peak = None
            for part in chunks:
                scores = mm(k_s[part, :], q, 1, 1)
                s_s[slot, part, :] = scores
                top = jnp.max(scores.reshape(-1, 8, rows), axis=0)
                peak = top if peak is None else jnp.maximum(peak, top)
            peak = jnp.max(peak, axis=0, keepdims=True)
            total = None
            for part in chunks:
                p_s[slot, part, :] = mm(v_s[part, :], do, 1, 1)
                expo = jnp.exp2((s_s[slot, part, :] - peak) * (scale * LOG2E))
                s_s[slot, part, :] = expo
                add = jnp.sum(expo.reshape(-1, 8, rows), axis=0)
                total = add if total is None else total + add
            inverse = 1.0 / jnp.sum(total, axis=0, keepdims=True)
            out = None
            for part in chunks:
                low = (s_s[slot, part, :] * inverse).astype(BF)
                l_s[slot, part, :] = low
                add = mm(vt_s[:, part], low, 1, 0)
                out = add if out is None else out + add
                dv_s[part, :] += mm(low, do, 1, 0)
            delta = jnp.sum(out * do.astype(F32).T, axis=0, keepdims=True)
            dq = None
            for part in chunks:
                dscores = l_s[slot, part, :].astype(F32) * (p_s[slot, part, :] - delta)
                dscores = dscores.astype(BF)
                dk_s[part, :] += mm(dscores, q[:, :128], 1, 0)
                add = mm(kt_s[:, part], dscores, 1, 0)
                dq = add if dq is None else dq + add
            attn[rng, :] = out.T.astype(BF)
            dqkv[rng, :128] = (dq * scale).T.astype(BF)
        return carry

    lax.fori_loop(0, 8 // PAIR, step, 0)
    dqkv[:, 128:256] = (dk_s[...] * scale).astype(BF)
    dqkv[:, 256:] = dv_s[...].astype(BF)


def attention(pos, parts, places, dout, ids, scale):
    total = ids.shape[1]
    return call(
        functools.partial(attention_kernel, scale, places),
        "attention",
        (shape(BF, total, 128), shape(BF, total, 384)),
        vmem=48 * 1024 * 1024,
        in_specs=[SCALARS] + [WHOLE] * (len(parts) + 2),
        out_specs=(WHOLE, WHOLE),
        scratch_shapes=[
            pltpu.VMEM((total, 256), BF),
            pltpu.VMEM((total, 256), BF),
            pltpu.VMEM((total, 128), BF),
            pltpu.VMEM((128, total), BF),
            pltpu.VMEM((128, total), BF),
            pltpu.VMEM((total, 128), F32),
            pltpu.VMEM((total, 128), F32),
            pltpu.VMEM((2, total, total // 8), F32),
            pltpu.VMEM((2, total, total // 8), F32),
            pltpu.VMEM((2, total, total // 8), BF),
        ],
    )(pos, *parts, dout, ids)


def chosen_rows(dp, source, half, target):
    for r in range(8):
        for s in range(8):
            rows = pl.ds(pl.multiple_of(s * 128 + (dp ^ (2 * r + half)) * 8, 8), 8)
            target[r * 64 + s * 8 : r * 64 + s * 8 + 8, :] = source[rows, :]


def projection_kernel(places, pos, get, gain, keep, send, own_gain, grad, other, sums):
    dqkv, weights = get(0), get(1)
    rows = dqkv.shape[0] // 8
    total = None
    for i, (r, offset) in enumerate(places):
        normed = get(2 + i)
        size = normed.shape[0]
        rng = pl.ds(pl.multiple_of((pos[0] ^ r) * rows + offset, size), size)
        term = mm(dqkv[rng, :], normed[...], 0, 0)
        total = term if total is None else total + term
    grad[...] = total.T
    weighted = jnp.sum(total * weights[...].T.astype(F32), axis=0, keepdims=True) / gain[...]
    sums[...] = jnp.zeros_like(sums)
    for j in range(8):
        sums[j : j + 1, :] = weighted[:, j * 128 : (j + 1) * 128]
    high = sums[...].astype(BF)
    low = (sums[...] - high.astype(F32)).astype(BF)
    own_gain[...] = (high.astype(F32) + low.astype(F32))[:8, :]
    chosen_rows(pos[1], grad, 0, keep)
    chosen_rows(pos[1], grad, 1, other)
    send[:512, :] = other[...].astype(BF)
    send[512:, :128] = high
    send[512:, 128:256] = low
    send[512:, 256:] = jnp.zeros_like(low)


def side_by_side(source, target):
    for h in range(HEADS):
        target[:, h * 128 : (h + 1) * 128] = source[h]


def output_gradient_kernel(
    pos, get, send_near, send_far, keep, middle, gain_sum, grad, chosen, flat, twin, sums
):
    side_by_side(get(0), flat)
    own = mm(flat[...], get(1)[...], 0, 0)
    side_by_side(get(2), twin)
    grad[...] = own + mm(twin[...], get(3)[...], 0, 0)
    chosen_rows(pos[1], grad, 0, chosen)
    arrived = get(5)[...].astype(F32)
    qkv = get(4)[...] + arrived[:512, :]
    left, right = slice(0, 640), slice(640, 1408)
    first, second = qkv[:, :128], qkv[:, 128:]
    send_near[:256, :128] = first[128:384].astype(BF)
    send_near[:256, 128:] = chosen[128:384, :512].astype(BF)
    send_far[:, :256] = second[256:].astype(BF)
    send_far[:, 256:] = chosen[256:, 512:].astype(BF)
    for target, near_rows, far_rows in (
        (keep, slice(0, 128), slice(0, 128)),
        (middle, slice(384, 512), slice(128, 256)),
    ):
        target[:, left] = jnp.concatenate([first[near_rows], chosen[near_rows, :512]], axis=1)
        target[:, right] = jnp.concatenate([second[far_rows], chosen[far_rows, 512:]], axis=1)
    sums[...] = jnp.zeros_like(sums)
    sums[:8, :] = get(6)[...] + arrived[512:520, :128] + arrived[512:520, 128:256]
    high = sums[...].astype(BF)
    low = (sums[...] - high.astype(F32)).astype(BF)
    gain_sum[...] = (high.astype(F32) + low.astype(F32))[:8, :]
    send_near[256:, :128] = high
    send_near[256:, 128:256] = low
    send_near[256:, 256:] = jnp.zeros((16, 384), BF)


def layer_out_kernel(get, layer_out, flat):
    side_by_side(get(1), flat)
    layer_out[...] = (get(0)[...].astype(F32) + mm(flat[...], get(2)[...], 1, 0)).astype(BF)


def frame_gradient_kernel(get, gain, w_qkv, result, weights, flat, semaphores):
    width = get(0).shape[1]
    copies = []
    for t in range(3):
        part = w_qkv.at[:, t * width : (t + 1) * width]
        copies.append(pltpu.make_async_copy(part, weights.at[t], semaphores.at[t]))
    for copy in copies:
        copy.start()
    xhat, rstd = layernorm(get(0)[...].astype(F32))
    total = None
    for t in range(3):
        for h in range(HEADS):
            flat[t, :, h * 128 : (h + 1) * 128] = get(1)[h][:, t * 128 : (t + 1) * 128]
        copies[t].wait()
        term = mm(weights[t], flat[t], 1, 1)
        total = term if total is None else total + term
    g = total.T * gain[...]
    mean_g = jnp.mean(g, axis=-1, keepdims=True)
    mean_gx = jnp.mean(g * xhat, axis=-1, keepdims=True)
    result[...] = (get(2)[...].astype(F32) + rstd * (g - mean_g - xhat * mean_gx)).astype(BF)


def finish_kernel(got, grad_wqkv, grad_wout, grad_gain):
    total, sums = None, None
    for s in range(8):
        part = got[s]
        for t in range(3):
            start = t * 1024 + s * 128
            grad_wqkv[:, start : start + 128] = part[:, t * 128 : (t + 1) * 128]
        wout = part[:, 384:1408].astype(F32)
        gain = part[:, 1408:1536].astype(F32) + part[:, 1536:].astype(F32)
        total = wout if total is None else total + wout
        sums = gain if sums is None else sums + gain
    grad_wout[...] = total.astype(BF)
    grad_gain[...] = sums


def high_low(x):
    high = lax.reduce_precision(x, 8, 7)
    low = lax.reduce_precision(x - high, 8, 7)
    return high, low


def packed(x, columns):
    high, low = high_low(x)
    both = jnp.concatenate([high, low], axis=1).astype(BF)
    return jnp.pad(both, ((0, 0), (0, columns - 256)))


def unpacked(x):
    return x[:, :128].astype(F32) + x[:, 128:256].astype(F32)


def settled(x):
    high, low = high_low(x)
    return high + low


def on_device(frames, layernorm_gain, w_qkv, w_out, segment_ids, output_gradient):
    x = frames[0]
    grad_out = output_gradient[0]
    rows, width = x.shape
    head = width // HEADS
    scale = head**-0.5
    pos = jnp.stack([lax.axis_index("seq"), lax.axis_index("dp")]).astype(jnp.int32)
    gain_row = layernorm_gain[None, :]

    own = call(
        layernorm_kernel, "layernorm", shape(BF, rows, width), in_specs=[WHOLE] * 2, out_specs=WHOLE
    )(x, gain_row)
    grad_twin = dp_swap(grad_out, 1)
    beside = seq_swap(own, 1)
    after, before = seq_swap(own, 2), seq_swap(own, 6)
    half = rows // 2
    far = [seq_swap(after[:half], 6), seq_swap(before[half:], 2)]
    beyond = [seq_swap(part, 1) for part in far]
    normed = {
        (0, 0): own,
        (1, 0): beside,
        (2, 0): after,
        (6, 0): before,
        (3, 0): seq_swap(beside, 2),
        (7, 0): seq_swap(beside, 6),
        (4, 0): far[0],
        (4, half): far[1],
        (5, 0): beyond[0],
        (5, half): beyond[1],
    }
    places, normed = list(normed), list(normed.values())

    dattn, w_head = staged(
        dattn_kernel,
        "dattn",
        [shape(BF, HEADS, rows, head), shape(BF, width, 384)],
        [pos],
        [grad_out, w_out],
        left=[w_qkv],
        scratch=[pltpu.SemaphoreType.DMA((3,))],
    )
    parts = [mm(n, w_head, 1, 0).astype(BF) for n in normed]
    dattn, grad_twin, _ = lax.optimization_barrier((dattn, grad_twin, beyond[1]))
    dout = seq_exchange(dattn)

    attn_head, dqkv_head = attention(pos, parts, places, dout, segment_ids, scale)
    attn = seq_exchange(attn_head.reshape(8, rows, head))
    dqkv = seq_exchange(dqkv_head.reshape(8, rows, 384))
    wqkv_keep, wqkv_send, gain_part = staged(
        functools.partial(projection_kernel, places),
        "projection_gradient",
        [shape(F32, 512, 384), shape(BF, 528, 384), shape(F32, 8, 128)],
        [pos],
        [dqkv_head, w_head] + normed,
        [gain_row],
        scratch=[
            pltpu.VMEM((1024, 384), F32),
            pltpu.VMEM((512, 384), F32),
            pltpu.VMEM((16, 128), F32),
        ],
    )
    attn, wqkv_send, gain_part = lax.optimization_barrier((attn, wqkv_send, gain_part))
    attn_twin = dp_swap(attn, 1)
    got = dp_swap(wqkv_send, 1)
    near, away, keep, middle, gain_sum = staged(
        output_gradient_kernel,
        "output_gradient",
        [shape(BF, 272, 640), shape(BF, 256, 768)]
        + [shape(F32, 128, 1408)] * 2
        + [shape(F32, 8, 128)],
        [pos],
        [attn, grad_out, attn_twin, grad_twin, wqkv_keep, got, gain_part],
        scratch=[
            pltpu.VMEM((1024, 1024), F32),
            pltpu.VMEM((512, 1024), F32),
            pltpu.VMEM((rows, width), BF),
            pltpu.VMEM((rows, width), BF),
            pltpu.VMEM((16, 128), F32),
        ],
        vmem=40 * 1024 * 1024,
    )
    near, away = dp_swap(near, 4), dp_swap(away, 12)
    (layer_out,) = staged(
        layer_out_kernel,
        "layer_out",
        [shape(BF, rows, width)],
        [],
        [x, attn, w_out],
        scratch=[pltpu.VMEM((rows, width), BF)],
    )
    near, away, layer_out = lax.optimization_barrier((near, away, layer_out))
    gain_sum = gain_sum + unpacked(near[256:264])
    near_next = (middle[:, :640] + near[128:256].astype(F32)).astype(BF)
    near_next = dp_swap(jnp.concatenate([near_next, packed(gain_sum, 640)], axis=0), 12)
    away_next = dp_swap((middle[:, 640:] + away[:128].astype(F32)).astype(BF), 4)
    gain_sum = settled(gain_sum) + unpacked(near_next[128:])
    sums = keep + jnp.concatenate(
        [
            near[:128].astype(F32) + near_next[:128].astype(F32),
            away[128:].astype(F32) + away_next.astype(F32),
        ],
        axis=1,
    )
    got = dp_swap(jnp.concatenate([sums[64:].astype(BF), packed(gain_sum, 1408)], axis=0), 2)
    gain_sum = settled(gain_sum) + unpacked(got[64:])
    sums = sums[:64] + got[:64].astype(F32)
    sums = jnp.concatenate(
        [sums[:, :128], sums[:, 640:896], sums[:, 128:640], sums[:, 896:]], axis=1
    )
    sums, dqkv = lax.optimization_barrier((sums, dqkv))
    (frame_grad,) = staged(
        frame_gradient_kernel,
        "frame_gradient",
        [shape(BF, rows, width)],
        [],
        [x, dqkv, grad_out],
        [gain_row],
        [w_qkv],
        [
            pltpu.VMEM((3, width, width), BF),
            pltpu.VMEM((3, rows, width), BF),
            pltpu.SemaphoreType.DMA((3,)),
        ],
    )

    note = jnp.broadcast_to(packed(gain_sum, 256)[None], (8, 8, 256))
    got = seq_exchange(jnp.concatenate([sums.reshape(8, 8, 1408).astype(BF), note], axis=2))
    grad_wqkv, grad_wout, grad_gain = call(
        finish_kernel,
        "finish",
        (shape(BF, 8, 3 * width), shape(BF, 8, width), shape(F32, 8, 128)),
        16 * 1024 * 1024,
        in_specs=[WHOLE],
        out_specs=(WHOLE,) * 3,
    )(got)
    grad_gain = grad_gain.reshape(width)
    return (
        layer_out[None],
        frame_grad[None],
        grad_wqkv,
        grad_wout,
        grad_gain,
    )


def solution(mesh):
    placed = (P("dp", "seq", None), P(), P(), P(), P("dp", None), P("dp", "seq", None))
    return jax.shard_map(
        on_device,
        mesh=mesh,
        in_specs=placed,
        out_specs=(
            P("dp", "seq", None),
            P("dp", "seq", None),
            P(("seq", "dp"), None),
            P(("seq", "dp"), None),
            P(),
        ),
        check_vma=False,
    )
```

```python
import functools

import jax
import jax.numpy as jnp
from jax import lax
from jax.experimental import pallas as pl
from jax.experimental.pallas import tpu as pltpu
from jax.sharding import PartitionSpec as P

HEADS = 8
BF = jnp.bfloat16
F32 = jnp.float32
LOG2E = 1.4426950408889634
PAIR = 8
CHUNK = 256
VMEM_LIMIT = 60 * 1024 * 1024
WHOLE = pl.BlockSpec(memory_space=pltpu.VMEM)
SCALARS = pl.BlockSpec(memory_space=pltpu.SMEM)


def seq_swap(x, bits):
    return lax.ppermute(x, "seq", [(i, i ^ bits) for i in range(8)])


def dp_swap(x, bits):
    return lax.ppermute(x, "dp", [(i, i ^ bits) for i in range(16)])


def seq_exchange(x):
    return lax.all_to_all(x, "seq", 0, 0, tiled=True)


def mm(a, b, ca, cb):
    return lax.dot_general(a, b, (((ca,), (cb,)), ((), ())), preferred_element_type=F32)


def call(kernel, name, out_shape, vmem=VMEM_LIMIT, **options):
    return pl.pallas_call(
        kernel,
        out_shape=out_shape,
        compiler_params=pltpu.CompilerParams(vmem_limit_bytes=vmem),
        name=name,
        **options,
    )


def shape(dtype, *dims):
    return jax.ShapeDtypeStruct(dims, dtype)


def layernorm(x):
    center = x - jnp.mean(x, axis=-1, keepdims=True)
    rstd = lax.rsqrt(jnp.mean(center * center, axis=-1, keepdims=True) + 1e-05)
    return center * rstd, rstd


def staged(
    body, name, out_shape, scalars, arrays, plain=(), left=(), scratch=(), vmem=VMEM_LIMIT
):
    n, m, k = len(scalars), len(arrays), len(plain) + len(left)

    def kernel(*refs):
        sources, others = refs[n : n + m], refs[n + m : n + m + k]
        outs = refs[n + m + k : n + m + k + len(out_shape)]
        rest = refs[n + m + k + len(out_shape) :]
        buffers, semaphores, rest = rest[:m], rest[m], rest[m + 1 :]
        copies = [
            pltpu.make_async_copy(sources[i], buffers[i], semaphores.at[i]) for i in range(m)
        ]
        for copy in copies:
            copy.start()
        waited = set()

        def get(i):
            if i not in waited:
                waited.add(i)
                copies[i].wait()
            return buffers[i]

        body(*refs[:n], get, *others, *outs, *rest)
        for i in range(m):
            get(i)

    return call(
        kernel,
        name,
        tuple(out_shape),
        vmem,
        in_specs=[SCALARS] * n
        + [pl.BlockSpec(memory_space=pltpu.HBM)] * m
        + [WHOLE] * len(plain)
        + [pl.BlockSpec(memory_space=pltpu.HBM)] * len(left),
        out_specs=(WHOLE,) * len(out_shape),
        scratch_shapes=[pltpu.VMEM(a.shape, a.dtype) for a in arrays]
        + [pltpu.SemaphoreType.DMA((m,))]
        + list(scratch),
    )(*scalars, *arrays, *plain, *left)


def layernorm_kernel(frames, gain, normed):
    xhat, _ = layernorm(frames[...].astype(F32))
    normed[...] = (xhat * gain[...]).astype(BF)


def dattn_kernel(pos, get, w_qkv, dattn, w_head, semaphores):
    copies = []
    for t in range(3):
        start = pl.multiple_of(t * 1024 + pos[0] * 128, 128)
        copies.append(
            pltpu.make_async_copy(
                w_qkv.at[:, pl.ds(start, 128)],
                w_head.at[:, t * 128 : (t + 1) * 128],
                semaphores.at[t],
            )
        )
    for copy in copies:
        copy.start()
    full = mm(get(0)[...], get(1)[...], 1, 1).astype(BF)
    for h in range(HEADS):
        dattn[h] = full[:, h * 128 : (h + 1) * 128]
    for copy in copies:
        copy.wait()


def attention_kernel(scale, places, pos, *refs):
    count = len(places)
    parts, (dout, ids) = refs[:count], refs[count : count + 2]
    attn, dqkv, q_s, k_s, v_s, kt_s, vt_s, dk_s, dv_s, s_s, p_s, l_s = refs[count + 2 :]
    rows = dout.shape[1]
    for part, (r, offset) in zip(parts, places):
        size = part.shape[0]
        rng = pl.ds(pl.multiple_of((pos[0] ^ r) * rows + offset, size), size)
        q_s[rng, :128] = part[:, :128]
        k_s[rng, :128] = part[:, 128:256]
        v_s[rng, :] = part[:, 256:]
    names = lax.broadcasted_iota(jnp.int32, (128, 8 * rows), 0)
    same = jnp.where(ids[...] == names, 1.0, 0.0).T
    q_s[:, 128:] = ((same - 1.0) * 1e30).astype(BF)
    k_s[:, 128:] = same.astype(BF)
    kt_s[...] = k_s[:, :128].T
    vt_s[...] = v_s[...].T
    dk_s[...] = jnp.zeros_like(dk_s)
    dv_s[...] = jnp.zeros_like(dv_s)

    size = min(CHUNK, 8 * rows)
    chunks = [slice(c, c + size) for c in range(0, 8 * rows, size)]

    def step(i, carry):
        for u in range(PAIR):
            block = i * PAIR + u
            rng = pl.ds(pl.multiple_of(block * rows, rows), rows)
            q, do, slot = q_s[rng, :], dout[block], u % 2
            peak = None
            for part in chunks:
                scores = mm(k_s[part, :], q, 1, 1)
                s_s[slot, part, :] = scores
                top = jnp.max(scores.reshape(-1, 8, rows), axis=0)
                peak = top if peak is None else jnp.maximum(peak, top)
            peak = jnp.max(peak, axis=0, keepdims=True)
            total = None
            for part in chunks:
                p_s[slot, part, :] = mm(v_s[part, :], do, 1, 1)
                expo = jnp.exp2((s_s[slot, part, :] - peak) * (scale * LOG2E))
                s_s[slot, part, :] = expo
                add = jnp.sum(expo.reshape(-1, 8, rows), axis=0)
                total = add if total is None else total + add
            inverse = 1.0 / jnp.sum(total, axis=0, keepdims=True)
            out = None
            for part in chunks:
                low = (s_s[slot, part, :] * inverse).astype(BF)
                l_s[slot, part, :] = low
                add = mm(vt_s[:, part], low, 1, 0)
                out = add if out is None else out + add
                dv_s[part, :] += mm(low, do, 1, 0)
            delta = jnp.sum(out * do.astype(F32).T, axis=0, keepdims=True)
            dq = None
            for part in chunks:
                dscores = l_s[slot, part, :].astype(F32) * (p_s[slot, part, :] - delta)
                dscores = dscores.astype(BF)
                dk_s[part, :] += mm(dscores, q[:, :128], 1, 0)
                add = mm(kt_s[:, part], dscores, 1, 0)
                dq = add if dq is None else dq + add
            attn[rng, :] = out.T.astype(BF)
            dqkv[rng, :128] = (dq * scale).T.astype(BF)
        return carry

    lax.fori_loop(0, 8 // PAIR, step, 0)
    dqkv[:, 128:256] = (dk_s[...] * scale).astype(BF)
    dqkv[:, 256:] = dv_s[...].astype(BF)


def attention(pos, parts, places, dout, ids, scale):
    total = ids.shape[1]
    return call(
        functools.partial(attention_kernel, scale, places),
        "attention",
        (shape(BF, total, 128), shape(BF, total, 384)),
        vmem=48 * 1024 * 1024,
        in_specs=[SCALARS] + [WHOLE] * (len(parts) + 2),
        out_specs=(WHOLE, WHOLE),
        scratch_shapes=[
            pltpu.VMEM((total, 256), BF),
            pltpu.VMEM((total, 256), BF),
            pltpu.VMEM((total, 128), BF),
            pltpu.VMEM((128, total), BF),
            pltpu.VMEM((128, total), BF),
            pltpu.VMEM((total, 128), F32),
            pltpu.VMEM((total, 128), F32),
            pltpu.VMEM((2, total, total // 8), F32),
            pltpu.VMEM((2, total, total // 8), F32),
            pltpu.VMEM((2, total, total // 8), BF),
        ],
    )(pos, *parts, dout, ids)


def chosen_rows(dp, source, half, target):
    for r in range(8):
        for s in range(8):
            rows = pl.ds(pl.multiple_of(s * 128 + (dp ^ (2 * r + half)) * 8, 8), 8)
            target[r * 64 + s * 8 : r * 64 + s * 8 + 8, :] = source[rows, :]


def projection_kernel(places, pos, get, gain, keep, send, own_gain, grad, other, sums):
    dqkv, weights = get(0), get(1)
    rows = dqkv.shape[0] // 8
    total = None
    for i, (r, offset) in enumerate(places):
        normed = get(2 + i)
        size = normed.shape[0]
        rng = pl.ds(pl.multiple_of((pos[0] ^ r) * rows + offset, size), size)
        term = mm(dqkv[rng, :], normed[...], 0, 0)
        total = term if total is None else total + term
    grad[...] = total.T
    weighted = jnp.sum(total * weights[...].T.astype(F32), axis=0, keepdims=True) / gain[...]
    sums[...] = jnp.zeros_like(sums)
    for j in range(8):
        sums[j : j + 1, :] = weighted[:, j * 128 : (j + 1) * 128]
    high = sums[...].astype(BF)
    low = (sums[...] - high.astype(F32)).astype(BF)
    own_gain[...] = (high.astype(F32) + low.astype(F32))[:8, :]
    chosen_rows(pos[1], grad, 0, keep)
    chosen_rows(pos[1], grad, 1, other)
    send[:512, :] = other[...].astype(BF)
    send[512:, :128] = high
    send[512:, 128:256] = low
    send[512:, 256:] = jnp.zeros_like(low)


def side_by_side(source, target):
    for h in range(HEADS):
        target[:, h * 128 : (h + 1) * 128] = source[h]


def output_gradient_kernel(
    pos, get, send_near, send_far, keep, middle, gain_sum, grad, chosen, flat, twin, sums
):
    side_by_side(get(0), flat)
    own = mm(flat[...], get(1)[...], 0, 0)
    side_by_side(get(2), twin)
    grad[...] = own + mm(twin[...], get(3)[...], 0, 0)
    chosen_rows(pos[1], grad, 0, chosen)
    arrived = get(5)[...].astype(F32)
    qkv = get(4)[...] + arrived[:512, :]
    left, right = slice(0, 640), slice(640, 1408)
    first, second = qkv[:, :128], qkv[:, 128:]
    send_near[:256, :128] = first[128:384].astype(BF)
    send_near[:256, 128:] = chosen[128:384, :512].astype(BF)
    send_far[:, :256] = second[256:].astype(BF)
    send_far[:, 256:] = chosen[256:, 512:].astype(BF)
    for target, near_rows, far_rows in (
        (keep, slice(0, 128), slice(0, 128)),
        (middle, slice(384, 512), slice(128, 256)),
    ):
        target[:, left] = jnp.concatenate([first[near_rows], chosen[near_rows, :512]], axis=1)
        target[:, right] = jnp.concatenate([second[far_rows], chosen[far_rows, 512:]], axis=1)
    sums[...] = jnp.zeros_like(sums)
    sums[:8, :] = get(6)[...] + arrived[512:520, :128] + arrived[512:520, 128:256]
    high = sums[...].astype(BF)
    low = (sums[...] - high.astype(F32)).astype(BF)
    gain_sum[...] = (high.astype(F32) + low.astype(F32))[:8, :]
    send_near[256:, :128] = high
    send_near[256:, 128:256] = low
    send_near[256:, 256:] = jnp.zeros((16, 384), BF)


def layer_out_kernel(get, layer_out, flat):
    side_by_side(get(1), flat)
    layer_out[...] = (get(0)[...].astype(F32) + mm(flat[...], get(2)[...], 1, 0)).astype(BF)


def frame_gradient_kernel(get, gain, w_qkv, result, weights, flat, semaphores):
    width = get(0).shape[1]
    copies = []
    for t in range(3):
        part = w_qkv.at[:, t * width : (t + 1) * width]
        copies.append(pltpu.make_async_copy(part, weights.at[t], semaphores.at[t]))
    for copy in copies:
        copy.start()
    xhat, rstd = layernorm(get(0)[...].astype(F32))
    total = None
    for t in range(3):
        for h in range(HEADS):
            flat[t, :, h * 128 : (h + 1) * 128] = get(1)[h][:, t * 128 : (t + 1) * 128]
        copies[t].wait()
        term = mm(weights[t], flat[t], 1, 1)
        total = term if total is None else total + term
    g = total.T * gain[...]
    mean_g = jnp.mean(g, axis=-1, keepdims=True)
    mean_gx = jnp.mean(g * xhat, axis=-1, keepdims=True)
    result[...] = (get(2)[...].astype(F32) + rstd * (g - mean_g - xhat * mean_gx)).astype(BF)


def finish_kernel(got, grad_wqkv, grad_wout, grad_gain):
    total, sums = None, None
    for s in range(8):
        part = got[s]
        for t in range(3):
            start = t * 1024 + s * 128
            grad_wqkv[:, start : start + 128] = part[:, t * 128 : (t + 1) * 128]
        wout = part[:, 384:1408].astype(F32)
        gain = part[:, 1408:1536].astype(F32) + part[:, 1536:].astype(F32)
        total = wout if total is None else total + wout
        sums = gain if sums is None else sums + gain
    grad_wout[...] = total.astype(BF)
    grad_gain[...] = sums


def high_low(x):
    high = lax.reduce_precision(x, 8, 7)
    low = lax.reduce_precision(x - high, 8, 7)
    return high, low


def packed(x, columns):
    high, low = high_low(x)
    both = jnp.concatenate([high, low], axis=1).astype(BF)
    return jnp.pad(both, ((0, 0), (0, columns - 256)))


def unpacked(x):
    return x[:, :128].astype(F32) + x[:, 128:256].astype(F32)


def settled(x):
    high, low = high_low(x)
    return high + low


def on_device(frames, layernorm_gain, w_qkv, w_out, segment_ids, output_gradient):
    x = frames[0]
    grad_out = output_gradient[0]
    rows, width = x.shape
    head = width // HEADS
    scale = head**-0.5
    pos = jnp.stack([lax.axis_index("seq"), lax.axis_index("dp")]).astype(jnp.int32)
    gain_row = layernorm_gain[None, :]

    own = call(
        layernorm_kernel, "layernorm", shape(BF, rows, width), in_specs=[WHOLE] * 2, out_specs=WHOLE
    )(x, gain_row)
    grad_twin = dp_swap(grad_out, 1)
    beside = seq_swap(own, 1)
    after, before = seq_swap(own, 2), seq_swap(own, 6)
    half = rows // 2
    far = [seq_swap(after[:half], 6), seq_swap(before[half:], 2)]
    beyond = [seq_swap(part, 1) for part in far]
    normed = {
        (0, 0): own,
        (1, 0): beside,
        (2, 0): after,
        (6, 0): before,
        (3, 0): seq_swap(beside, 2),
        (7, 0): seq_swap(beside, 6),
        (4, 0): far[0],
        (4, half): far[1],
        (5, 0): beyond[0],
        (5, half): beyond[1],
    }
    places, normed = list(normed), list(normed.values())

    dattn, w_head = staged(
        dattn_kernel,
        "dattn",
        [shape(BF, HEADS, rows, head), shape(BF, width, 384)],
        [pos],
        [grad_out, w_out],
        left=[w_qkv],
        scratch=[pltpu.SemaphoreType.DMA((3,))],
    )
    parts = [mm(n, w_head, 1, 0).astype(BF) for n in normed]
    dattn, grad_twin, _ = lax.optimization_barrier((dattn, grad_twin, beyond[1]))
    dout = seq_exchange(dattn)

    attn_head, dqkv_head = attention(pos, parts, places, dout, segment_ids, scale)
    attn = seq_exchange(attn_head.reshape(8, rows, head))
    dqkv = seq_exchange(dqkv_head.reshape(8, rows, 384))
    wqkv_keep, wqkv_send, gain_part = staged(
        functools.partial(projection_kernel, places),
        "projection_gradient",
        [shape(F32, 512, 384), shape(BF, 528, 384), shape(F32, 8, 128)],
        [pos],
        [dqkv_head, w_head] + normed,
        [gain_row],
        scratch=[
            pltpu.VMEM((1024, 384), F32),
            pltpu.VMEM((512, 384), F32),
            pltpu.VMEM((16, 128), F32),
        ],
    )
    attn, wqkv_send, gain_part = lax.optimization_barrier((attn, wqkv_send, gain_part))
    attn_twin = dp_swap(attn, 1)
    got = dp_swap(wqkv_send, 1)
    near, away, keep, middle, gain_sum = staged(
        output_gradient_kernel,
        "output_gradient",
        [shape(BF, 272, 640), shape(BF, 256, 768)]
        + [shape(F32, 128, 1408)] * 2
        + [shape(F32, 8, 128)],
        [pos],
        [attn, grad_out, attn_twin, grad_twin, wqkv_keep, got, gain_part],
        scratch=[
            pltpu.VMEM((1024, 1024), F32),
            pltpu.VMEM((512, 1024), F32),
            pltpu.VMEM((rows, width), BF),
            pltpu.VMEM((rows, width), BF),
            pltpu.VMEM((16, 128), F32),
        ],
        vmem=40 * 1024 * 1024,
    )
    near, away = dp_swap(near, 4), dp_swap(away, 12)
    (layer_out,) = staged(
        layer_out_kernel,
        "layer_out",
        [shape(BF, rows, width)],
        [],
        [x, attn, w_out],
        scratch=[pltpu.VMEM((rows, width), BF)],
    )
    near, away, layer_out = lax.optimization_barrier((near, away, layer_out))
    gain_sum = gain_sum + unpacked(near[256:264])
    near_next = (middle[:, :640] + near[128:256].astype(F32)).astype(BF)
    near_next = dp_swap(jnp.concatenate([near_next, packed(gain_sum, 640)], axis=0), 12)
    away_next = dp_swap((middle[:, 640:] + away[:128].astype(F32)).astype(BF), 4)
    gain_sum = settled(gain_sum) + unpacked(near_next[128:])
    sums = keep + jnp.concatenate(
        [
            near[:128].astype(F32) + near_next[:128].astype(F32),
            away[128:].astype(F32) + away_next.astype(F32),
        ],
        axis=1,
    )
    got = dp_swap(jnp.concatenate([sums[64:].astype(BF), packed(gain_sum, 1408)], axis=0), 2)
    gain_sum = settled(gain_sum) + unpacked(got[64:])
    sums = sums[:64] + got[:64].astype(F32)
    sums = jnp.concatenate(
        [sums[:, :128], sums[:, 640:896], sums[:, 128:640], sums[:, 896:]], axis=1
    )
    sums, dqkv = lax.optimization_barrier((sums, dqkv))
    (frame_grad,) = staged(
        frame_gradient_kernel,
        "frame_gradient",
        [shape(BF, rows, width)],
        [],
        [x, dqkv, grad_out],
        [gain_row],
        [w_qkv],
        [
            pltpu.VMEM((3, width, width), BF),
            pltpu.VMEM((3, rows, width), BF),
            pltpu.SemaphoreType.DMA((3,)),
        ],
    )

    note = jnp.broadcast_to(packed(gain_sum, 256)[None], (8, 8, 256))
    got = seq_exchange(jnp.concatenate([sums.reshape(8, 8, 1408).astype(BF), note], axis=2))
    grad_wqkv, grad_wout, grad_gain = call(
        finish_kernel,
        "finish",
        (shape(BF, 8, 3 * width), shape(BF, 8, width), shape(F32, 8, 128)),
        16 * 1024 * 1024,
        in_specs=[WHOLE],
        out_specs=(WHOLE,) * 3,
    )(got)
    grad_gain = grad_gain.reshape(width)
    return (
        layer_out[None],
        frame_grad[None],
        grad_wqkv,
        grad_wout,
        grad_gain,
    )


def solution(mesh):
    placed = (P("dp", "seq", None), P(), P(), P(), P("dp", None), P("dp", "seq", None))
    return jax.shard_map(
        on_device,
        mesh=mesh,
        in_specs=placed,
        out_specs=(
            P("dp", "seq", None),
            P("dp", "seq", None),
            P(("seq", "dp"), None),
            P(("seq", "dp"), None),
            P(),
        ),
        check_vma=False,
    )
```
